32 devices in a mesh: grp: 2 (over x), exp: 16 (over z, y, core).
Axes of the slice: x: 2, y: 2, z: 4, core: 2. Of those that a mesh axis runs over, the one named last changes fastest.
Arguments:
- latent_in: bfloat16 [2048, 1024], P(('grp', 'exp')), parts along dimension 0, may hold values from -6 to 6
- routes: int32 [2048, 8], P(('grp', 'exp')), parts along dimension 0, may hold values from 0 to 31, all different within a row; in each aligned block of 64 rows (0 to 63, 64 to 127, ...) at most 32 rows name the same one
- router: bfloat16 [1024, 32], P(None, 'exp'), may hold values from -0.1875 to 0.1875
- gate_up: bfloat16 [32, 1024, 2048], P('exp'), may hold values from -0.1875 to 0.1875
- expert_down: bfloat16 [32, 1024, 1024], P('exp'), may hold values from -0.1875 to 0.1875
Outputs:
- mixed: bfloat16 [2048, 1024], P(('grp', 'exp')), parts along dimension 0
The draws below stay inside these ranges and needn't reach their ends.
There are 2 independent parts, one for each index of `grp`. The reference program is written for one: setup_inputs(seed, part) draws one part's arguments, and reference() takes and returns one part's arrays. A program takes and returns all parts, laid end to end along the dimension named above; an argument that names none is the same for every part. Nothing has to cross between parts.
Inputs may be any that keep to these rules, and one draw needn't show every extreme that they name: `routes`: each token names 8 different experts. Among the 64 tokens of one device (aligned blocks of rows), no expert is named more than 32 times, and in every draw some device names some expert exactly 32 times.
All inputs are finite; a program needn't handle non-finite values.
Results may differ from the reference program's by a relative error of at most 0.0075.
Values may be sent and summed in bfloat16 or wider, within the bound.
No kernel may reach another device: no remote copies, remote signals or barrier semaphores. Data moves between devices by JAX's collectives and lax.ppermute only.
A program may use at most 64 MiB of HBM per device.

```python
import math
import jax
import jax.numpy as jnp
import numpy as np
from jax import lax

LAT = 1024
EFF = 1024
TOP = 8
TOK_DEV = 64
EXPERTS = 32
TOKENS = 1024
CAP = 32
N_EXP = 16


def block_levels(own_key, shape, cuts, low, top_value):
    loudness = 1.0
    for axis_at, parts in cuts:
        steps = jax.random.uniform(jax.random.fold_in(jax.random.fold_in(own_key, 6), axis_at), (parts,), jnp.float32, low / len(cuts), top_value / len(cuts))
        loudness = loudness * jnp.repeat(jnp.exp(steps), shape[axis_at] // parts).reshape((-1,) + (1,) * (len(shape) - 1 - axis_at))
    return loudness


def deal_out(key, own, number, rows, amount, top, bound, skew):
    sequence = jax.random.permutation(key, amount)
    crowded, usual = shares(amount, rows * top, bound, skew, True), shares(amount, rows * top, bound, skew, False)
    places = jnp.arange(amount)

    def named(tallies, turn):
        used = int((tallies > 0).sum())
        fixed = max(1, used // 4)
        passed = fixed + (places - fixed + turn * (used - fixed)) % max(1, amount - fixed)
        return jnp.zeros((amount,), jnp.int32).at[sequence[jnp.where(places < fixed, places, passed)]].set(jnp.asarray(tallies, jnp.int32))

    tallies = jnp.where(number % 4 == 0, named(crowded, number // 4), named(usual, number - number // 4 - 1))
    mixed = jax.random.permutation(jax.random.fold_in(own, 3), amount)
    source_of, receiver = mixed[0:amount // 2 * 2:2], mixed[1:amount // 2 * 2:2]
    slack = jnp.minimum(tallies[source_of] - 1, bound - tallies[receiver]) // 2
    slack = jnp.where((source_of == sequence[0]) | (receiver == sequence[0]) | (tallies[receiver] == 0), 0, jnp.maximum(slack, 0))
    passed = jax.random.randint(jax.random.fold_in(own, 4), (amount // 2,), 0, 1 << 20) % (slack + 1)
    tallies = tallies.at[source_of].add(-passed).at[receiver].add(passed)
    members = jnp.searchsorted(jnp.cumsum(tallies), jnp.arange(rows * top), side="right").astype(jnp.int32)
    table = members.reshape(top, rows).T
    table = table[jax.random.permutation(jax.random.fold_in(own, 1), rows)]
    turn = jax.random.randint(jax.random.fold_in(own, 2), (rows, 1), 0, top)
    return jnp.take_along_axis(table, (jnp.arange(top)[None, :] + turn) % top, axis=1)


def shares(number_of, total, reach, lean, full):
    weights = [(1 << 20) // math.isqrt(rank ** lean) + 1 for rank in range(1, number_of + 1)]
    largest = reach if full else min(reach, max(-(-total // number_of), total * weights[0] // sum(weights)))
    least = 1 if total - largest >= number_of - 1 else 0
    holding, rest = [largest] + [least] * (number_of - 1), total - largest - least * (number_of - 1)
    while rest > 0:
        candidates = [i for i in range(1, number_of) if holding[i] < largest] or [i for i in range(1, number_of) if holding[i] < reach]
        pool, budget = sum([weights[i] for i in candidates]), rest
        for i in candidates:
            addition = min(reach - holding[i], max(1, budget * weights[i] // pool), rest)
            holding[i] = holding[i] + addition
            rest = rest - addition
    return np.array(holding)


def bell_draw(rng, extent, scale, bound, pieces=(), held_as=jnp.bfloat16):
    level = block_levels(rng, extent, pieces, -0.22, 0.18) if pieces else 1.0
    drawn = jax.random.normal(rng, extent, jnp.float32) * scale * level
    return jnp.minimum(jnp.maximum(drawn, -bound), bound).astype(held_as)


def setup_inputs(seed: int = 0, part: int = 0) -> dict:
    streams_of = jax.random.split(jax.random.key(seed), 6)
    own_keys = jax.random.split(jax.random.fold_in(streams_of[5], part), 6)
    latent_in = bell_draw(own_keys[0], (TOKENS, LAT), 1.0, 6.0, ((0, 16),))
    routes_keys = jax.random.split(jax.random.fold_in(own_keys[1], 1), TOKENS // TOK_DEV)
    routes_turns = jax.random.permutation(jax.random.fold_in(own_keys[1], 3), TOKENS // TOK_DEV)
    routes = jax.vmap(lambda own, number: deal_out(jax.random.fold_in(own_keys[1], 2), own, number, TOK_DEV, EXPERTS, TOP, CAP, 2))(routes_keys, routes_turns).reshape((TOKENS, TOP))
    router = bell_draw(streams_of[2], (LAT, EXPERTS), LAT ** -0.5, 0.1875, ((1, 16),))
    gate_up = bell_draw(streams_of[3], (EXPERTS, LAT, 2 * EFF), LAT ** -0.5, 0.1875, ((0, 16),))
    expert_down = bell_draw(streams_of[4], (EXPERTS, EFF, LAT), EFF ** -0.5, 0.1875, ((0, 16),))
    return dict(latent_in=latent_in, routes=routes, router=router, gate_up=gate_up, expert_down=expert_down)


def reference(latent_in, routes, router, gate_up, expert_down):
    logits = jnp.dot(latent_in, router, preferred_element_type=jnp.float32)
    score = jax.nn.sigmoid(jnp.take_along_axis(logits, routes, axis=1))
    weight = score / jnp.sum(score, axis=1, keepdims=True)
    blocks = routes.reshape(N_EXP, TOK_DEV * TOP)
    labels = jnp.arange(EXPERTS, dtype=jnp.int32)
    matches = (blocks[:, :, None] == labels[None, None, :]).astype(jnp.int32)
    before = jnp.cumsum(matches, axis=1) - matches
    position = jnp.sum(before * matches, axis=2)
    source = jnp.arange(N_EXP, dtype=jnp.int32)[:, None] * CAP
    slot_index = (source + position).reshape(TOKENS * TOP).astype(jnp.int32)
    expert_ids = routes.reshape(TOKENS * TOP).astype(jnp.int32)
    repeated = jnp.repeat(latent_in, TOP, axis=0)
    buffers = jnp.zeros((EXPERTS, N_EXP * CAP, LAT), jnp.bfloat16)
    buffers = buffers.at[expert_ids, slot_index].set(repeated)

    def one_expert(packed):
        rows, weights_a, weights_b = packed
        both = jnp.dot(rows, weights_a, preferred_element_type=jnp.float32)
        inner = (jax.nn.silu(both[:, :EFF]) * both[:, EFF:]).astype(jnp.bfloat16)
        return jnp.dot(inner, weights_b, preferred_element_type=jnp.float32).astype(jnp.bfloat16)

    results = lax.map(one_expert, (buffers, gate_up, expert_down))
    picked = results[expert_ids, slot_index].astype(jnp.float32)
    picked = picked.reshape(TOKENS, TOP, LAT) * weight[:, :, None]
    return jnp.sum(picked, axis=1).astype(jnp.bfloat16)
```

```python
import jax
import jax.numpy as jnp
from jax import lax
from jax.sharding import PartitionSpec as P


def on_device(latent_in, routes, router, gate_up, expert_down):
    n_dev = lax.axis_size("exp")
    local = gate_up.shape[0]
    eff = expert_down.shape[1]
    rows, lat = latent_in.shape
    me = lax.axis_index("exp")
    tokens = lax.all_gather(latent_in, "exp", axis=0, tiled=True)
    chosen = lax.all_gather(routes, "exp", axis=0, tiled=True)
    columns = lax.all_gather(router, "exp", axis=1, tiled=True)

    def part(tok, ids):
        logits = jnp.dot(tok, columns, preferred_element_type=jnp.float32)
        labels = jnp.arange(n_dev * local, dtype=jnp.int32)
        mask = jnp.any(ids[:, :, None] == labels[None, None, :], axis=1)
        score = jnp.where(mask, jax.nn.sigmoid(logits), 0.0)
        weight = score / jnp.sum(score, axis=1, keepdims=True)
        mine = lax.dynamic_slice_in_dim(weight, me * local, local, axis=1)
        inner = []
        for e in range(local):
            both = jnp.dot(tok, gate_up[e], preferred_element_type=jnp.float32)
            one = jax.nn.silu(both[:, :eff]) * both[:, eff:] * mine[:, e : e + 1]
            inner.append(one.astype(jnp.bfloat16))
        inner = jnp.concatenate(inner, axis=1)
        down = expert_down.reshape(local * eff, lat)
        return jnp.dot(inner, down, preferred_element_type=jnp.float32).astype(jnp.bfloat16)

    step = 16 * rows if n_dev == 16 else 4 * rows
    if n_dev * rows == step:
        sums = part(tokens, chosen)
    else:
        sums = lax.map(
            lambda pair: part(*pair),
            (tokens.reshape(-1, step, lat), chosen.reshape(-1, step, chosen.shape[1])),
        ).reshape(n_dev * rows, lat)
    return lax.psum_scatter(sums, "exp", scatter_dimension=0, tiled=True)


def solution(mesh):
    placed = (
        P(("grp", "exp"), None),
        P(("grp", "exp"), None),
        P(None, "exp"),
        P("exp", None, None),
        P("exp", None, None),
    )
    return jax.shard_map(
        on_device, mesh=mesh, in_specs=placed, out_specs=P(("grp", "exp"), None), check_vma=False
    )
```

```python
import jax
import jax.numpy as jnp
from jax import lax
from jax.sharding import PartitionSpec as P

GROUP = 16


def on_device(latent_in, routes, router, gate_up, expert_down):
    n_dev = lax.axis_size("exp")
    local = gate_up.shape[0]
    eff = expert_down.shape[1]
    rows, lat = latent_in.shape
    top = routes.shape[1]
    me = lax.axis_index("exp")

    def swap(x, bits):
        return lax.ppermute(x, "exp", [(i, i ^ bits) for i in range(n_dev)])

    per_row = local * lat // rows
    small = jnp.concatenate(
        [
            routes.astype(jnp.bfloat16),
            router.T.reshape(rows, per_row),
            jnp.zeros((rows, 128 - top - per_row), jnp.bfloat16),
        ],
        axis=1,
    )
    bit = 1
    while bit < n_dev:
        small = jnp.concatenate([small, swap(small, bit)], axis=0)
        bit *= 2
    small = small.reshape(n_dev, rows, 128)
    group_ids = small[:GROUP, :, :top]
    columns = small[:, :, top : top + per_row].reshape(n_dev * local, lat)
    labels = ((me ^ jnp.arange(n_dev, dtype=jnp.int32))[:, None] * local + jnp.arange(local)).reshape(-1)
    down = expert_down.reshape(local * eff, lat)

    def group_pass(mine, ids):
        ids = ids.astype(jnp.int32)
        batches = []
        for k in range(GROUP // 4):
            one = mine if k == 0 else swap(mine, 4 * k)
            pair = jnp.concatenate([one, swap(one, 2)], axis=0)
            batches.append((pair, swap(pair, 1)))
        total = None
        for k in range(GROUP // 4):
            pair, other = batches[k]
            tok = jnp.concatenate([pair, other], axis=0)
            tok_ids = jnp.concatenate([ids[4 * k + i] for i in (0, 2, 1, 3)], axis=0)
            logits = lax.dot_general(
                tok, columns, (((1,), (1,)), ((), ())), preferred_element_type=jnp.float32
            )
            mask = jnp.any(tok_ids[:, :, None] == labels[None, None, :], axis=1)
            score = jnp.where(mask, jax.nn.sigmoid(logits), 0.0)
            weight = score[:, :local] / jnp.sum(score, axis=1, keepdims=True)
            inner = []
            for e in range(local):
                both = jnp.dot(tok, gate_up[e], preferred_element_type=jnp.float32)
                one = jax.nn.silu(both[:, :eff]) * both[:, eff:] * weight[:, e : e + 1]
                inner.append(one.astype(jnp.bfloat16))
            sums = jnp.dot(
                jnp.concatenate(inner, axis=1), down, preferred_element_type=jnp.float32
            )
            half = 2 * rows
            sums = sums[:half] + swap(sums[half:].astype(jnp.bfloat16), 1).astype(jnp.float32)
            sums = sums[:rows] + swap(sums[rows:].astype(jnp.bfloat16), 2).astype(jnp.float32)
            if k > 0:
                sums = swap(sums.astype(jnp.bfloat16), 4 * k).astype(jnp.float32)
            total = sums if total is None else total + sums
        return total

    if n_dev == GROUP:
        return group_pass(latent_in, group_ids).astype(jnp.bfloat16)

    def next_group(x):
        return lax.ppermute(x, "exp", [(i, (i + GROUP) % n_dev) for i in range(n_dev)])

    def step(carry, _):
        mine, ids, total = carry
        total = total + group_pass(mine, ids)
        return (next_group(mine), next_group(ids), next_group(total)), None

    start = (latent_in, group_ids, jnp.zeros((rows, lat), jnp.float32))
    (_, _, total), _ = lax.scan(step, start, None, length=n_dev // GROUP)
    return total.astype(jnp.bfloat16)


def solution(mesh):
    placed = (
        P(("grp", "exp"), None),
        P(("grp", "exp"), None),
        P(None, "exp"),
        P("exp", None, None),
        P("exp", None, None),
    )
    return jax.shard_map(
        on_device, mesh=mesh, in_specs=placed, out_specs=P(("grp", "exp"), None), check_vma=False
    )
```

```python
import functools

import jax
import jax.numpy as jnp
from jax import lax
from jax.experimental import pallas as pl
from jax.experimental.pallas import tpu as pltpu
from jax.sharding import PartitionSpec as P

GROUP = 16
TAIL = 128
SCALE = 2.0**40


def pack_kernel(ids_ref, row_ref, out_ref):
    rows, top = row_ref.shape[0], ids_ref.shape[0]
    lat = row_ref.shape[1]
    out_ref[:, :lat] = row_ref[...]
    ids = ids_ref[...].astype(jnp.float32)
    wide = jnp.concatenate([ids, jnp.full((top, TAIL - rows), -1.0, jnp.float32)], axis=1)
    wide = jnp.concatenate([wide, jnp.full((TAIL - top, TAIL), -1.0, jnp.float32)], axis=0)
    out_ref[:, lat:] = wide.T[:rows].astype(jnp.bfloat16)


STEP = 256


def weight_copies(up_hbm, down_hbm, up_ref, down_ref, sems):
    local, _, eff2 = up_ref.shape
    eff, lat = eff2 // 2, down_ref.shape[1]
    pieces = []
    for e in range(local):
        for c in range(0, eff, STEP):
            for at in (c, eff + c):
                pieces.append((up_hbm.at[e, :, pl.ds(at, STEP)], up_ref.at[e, :, pl.ds(at, STEP)]))
    for c in range(0, lat, STEP):
        pieces.append((down_hbm.at[:, pl.ds(c, STEP)], down_ref.at[:, pl.ds(c, STEP)]))
    return [pltpu.make_async_copy(src, dst, sems.at[i]) for i, (src, dst) in enumerate(pieces)]


def expert_body(first_ref, pair_ref, other_ref, router_ref, up_ref, down_ref, keep_ref, send_ref, inner_ref, copies):
    half, wide = pair_ref.shape
    lat = wide - TAIL
    local, _, eff2 = up_ref.shape
    eff = eff2 // 2
    copies = iter(copies)

    def ready(number):
        for _, copy in zip(range(number), copies):
            copy.wait()

    x = jnp.concatenate([pair_ref[:, :lat], other_ref[:, :lat]], axis=0)
    tail = jnp.concatenate([pair_ref[:, lat:], other_ref[:, lat:]], axis=0).astype(jnp.float32)
    logits = lax.dot_general(
        x, router_ref[...], (((1,), (1,)), ((), ())), preferred_element_type=jnp.float32
    )
    sums = jnp.zeros((2 * half, 1), jnp.float32)
    for e in range(local):
        label = (first_ref[0] + e).astype(jnp.float32)
        mask = jnp.max(jnp.where(tail == label, 1.0, 0.0), axis=1, keepdims=True)
        score = jax.nn.sigmoid(logits[:, e : e + 1]) * (mask * SCALE)
        sums = sums + score
        for c in range(0, eff, STEP):
            ready(2)
            gate = jnp.dot(x, up_ref[e, :, c : c + STEP], preferred_element_type=jnp.float32)
            up = jnp.dot(x, up_ref[e, :, eff + c : eff + c + STEP], preferred_element_type=jnp.float32)
            inner_ref[:, e * eff + c : e * eff + c + STEP] = (
                gate / (1.0 + jnp.exp(-gate)) * up * score
            ).astype(jnp.bfloat16)
    inner = inner_ref[...]
    for c in range(0, lat, STEP):
        ready(1)
        part = jnp.dot(inner, down_ref[:, c : c + STEP], preferred_element_type=jnp.float32)
        keep_ref[:, c : c + STEP] = part[:half]
        send_ref[:, c : c + STEP] = part[half:].astype(jnp.bfloat16)
    lane = lax.broadcasted_iota(jnp.int32, (2 * half, TAIL), 1)
    sums = jnp.where(lane == 0, sums, 0.0)
    keep_ref[:, lat:] = sums[:half]
    send_ref[:, lat:] = sums[half:].astype(jnp.bfloat16)


def first_kernel(first_ref, pair_ref, other_ref, router_ref, up_hbm, down_hbm, keep_ref, send_ref, up_ref, down_ref, inner_ref, sems):
    copies = weight_copies(up_hbm, down_hbm, up_ref, down_ref, sems)
    for copy in copies:
        copy.start()
    expert_body(
        first_ref, pair_ref, other_ref, router_ref, up_ref, down_ref, keep_ref, send_ref, inner_ref, copies
    )


def next_kernel(first_ref, pair_ref, other_ref, router_ref, up_ref, down_ref, _, keep_ref, send_ref, inner_ref):
    expert_body(first_ref, pair_ref, other_ref, router_ref, up_ref, down_ref, keep_ref, send_ref, inner_ref, [])


def in_vmem(x):
    return pltpu.with_memory_space_constraint(x, pltpu.VMEM)


def in_hbm(x):
    return pltpu.with_memory_space_constraint(x, pltpu.HBM)


def on_device(latent_in, routes, router, gate_up, expert_down):
    n_dev = lax.axis_size("exp")
    local = gate_up.shape[0]
    eff = expert_down.shape[1]
    rows, lat = latent_in.shape
    wide = lat + TAIL
    me = lax.axis_index("exp")

    def swap(x, bits):
        return lax.ppermute(x, "exp", [(i, i ^ bits) for i in range(n_dev)])

    vmem = pl.BlockSpec(memory_space=pltpu.VMEM)
    packet = pl.pallas_call(
        pack_kernel,
        out_shape=jax.ShapeDtypeStruct((rows, wide), jnp.bfloat16),
        in_specs=[vmem, vmem],
        out_specs=vmem,
        name="pack",
    )(routes.T, latent_in)
    first = (me * local).astype(jnp.int32).reshape(1)
    columns = in_vmem(jnp.pad(router.T, ((0, 16 - local), (0, 0))))
    down = expert_down.reshape(local * eff, lat)

    batch = 4 * rows
    flops = 2 * batch * local * eff * lat * 3
    smem = pl.BlockSpec(memory_space=pltpu.SMEM)
    anywhere = pl.BlockSpec(memory_space=pl.ANY)
    results = [
        pltpu.VMEM((2 * rows, wide), jnp.float32),
        pltpu.VMEM((2 * rows, wide), jnp.bfloat16),
    ]
    inner = pltpu.VMEM((batch, local * eff), jnp.bfloat16)
    params = pltpu.CompilerParams(vmem_limit_bytes=16 * 1024 * 1024)
    cost = pl.CostEstimate(flops=flops, bytes_accessed=0, transcendentals=0)
    n_copies = local * 2 * eff // STEP + lat // STEP
    run_first = pl.pallas_call(
        first_kernel,
        out_shape=results + [pltpu.VMEM(gate_up.shape, gate_up.dtype), pltpu.VMEM(down.shape, down.dtype)],
        in_specs=[smem, vmem, vmem, vmem, anywhere, anywhere],
        out_specs=[vmem] * 4,
        scratch_shapes=[inner, pltpu.SemaphoreType.DMA((n_copies,))],
        compiler_params=params,
        cost_estimate=cost,
        name="experts_first",
    )
    run_next = pl.pallas_call(
        next_kernel,
        out_shape=results,
        in_specs=[smem] + [vmem] * 5 + [anywhere],
        out_specs=[vmem] * 2,
        scratch_shapes=[inner],
        compiler_params=params,
        cost_estimate=cost,
        name="experts_next",
    )

    def group_pass(mine):
        z1 = swap(mine, 4)
        z2 = swap(mine, 8)
        z3 = swap(z2, 4)
        total = None
        for k, one in enumerate((mine, z1, z2, z3)):
            pair = jnp.concatenate([one, swap(one, 2)], axis=0)
            other = swap(pair, 1)
            pair, other = in_vmem(pair), in_vmem(other)
            if k == 0:
                keep, send, up_v, down_v = run_first(first, pair, other, columns, in_hbm(gate_up), in_hbm(down))
            else:
                keep, send = run_next(first, pair, other, columns, in_vmem(up_v), in_vmem(down_v), in_vmem(last))
            last = send
            sums = keep + swap(send, 1).astype(jnp.float32)
            sums = sums[:rows] + swap(sums[rows:].astype(jnp.bfloat16), 2).astype(jnp.float32)
            if k > 0:
                sums = swap(sums.astype(jnp.bfloat16), 4 * k).astype(jnp.float32)
            total = sums if total is None else total + sums
        return total

    def finish(total):
        return (total[:, :lat] / total[:, lat : lat + 1]).astype(jnp.bfloat16)

    if n_dev == GROUP:
        return finish(group_pass(packet))

    def next_group(x):
        return lax.ppermute(x, "exp", [(i, (i + GROUP) % n_dev) for i in range(n_dev)])

    def step(carry, _):
        mine, total = carry
        total = total + group_pass(mine)
        return (next_group(mine), next_group(total)), None

    start = (packet, jnp.zeros((rows, wide), jnp.float32))
    (_, total), _ = lax.scan(step, start, None, length=n_dev // GROUP)
    return finish(total)


def solution(mesh):
    placed = (
        P(("grp", "exp"), None),
        P(("grp", "exp"), None),
        P(None, "exp"),
        P("exp", None, None),
        P("exp", None, None),
    )
    return jax.shard_map(
        on_device, mesh=mesh, in_specs=placed, out_specs=P(("grp", "exp"), None), check_vma=False
    )
```

```python
import jax
import jax.numpy as jnp
from jax import lax
from jax.experimental import pallas as pl
from jax.experimental.pallas import tpu as pltpu
from jax.sharding import PartitionSpec as P

GROUP = 16
TAIL = 128
SCALE = 2.0**40
STEP = 256
PIECE = 256


def pack_kernel(ids_ref, row_ref, out_ref):
    rows, lat = row_ref.shape
    top = ids_ref.shape[0]
    out_ref[:, :lat] = row_ref[...]
    ids = ids_ref[...].astype(jnp.float32)
    ids = jnp.concatenate([ids, jnp.full((top, TAIL - rows), -1.0, jnp.float32)], axis=1)
    ids = jnp.concatenate([ids, jnp.full((TAIL - top, TAIL), -1.0, jnp.float32)], axis=0)
    out_ref[:, lat:] = ids.T[:rows].astype(jnp.bfloat16)


def load_kernel(router_ref, up_hbm, down_hbm, dep_ref, columns_ref, up_ref, down_ref, sems):
    copies = []
    for src, dst in ((up_hbm, up_ref), (down_hbm, down_ref)):
        for e in range(src.shape[0]):
            for r in range(0, src.shape[1], PIECE):
                at = (e, pl.ds(r, PIECE))
                copies.append(pltpu.make_async_copy(src.at[at], dst.at[at], sems.at[len(copies)]))
    for copy in copies:
        copy.start()
    columns_ref[...] = jnp.zeros_like(columns_ref)
    columns_ref[: router_ref.shape[0], :] = router_ref[...]
    for copy in copies:
        copy.wait()


def join_kernel(a_ref, b_ref, *refs):
    out_ref = refs[-1]
    rows = a_ref.shape[0]
    out_ref[:rows] = a_ref[...]
    out_ref[rows:] = b_ref[...]


def expert_kernel(first_ref, pair_ref, other_ref, columns_ref, up_ref, down_ref, *refs):
    keep_ref, send_ref, inner_ref = refs[-3:]
    half, wide = pair_ref.shape
    lat = wide - TAIL
    local, eff, _ = down_ref.shape
    x = jnp.concatenate([pair_ref[:, :lat], other_ref[:, :lat]], axis=0)
    tail = jnp.concatenate([pair_ref[:, lat:], other_ref[:, lat:]], axis=0).astype(jnp.float32)
    logits = lax.dot_general(
        x, columns_ref[...], (((1,), (1,)), ((), ())), preferred_element_type=jnp.float32
    )
    sums = jnp.zeros((2 * half, 1), jnp.float32)
    for e in range(local):
        label = (first_ref[0] + e).astype(jnp.float32)
        mask = jnp.max(jnp.where(tail == label, 1.0, 0.0), axis=1, keepdims=True)
        score = jax.nn.sigmoid(logits[:, e : e + 1]) * (mask * SCALE)
        sums = sums + score
        for c in range(0, eff, STEP):
            gate = jnp.dot(x, up_ref[e, :, c : c + STEP], preferred_element_type=jnp.float32)
            up = jnp.dot(x, up_ref[e, :, eff + c : eff + c + STEP], preferred_element_type=jnp.float32)
            inner_ref[:, e * eff + c : e * eff + c + STEP] = (
                gate / (1.0 + jnp.exp(-gate)) * up * score
            ).astype(jnp.bfloat16)
    inner = inner_ref[...]
    for c in range(0, lat, STEP):
        down = down_ref[:, :, c : c + STEP].reshape(local * eff, STEP)
        part = jnp.dot(inner, down, preferred_element_type=jnp.float32)
        keep_ref[:, c : c + STEP] = part[:half]
        send_ref[:, c : c + STEP] = part[half:].astype(jnp.bfloat16)
    lane = lax.broadcasted_iota(jnp.int32, (2 * half, TAIL), 1)
    sums = jnp.where(lane == 0, sums, 0.0)
    keep_ref[:, lat:] = sums[:half]
    send_ref[:, lat:] = sums[half:].astype(jnp.bfloat16)


def fold_kernel(mine_ref, came_ref, *refs):
    keep_ref, send_ref = refs[-2:]
    rows = keep_ref.shape[0]
    keep_ref[...] = mine_ref[:rows] + came_ref[:rows].astype(jnp.float32)
    send_ref[...] = (mine_ref[rows:] + came_ref[rows:].astype(jnp.float32)).astype(jnp.bfloat16)


def add_kernel(mine_ref, came_ref, out_ref):
    out_ref[...] = (mine_ref[...] + came_ref[...].astype(jnp.float32)).astype(jnp.bfloat16)


def total_kernel(*refs):
    total_ref = refs[-1]
    total = refs[0][...]
    for ref in refs[1:-1]:
        total = total + ref[...].astype(jnp.float32)
    total_ref[...] = total


def finish_kernel(*refs):
    out_ref = refs[-1]
    lat = out_ref.shape[1]
    total = refs[0][...]
    for ref in refs[1:-1]:
        total = total + ref[...].astype(jnp.float32)
    out_ref[...] = (total[:, :lat] / total[:, lat : lat + 1]).astype(jnp.bfloat16)


def in_vmem(x):
    return pltpu.with_memory_space_constraint(x, pltpu.VMEM)


def in_hbm(x):
    return pltpu.with_memory_space_constraint(x, pltpu.HBM)


VMEM = pl.BlockSpec(memory_space=pltpu.VMEM)
ANY = pl.BlockSpec(memory_space=pl.ANY)


def call(kernel, outs, args, deps=(), smem=(), hbm=(), scratch=(), cost=None):
    specs = [pl.BlockSpec(memory_space=pltpu.SMEM)] * len(smem) + [VMEM] * len(args)
    specs += [ANY] * (len(hbm) + len(deps))
    operands = list(smem) + [in_vmem(a) for a in args] + [in_hbm(h) for h in hbm] + [in_vmem(d) for d in deps]
    return pl.pallas_call(
        kernel,
        out_shape=outs,
        in_specs=specs,
        out_specs=[VMEM] * len(outs),
        scratch_shapes=list(scratch),
        compiler_params=pltpu.CompilerParams(vmem_limit_bytes=16 * 1024 * 1024),
        cost_estimate=cost or pl.CostEstimate(flops=0, bytes_accessed=200_000, transcendentals=0),
        name=kernel.__name__.removesuffix("_kernel"),
    )(*operands)


def on_device(latent_in, routes, router, gate_up, expert_down):
    n_dev = lax.axis_size("exp")
    local = gate_up.shape[0]
    eff = expert_down.shape[1]
    rows, lat = latent_in.shape
    wide = lat + TAIL
    first = (lax.axis_index("exp") * local).astype(jnp.int32).reshape(1)

    def swap(x, bits):
        return lax.ppermute(x, "exp", [(i, i ^ bits) for i in range(n_dev)])

    def space(height, dtype):
        return pltpu.VMEM((height, wide), dtype)

    def weights(dep):
        moved = gate_up.size + expert_down.size
        return call(
            load_kernel,
            [
                pltpu.VMEM((16, lat), jnp.bfloat16),
                pltpu.VMEM(gate_up.shape, gate_up.dtype),
                pltpu.VMEM(expert_down.shape, expert_down.dtype),
            ],
            [router.T],
            deps=[dep],
            hbm=[gate_up, expert_down],
            scratch=[pltpu.SemaphoreType.DMA((local * (lat + eff) // PIECE,))],
            cost=pl.CostEstimate(flops=0, bytes_accessed=4 * moved, transcendentals=0),
        )

    def join(a, b, deps=()):
        return call(join_kernel, [space(2 * rows, jnp.bfloat16)], [a, b], deps)[0]

    def experts(pair, other, loaded, deps=()):
        return call(
            expert_kernel,
            [space(2 * rows, jnp.float32), space(2 * rows, jnp.bfloat16)],
            [pair, other, *loaded],
            deps,
            smem=[first],
            scratch=[pltpu.VMEM((4 * rows, local * eff), jnp.bfloat16)],
            cost=pl.CostEstimate(
                flops=2 * 4 * rows * local * eff * lat * 3, bytes_accessed=0, transcendentals=0
            ),
        )

    def fold(mine, came, deps=()):
        return call(fold_kernel, [space(rows, jnp.float32), space(rows, jnp.bfloat16)], [mine, came], deps)

    def add(mine, came):
        return call(add_kernel, [space(rows, jnp.bfloat16)], [mine, came])[0]

    def group_pass(mine):
        block = {0: mine, 2: swap(mine, 8), 1: swap(mine, 4)}
        block[3] = swap(block[2], 4)
        other = {k: swap(block[k], 2) for k in (2, 1, 3, 0)}
        loaded = weights(block[2])
        pair, far = {}, {}
        keep, send, came, fold_keep, fold_send, y_came, z_send = {}, {}, {}, {}, {}, {}, {}

        def gather(k, deps=()):
            pair[k] = join(block[k], other[k], deps)
            far[k] = swap(pair[k], 1)

        def compute(k, deps=()):
            keep[k], send[k] = experts(pair[k], far[k], loaded, deps)
            came[k] = swap(send[k], 1)

        def reduce_core(k):
            fold_keep[k], fold_send[k] = fold(keep[k], came[k])
            y_came[k] = swap(fold_send[k], 2)

        def reduce_y(k):
            z_send[k] = add(fold_keep[k], y_came[k])
            return swap(z_send[k], 4 * k)

        gather(2)
        compute(2, [block[1], block[3]])
        gather(3, [send[2]])
        gather(1, [send[2]])
        compute(3, [send[2], pair[1]])
        gather(0, [send[3]])
        reduce_core(2)
        compute(1, [send[3], fold_send[2], pair[0]])
        reduce_core(3)
        z_2 = reduce_y(2)
        compute(0, [send[1], fold_send[3], z_send[2]])
        reduce_core(1)
        z_3 = reduce_y(3)
        z_1 = reduce_y(1)
        reduce_core(0)
        return fold_keep[0], y_came[0], z_1, z_2, z_3

    packet = call(pack_kernel, [space(rows, jnp.bfloat16)], [routes.T, latent_in])[0]

    def finish(parts):
        return pl.pallas_call(
            finish_kernel,
            out_shape=jax.ShapeDtypeStruct((rows, lat), jnp.bfloat16),
            in_specs=[VMEM] * len(parts),
            out_specs=VMEM,
            name="finish",
        )(*[in_vmem(p) for p in parts])

    if n_dev == GROUP:
        return finish(group_pass(packet))

    def next_group(x):
        return lax.ppermute(x, "exp", [(i, (i + GROUP) % n_dev) for i in range(n_dev)])

    def step(carry, _):
        mine, total = carry
        total = call(total_kernel, [space(rows, jnp.float32)], [total, *group_pass(mine)])[0]
        return (next_group(mine), next_group(total)), None

    start = (packet, jnp.zeros((rows, wide), jnp.float32))
    (_, total), _ = lax.scan(step, start, None, length=n_dev // GROUP)
    return finish([total])


def solution(mesh):
    placed = (
        P(("grp", "exp"), None),
        P(("grp", "exp"), None),
        P(None, "exp"),
        P("exp", None, None),
        P("exp", None, None),
    )
    return jax.shard_map(
        on_device, mesh=mesh, in_specs=placed, out_specs=P(("grp", "exp"), None), check_vma=False
    )
```

```python
import functools

import jax
import jax.numpy as jnp
from jax import lax
from jax.experimental import pallas as pl
from jax.experimental.pallas import tpu as pltpu
from jax.sharding import PartitionSpec as P

GROUP = 16
TAIL = 128
K_COST = 10
SCALE = 2.0**40
STEP = 256
PIECE = 256


def pack_kernel(ids_ref, row_ref, out_ref):
    rows, lat = row_ref.shape
    top = ids_ref.shape[0]
    out_ref[:, :lat] = row_ref[...]
    ids = ids_ref[...].astype(jnp.float32)
    ids = jnp.concatenate([ids, jnp.full((top, TAIL - rows), -1.0, jnp.float32)], axis=1)
    ids = jnp.concatenate([ids, jnp.full((TAIL - top, TAIL), -1.0, jnp.float32)], axis=0)
    out_ref[:, lat:] = ids.T[:rows].astype(jnp.bfloat16)


def load_kernel(router_ref, up_hbm, down_hbm, dep_ref, columns_ref, up_ref, down_ref, sems):
    copies = []
    for src, dst in ((up_hbm, up_ref), (down_hbm, down_ref)):
        for e in range(src.shape[0]):
            for r in range(0, src.shape[1], PIECE):
                at = (e, pl.ds(r, PIECE))
                copies.append(pltpu.make_async_copy(src.at[at], dst.at[at], sems.at[len(copies)]))
    for copy in copies:
        copy.start()
    columns_ref[...] = jnp.zeros_like(columns_ref)
    columns_ref[: router_ref.shape[0], :] = router_ref[...]
    for copy in copies:
        copy.wait()


def join_kernel(a_ref, b_ref, *refs):
    out_ref = refs[-1]
    rows = a_ref.shape[0]
    out_ref[:rows] = a_ref[...]
    out_ref[rows:] = b_ref[...]


def expert_kernel(two, first_ref, pair_ref, other_ref, columns_ref, up_ref, down_ref, *refs):
    inner_ref, result_ref = refs[-2:]
    half, wide = pair_ref.shape
    lat = wide - TAIL
    local, eff, _ = down_ref.shape
    slots = result_ref.shape[0] // local
    x = jnp.concatenate([pair_ref[:, :lat], other_ref[:, :lat]], axis=0)
    tail = jnp.concatenate([pair_ref[:, lat:], other_ref[:, lat:]], axis=0).astype(jnp.float32)

    outs = refs[-4 - two : -2]

    def put(lanes, value):
        outs[0][:, lanes] = value[:half]
        height = half // (1 + two)
        for i, out in enumerate(outs[1:]):
            out[:, lanes] = value[half + i * height : half + (i + 1) * height].astype(jnp.bfloat16)

    def logits_of(rows):
        return lax.dot_general(
            rows, columns_ref[...], (((1,), (1,)), ((), ())), preferred_element_type=jnp.float32
        )

    logits = logits_of(x)
    lane = lax.broadcasted_iota(jnp.int32, (2 * half, TAIL), 1)
    masks, sums = [], jnp.zeros((2 * half, 1), jnp.float32)
    marks = jnp.zeros((2 * half, TAIL), jnp.float32)
    for e in range(local):
        label = (first_ref[0] + e).astype(jnp.float32)
        mask = jnp.max(jnp.where(tail == label, 1.0, 0.0), axis=1, keepdims=True)
        sums = sums + jax.nn.sigmoid(logits[:, e : e + 1]) * (mask * SCALE)
        marks = jnp.where(lane == e, mask, marks)
        masks.append(mask)
    row = lax.broadcasted_iota(jnp.int32, (2 * half, 2 * half), 0)
    col = lax.broadcasted_iota(jnp.int32, (2 * half, 2 * half), 1)
    before = jnp.where(col < row, 1.0, 0.0).astype(jnp.bfloat16)
    place = jnp.dot(before, marks.astype(jnp.bfloat16), preferred_element_type=jnp.float32)
    slot = lax.broadcasted_iota(jnp.int32, (2 * half, slots), 1).astype(jnp.float32)
    spread = jnp.concatenate(
        [jnp.where((slot == place[:, e : e + 1]) & (masks[e] > 0.0), 1.0, 0.0) for e in range(local)], axis=1
    ).astype(jnp.bfloat16)
    packed = lax.dot_general(
        spread, x, (((0,), (0,)), ((), ())), preferred_element_type=jnp.float32
    ).astype(jnp.bfloat16)
    scores = jax.nn.sigmoid(logits_of(packed)) * SCALE
    for e in range(local):
        mine = slice(e * slots, (e + 1) * slots)
        rows = packed[mine]
        score = scores[mine, e : e + 1]
        for c in range(0, eff, STEP):
            gate = jnp.dot(rows, up_ref[e, :, c : c + STEP], preferred_element_type=jnp.float32)
            up = jnp.dot(rows, up_ref[e, :, eff + c : eff + c + STEP], preferred_element_type=jnp.float32)
            inner_ref[mine, c : c + STEP] = (gate / (1.0 + jnp.exp(-gate)) * up * score).astype(jnp.bfloat16)
    for e in range(local):
        mine = slice(e * slots, (e + 1) * slots)
        result_ref[mine, :] = jnp.dot(
            inner_ref[mine, :], down_ref[e], preferred_element_type=jnp.float32
        ).astype(jnp.bfloat16)
    for c in range(0, lat, STEP):
        part = jnp.dot(spread, result_ref[:, c : c + STEP], preferred_element_type=jnp.float32)
        put(slice(c, c + STEP), part)
    put(slice(lat, wide), jnp.where(lane == 0, sums, 0.0))


def tie_kernel(*refs):
    pass


def fold_kernel(mine_ref, *refs):
    keep_ref, send_ref = refs[-2:]
    rows = keep_ref.shape[0]
    came = [refs[0][:rows], refs[0][rows:]] if len(refs) == 3 else [refs[0][...], refs[1][...]]
    keep_ref[...] = mine_ref[:rows] + came[0].astype(jnp.float32)
    send_ref[...] = (mine_ref[rows:] + came[1].astype(jnp.float32)).astype(jnp.bfloat16)


def add_kernel(mine_ref, came_ref, *refs):
    out_ref = refs[-1]
    out_ref[...] = (mine_ref[...] + came_ref[...].astype(jnp.float32)).astype(jnp.bfloat16)


def total_kernel(*refs):
    total_ref = refs[-1]
    total = refs[0][...]
    for ref in refs[1:-1]:
        total = total + ref[...].astype(jnp.float32)
    total_ref[...] = total


def finish_kernel(*refs):
    out_ref = refs[-1]
    lat = out_ref.shape[1]
    total = refs[0][...]
    for ref in refs[1:-1]:
        total = total + ref[...].astype(jnp.float32)
    out_ref[...] = (total[:, :lat] / total[:, lat : lat + 1]).astype(jnp.bfloat16)


def in_vmem(x):
    return pltpu.with_memory_space_constraint(x, pltpu.VMEM)


def in_hbm(x):
    return pltpu.with_memory_space_constraint(x, pltpu.HBM)


VMEM = pl.BlockSpec(memory_space=pltpu.VMEM)
ANY = pl.BlockSpec(memory_space=pl.ANY)


def modelled(us):
    return pl.CostEstimate(flops=0, bytes_accessed=int(us * 3.69e6), transcendentals=0)


def call(kernel, outs, args, deps=(), smem=(), hbm=(), scratch=(), cost=None, aliases=None):
    specs = [pl.BlockSpec(memory_space=pltpu.SMEM)] * len(smem) + [VMEM] * len(args)
    specs += [ANY] * (len(hbm) + len(deps))
    operands = list(smem) + [in_vmem(a) for a in args] + [in_hbm(h) for h in hbm] + [in_vmem(d) for d in deps]
    return pl.pallas_call(
        kernel,
        out_shape=outs,
        in_specs=specs,
        out_specs=[VMEM] * len(outs),
        scratch_shapes=list(scratch),
        compiler_params=pltpu.CompilerParams(vmem_limit_bytes=16 * 1024 * 1024),
        cost_estimate=cost or modelled(0.1),
        input_output_aliases=aliases or {},
        name=getattr(kernel, "func", kernel).__name__.removesuffix("_kernel"),
    )(*operands)


def on_device(latent_in, routes, router, gate_up, expert_down):
    n_dev = lax.axis_size("exp")
    local = gate_up.shape[0]
    eff = expert_down.shape[1]
    rows, lat = latent_in.shape
    wide = lat + TAIL
    first = (lax.axis_index("exp") * local).astype(jnp.int32).reshape(1)

    def swap(x, bits):
        return lax.ppermute(x, "exp", [(i, i ^ bits) for i in range(n_dev)])

    def space(height, dtype):
        return pltpu.VMEM((height, wide), dtype)

    def weights(dep):
        return call(
            load_kernel,
            [
                pltpu.VMEM((16, lat), jnp.bfloat16),
                pltpu.VMEM(gate_up.shape, gate_up.dtype),
                pltpu.VMEM(expert_down.shape, expert_down.dtype),
            ],
            [router.T],
            deps=[dep],
            hbm=[gate_up, expert_down],
            scratch=[pltpu.SemaphoreType.DMA((local * (lat + eff) // PIECE,))],
            cost=modelled(5),
        )

    def join(a, b, deps=()):
        return call(join_kernel, [space(2 * rows, jnp.bfloat16)], [a, b], deps)[0]

    bound = 2 * ((rows * routes.shape[1] + local * n_dev - 1) // (local * n_dev))
    slots = 4 * bound

    def experts(pair, other, loaded, deps=(), two=0):
        return call(
            functools.partial(expert_kernel, two),
            [space(2 * rows, jnp.float32)] + [space(2 * rows // (1 + two), jnp.bfloat16)] * (1 + two),
            [pair, other, *loaded],
            deps,
            smem=[first],
            scratch=[
                pltpu.VMEM((local * slots, eff), jnp.bfloat16),
                pltpu.VMEM((local * slots, lat), jnp.bfloat16),
            ],
            cost=modelled(K_COST),
        )

    def tie(x, deps):
        return call(tie_kernel, [space(x.shape[0], x.dtype)], [x], deps, aliases={0: 0})[0]

    def fold(mine, *came):
        return call(fold_kernel, [space(rows, jnp.float32), space(rows, jnp.bfloat16)], [mine, *came])

    def add(mine, came, deps=(), cost=None):
        return call(add_kernel, [space(rows, jnp.bfloat16)], [mine, came], deps, cost=cost)[0]

    def group_pass(mine):
        loaded = weights(mine)
        z_2, z_1 = swap(mine, 8), swap(mine, 4)
        block = {0: mine, 2: tie(z_2, [loaded[0]]), 1: z_1}
        block[3] = swap(block[2], 4)
        other = {k: swap(block[k], 2) for k in (2, 1, 3, 0)}
        pair, far = {}, {}
        keep, send, came, fold_keep, fold_send, y_came, z_send = {}, {}, {}, {}, {}, {}, {}

        def gather(k, deps=()):
            pair[k] = join(block[k], other[k], deps)
            far[k] = swap(pair[k], 1)

        def compute(k, deps=(), two=0):
            keep[k], send[k], *more = experts(pair[k], far[k], loaded, deps, two)
            came[k] = [swap(part, 1) for part in (send[k], *more)]

        def reduce_core(k):
            fold_keep[k], fold_send[k] = fold(keep[k], *came[k])
            y_came[k] = swap(fold_send[k], 2)

        def reduce_y(k, deps=(), cost=None):
            z_send[k] = add(fold_keep[k], y_came[k], deps, cost)
            return swap(z_send[k], 4 * k)

        gather(2, [block[1], block[3]])
        compute(2)
        gather(3, [send[2]])
        gather(1)
        compute(3, [send[2], pair[1]])
        gather(0, [send[3]])
        reduce_core(2)
        compute(1, [send[3], fold_send[2], pair[0]], two=1)
        reduce_core(3)
        z_2 = reduce_y(2)
        compute(0, [send[1], fold_send[3], z_send[2]], two=1)
        reduce_core(1)
        z_3 = reduce_y(3, [z_2], modelled(K_COST))
        z_1 = reduce_y(1)
        reduce_core(0)
        return fold_keep[0], y_came[0], z_1, z_2, z_3

    packet = call(pack_kernel, [space(rows, jnp.bfloat16)], [routes.T, latent_in])[0]

    def finish(parts):
        return pl.pallas_call(
            finish_kernel,
            out_shape=jax.ShapeDtypeStruct((rows, lat), jnp.bfloat16),
            in_specs=[VMEM] * len(parts),
            out_specs=VMEM,
            name="finish",
        )(*[in_vmem(p) for p in parts])

    if n_dev == GROUP:
        return finish(group_pass(packet))

    def next_group(x):
        return lax.ppermute(x, "exp", [(i, (i + GROUP) % n_dev) for i in range(n_dev)])

    def step(carry, _):
        mine, total = carry
        total = call(total_kernel, [space(rows, jnp.float32)], [total, *group_pass(mine)])[0]
        return (next_group(mine), next_group(total)), None

    start = (packet, jnp.zeros((rows, wide), jnp.float32))
    (_, total), _ = lax.scan(step, start, None, length=n_dev // GROUP)
    return finish([total])


def solution(mesh):
    placed = (
        P(("grp", "exp"), None),
        P(("grp", "exp"), None),
        P(None, "exp"),
        P("exp", None, None),
        P("exp", None, None),
    )
    return jax.shard_map(
        on_device, mesh=mesh, in_specs=placed, out_specs=P(("grp", "exp"), None), check_vma=False
    )
```

```python
import functools

import jax
import jax.numpy as jnp
from jax import lax
from jax.experimental import pallas as pl
from jax.experimental.pallas import tpu as pltpu
from jax.sharding import PartitionSpec as P

GROUP = 16
TAIL = 128
K_COST = 10
SCALE = 2.0**40
STEP = 256
PIECE = 256


def pack_kernel(ids_hbm, row_hbm, out_ref, ids_ref, sems):
    rows, lat = row_hbm.shape
    top = ids_hbm.shape[0]
    get_ids = pltpu.make_async_copy(ids_hbm, ids_ref, sems.at[0])
    get_rows = pltpu.make_async_copy(row_hbm, out_ref.at[:, pl.ds(0, lat)], sems.at[1])
    get_ids.start()
    get_rows.start()
    get_ids.wait()
    ids = ids_ref[...].astype(jnp.float32)
    ids = jnp.concatenate([ids, jnp.full((top, TAIL - rows), -1.0, jnp.float32)], axis=1)
    ids = jnp.concatenate([ids, jnp.full((TAIL - top, TAIL), -1.0, jnp.float32)], axis=0)
    out_ref[:, lat:] = ids.T[:rows].astype(jnp.bfloat16)
    get_rows.wait()


def load_kernel(router_hbm, up_hbm, down_hbm, dep_ref, columns_ref, up_ref, down_ref, router_ref, sems):
    get_router = pltpu.make_async_copy(router_hbm, router_ref, sems.at[0])
    get_router.start()
    copies = []
    for src, dst in ((up_hbm, up_ref), (down_hbm, down_ref)):
        for e in range(src.shape[0]):
            for r in range(0, src.shape[1], PIECE):
                at = (e, pl.ds(r, PIECE))
                copies.append(pltpu.make_async_copy(src.at[at], dst.at[at], sems.at[1 + len(copies)]))
    for copy in copies:
        copy.start()
    columns_ref[...] = jnp.zeros_like(columns_ref)
    get_router.wait()
    columns_ref[: router_ref.shape[0], :] = router_ref[...]
    for copy in copies:
        copy.wait()


def join_kernel(a_ref, b_ref, *refs):
    out_ref = refs[-1]
    rows = a_ref.shape[0]
    out_ref[:rows] = a_ref[...]
    out_ref[rows:] = b_ref[...]


def expert_kernel(two, first_ref, pair_ref, other_ref, columns_ref, up_ref, down_ref, *refs):
    inner_ref, result_ref = refs[-2:]
    half, wide = pair_ref.shape
    lat = wide - TAIL
    local, eff, _ = down_ref.shape
    slots = result_ref.shape[0] // local
    x = jnp.concatenate([pair_ref[:, :lat], other_ref[:, :lat]], axis=0)
    tail = jnp.concatenate([pair_ref[:, lat:], other_ref[:, lat:]], axis=0).astype(jnp.float32)

    outs = refs[-4 - two : -2]

    def put(lanes, value):
        outs[0][:, lanes] = value[:half]
        height = half // (1 + two)
        for i, out in enumerate(outs[1:]):
            out[:, lanes] = value[half + i * height : half + (i + 1) * height].astype(jnp.bfloat16)

    def logits_of(rows):
        return lax.dot_general(
            rows, columns_ref[...], (((1,), (1,)), ((), ())), preferred_element_type=jnp.float32
        )

    logits = logits_of(x)
    lane = lax.broadcasted_iota(jnp.int32, (2 * half, TAIL), 1)
    masks, sums = [], jnp.zeros((2 * half, 1), jnp.float32)
    marks = jnp.zeros((2 * half, TAIL), jnp.float32)
    for e in range(local):
        label = (first_ref[0] + e).astype(jnp.float32)
        mask = jnp.max(jnp.where(tail == label, 1.0, 0.0), axis=1, keepdims=True)
        sums = sums + jax.nn.sigmoid(logits[:, e : e + 1]) * (mask * SCALE)
        marks = jnp.where(lane == e, mask, marks)
        masks.append(mask)
    row = lax.broadcasted_iota(jnp.int32, (2 * half, 2 * half), 0)
    col = lax.broadcasted_iota(jnp.int32, (2 * half, 2 * half), 1)
    before = jnp.where(col < row, 1.0, 0.0).astype(jnp.bfloat16)
    place = jnp.dot(before, marks.astype(jnp.bfloat16), preferred_element_type=jnp.float32)
    slot = lax.broadcasted_iota(jnp.int32, (2 * half, slots), 1).astype(jnp.float32)
    spread = jnp.concatenate(
        [jnp.where((slot == place[:, e : e + 1]) & (masks[e] > 0.0), 1.0, 0.0) for e in range(local)], axis=1
    ).astype(jnp.bfloat16)
    packed = lax.dot_general(
        spread, x, (((0,), (0,)), ((), ())), preferred_element_type=jnp.float32
    ).astype(jnp.bfloat16)
    scores = jax.nn.sigmoid(logits_of(packed)) * SCALE
    for e in range(local):
        mine = slice(e * slots, (e + 1) * slots)
        rows = packed[mine]
        score = scores[mine, e : e + 1]
        for c in range(0, eff, STEP):
            gate = jnp.dot(rows, up_ref[e, :, c : c + STEP], preferred_element_type=jnp.float32)
            up = jnp.dot(rows, up_ref[e, :, eff + c : eff + c + STEP], preferred_element_type=jnp.float32)
            inner_ref[mine, c : c + STEP] = (gate / (1.0 + jnp.exp(-gate)) * up * score).astype(jnp.bfloat16)
    for e in range(local):
        mine = slice(e * slots, (e + 1) * slots)
        result_ref[mine, :] = jnp.dot(
            inner_ref[mine, :], down_ref[e], preferred_element_type=jnp.float32
        ).astype(jnp.bfloat16)
    for c in range(0, lat, STEP):
        part = jnp.dot(spread, result_ref[:, c : c + STEP], preferred_element_type=jnp.float32)
        put(slice(c, c + STEP), part)
    put(slice(lat, wide), jnp.where(lane == 0, sums, 0.0))


def tie_kernel(*refs):
    pass


def fold_kernel(mine_ref, *refs):
    keep_ref, send_ref = refs[-2:]
    rows = keep_ref.shape[0]
    came = [refs[0][:rows], refs[0][rows:]] if len(refs) == 3 else [refs[0][...], refs[1][...]]
    keep_ref[...] = mine_ref[:rows] + came[0].astype(jnp.float32)
    send_ref[...] = (mine_ref[rows:] + came[1].astype(jnp.float32)).astype(jnp.bfloat16)


def add_kernel(mine_ref, came_ref, *refs):
    out_ref = refs[-1]
    out_ref[...] = (mine_ref[...] + came_ref[...].astype(jnp.float32)).astype(jnp.bfloat16)


def total_kernel(*refs):
    total_ref = refs[-1]
    total = refs[0][...]
    for ref in refs[1:-1]:
        total = total + ref[...].astype(jnp.float32)
    total_ref[...] = total


def finish_kernel(*refs):
    out_ref = refs[-1]
    lat = out_ref.shape[1]
    total = refs[0][...]
    for ref in refs[1:-1]:
        total = total + ref[...].astype(jnp.float32)
    out_ref[...] = (total[:, :lat] / total[:, lat : lat + 1]).astype(jnp.bfloat16)


def in_vmem(x):
    return pltpu.with_memory_space_constraint(x, pltpu.VMEM)


def in_hbm(x):
    return pltpu.with_memory_space_constraint(x, pltpu.HBM)


VMEM = pl.BlockSpec(memory_space=pltpu.VMEM)
ANY = pl.BlockSpec(memory_space=pl.ANY)


def modelled(us):
    return pl.CostEstimate(flops=0, bytes_accessed=int(us * 3.69e6), transcendentals=0)


def call(kernel, outs, args, deps=(), smem=(), hbm=(), scratch=(), cost=None, aliases=None):
    specs = [pl.BlockSpec(memory_space=pltpu.SMEM)] * len(smem) + [VMEM] * len(args)
    specs += [ANY] * (len(hbm) + len(deps))
    operands = list(smem) + [in_vmem(a) for a in args] + [in_hbm(h) for h in hbm] + [in_vmem(d) for d in deps]
    return pl.pallas_call(
        kernel,
        out_shape=outs,
        in_specs=specs,
        out_specs=[VMEM] * len(outs),
        scratch_shapes=list(scratch),
        compiler_params=pltpu.CompilerParams(vmem_limit_bytes=16 * 1024 * 1024),
        cost_estimate=cost or modelled(0.1),
        input_output_aliases=aliases or {},
        name=getattr(kernel, "func", kernel).__name__.removesuffix("_kernel"),
    )(*operands)


def on_device(latent_in, routes, router, gate_up, expert_down):
    n_dev = lax.axis_size("exp")
    local = gate_up.shape[0]
    eff = expert_down.shape[1]
    rows, lat = latent_in.shape
    wide = lat + TAIL
    first = (lax.axis_index("exp") * local).astype(jnp.int32).reshape(1)

    def swap(x, bits):
        return lax.ppermute(x, "exp", [(i, i ^ bits) for i in range(n_dev)])

    def space(height, dtype):
        return pltpu.VMEM((height, wide), dtype)

    def weights(dep):
        return call(
            load_kernel,
            [
                pltpu.VMEM((16, lat), jnp.bfloat16),
                pltpu.VMEM(gate_up.shape, gate_up.dtype),
                pltpu.VMEM(expert_down.shape, expert_down.dtype),
            ],
            [],
            deps=[dep],
            hbm=[router.T, gate_up, expert_down],
            scratch=[
                pltpu.VMEM((local, lat), jnp.bfloat16),
                pltpu.SemaphoreType.DMA((1 + local * (lat + eff) // PIECE,)),
            ],
            cost=modelled(5),
        )

    def join(a, b, deps=()):
        return call(join_kernel, [space(2 * rows, jnp.bfloat16)], [a, b], deps)[0]

    bound = 2 * ((rows * routes.shape[1] + local * n_dev - 1) // (local * n_dev))
    slots = 4 * bound

    def experts(pair, other, loaded, deps=(), two=0):
        return call(
            functools.partial(expert_kernel, two),
            [space(2 * rows, jnp.float32)] + [space(2 * rows // (1 + two), jnp.bfloat16)] * (1 + two),
            [pair, other, *loaded],
            deps,
            smem=[first],
            scratch=[
                pltpu.VMEM((local * slots, eff), jnp.bfloat16),
                pltpu.VMEM((local * slots, lat), jnp.bfloat16),
            ],
            cost=modelled(K_COST),
        )

    def tie(x, deps):
        return call(tie_kernel, [space(x.shape[0], x.dtype)], [x], deps, aliases={0: 0})[0]

    def fold(mine, *came):
        return call(fold_kernel, [space(rows, jnp.float32), space(rows, jnp.bfloat16)], [mine, *came])

    def add(mine, came, deps=(), cost=None):
        return call(add_kernel, [space(rows, jnp.bfloat16)], [mine, came], deps, cost=cost)[0]

    def group_pass(mine):
        loaded = weights(mine)
        z_2, z_1 = swap(mine, 8), swap(mine, 4)
        block = {0: mine, 2: tie(z_2, loaded), 1: z_1}
        block[3] = swap(block[2], 4)
        other = {k: swap(block[k], 2) for k in (2, 1, 3, 0)}
        pair, far = {}, {}
        keep, send, came, fold_keep, fold_send, y_came, z_send = {}, {}, {}, {}, {}, {}, {}

        def gather(k, deps=()):
            pair[k] = join(block[k], other[k], deps)
            far[k] = swap(pair[k], 1)

        def compute(k, deps=(), two=0):
            keep[k], send[k], *more = experts(pair[k], far[k], loaded, deps, two)
            came[k] = [swap(part, 1) for part in (send[k], *more)]

        def reduce_core(k):
            fold_keep[k], fold_send[k] = fold(keep[k], *came[k])
            y_came[k] = swap(fold_send[k], 2)

        def reduce_y(k, deps=(), cost=None):
            z_send[k] = add(fold_keep[k], y_came[k], deps, cost)
            return swap(z_send[k], 4 * k)

        gather(2, [block[1], block[3], *loaded])
        compute(2)
        gather(3, [send[2]])
        gather(1)
        compute(3, [send[2], pair[1]])
        gather(0, [send[3]])
        reduce_core(2)
        compute(1, [send[3], fold_send[2], pair[0]], two=1)
        reduce_core(3)
        z_2 = reduce_y(2)
        compute(0, [send[1], fold_send[3], z_send[2]], two=1)
        reduce_core(1)
        z_3 = reduce_y(3, [z_2], modelled(K_COST))
        z_1 = reduce_y(1)
        reduce_core(0)
        return fold_keep[0], y_came[0], z_1, z_2, z_3

    packet = call(
        pack_kernel,
        [space(rows, jnp.bfloat16)],
        [],
        hbm=[routes.T, latent_in],
        scratch=[pltpu.VMEM(routes.shape[::-1], routes.dtype), pltpu.SemaphoreType.DMA((2,))],
    )[0]

    def finish(parts):
        return pl.pallas_call(
            finish_kernel,
            out_shape=jax.ShapeDtypeStruct((rows, lat), jnp.bfloat16),
            in_specs=[VMEM] * len(parts),
            out_specs=VMEM,
            name="finish",
        )(*[in_vmem(p) for p in parts])

    if n_dev == GROUP:
        return finish(group_pass(packet))

    def next_group(x):
        return lax.ppermute(x, "exp", [(i, (i + GROUP) % n_dev) for i in range(n_dev)])

    def step(carry, _):
        mine, total = carry
        total = call(total_kernel, [space(rows, jnp.float32)], [total, *group_pass(mine)])[0]
        return (next_group(mine), next_group(total)), None

    start = (packet, jnp.zeros((rows, wide), jnp.float32))
    (_, total), _ = lax.scan(step, start, None, length=n_dev // GROUP)
    return finish([total])


def solution(mesh):
    placed = (
        P(("grp", "exp"), None),
        P(("grp", "exp"), None),
        P(None, "exp"),
        P("exp", None, None),
        P("exp", None, None),
    )
    return jax.shard_map(
        on_device, mesh=mesh, in_specs=placed, out_specs=P(("grp", "exp"), None), check_vma=False
    )
```

```python
import functools

import jax
import jax.numpy as jnp
from jax import lax
from jax.experimental import pallas as pl
from jax.experimental.pallas import tpu as pltpu
from jax.sharding import PartitionSpec as P

GROUP = 16
TAIL = 128
SCALE = 2.0**40
STEP = 256
PIECE = 256


def pack_kernel(ids_hbm, row_hbm, out_ref, ids_ref, sems):
    rows, lat = row_hbm.shape
    top = ids_hbm.shape[0]
    get_ids = pltpu.make_async_copy(ids_hbm, ids_ref, sems.at[0])
    get_rows = pltpu.make_async_copy(row_hbm, out_ref.at[:, pl.ds(0, lat)], sems.at[1])
    get_ids.start()
    get_rows.start()
    get_ids.wait()
    ids = ids_ref[...].astype(jnp.float32)
    ids = jnp.concatenate([ids, jnp.full((top, TAIL - rows), -1.0, jnp.float32)], axis=1)
    ids = jnp.concatenate([ids, jnp.full((TAIL - top, TAIL), -1.0, jnp.float32)], axis=0)
    out_ref[:, lat:] = ids.T[:rows].astype(jnp.bfloat16)
    get_rows.wait()


def load_kernel(router_hbm, up_hbm, down_hbm, dep_ref, columns_ref, up_ref, down_ref, router_ref, sems):
    get_router = pltpu.make_async_copy(router_hbm, router_ref, sems.at[0])
    get_router.start()
    copies = []
    for src, dst in ((up_hbm, up_ref), (down_hbm, down_ref)):
        for e in range(src.shape[0]):
            for r in range(0, src.shape[1], PIECE):
                at = (e, pl.ds(r, PIECE))
                copies.append(pltpu.make_async_copy(src.at[at], dst.at[at], sems.at[1 + len(copies)]))
    for copy in copies:
        copy.start()
    columns_ref[...] = jnp.zeros_like(columns_ref)
    get_router.wait()
    columns_ref[: router_ref.shape[0], :] = router_ref[...]
    for copy in copies:
        copy.wait()


def expert_kernel(first_ref, a_ref, b_ref, c_ref, d_ref, columns_ref, up_ref, down_ref, *refs):
    inner_ref, result_ref = refs[-2:]
    keep_ref, send_refs = refs[-5], refs[-4:-2]
    blocks = (a_ref, b_ref, c_ref, d_ref)
    rows, wide = a_ref.shape
    half, lat = 2 * rows, wide - TAIL
    local, eff, _ = down_ref.shape
    slots = result_ref.shape[0] // local
    x = jnp.concatenate([ref[:, :lat] for ref in blocks], axis=0)
    tail = jnp.concatenate([ref[:, lat:] for ref in blocks], axis=0).astype(jnp.float32)

    def put(lanes, value):
        keep_ref[:, lanes] = value[:half]
        for i, ref in enumerate(send_refs):
            ref[:, lanes] = value[half + i * rows : half + (i + 1) * rows].astype(jnp.bfloat16)

    def logits_of(values):
        return lax.dot_general(
            values, columns_ref[...], (((1,), (1,)), ((), ())), preferred_element_type=jnp.float32
        )

    logits = logits_of(x)
    lane = lax.broadcasted_iota(jnp.int32, (2 * half, TAIL), 1)
    masks, sums = [], jnp.zeros((2 * half, 1), jnp.float32)
    marks = jnp.zeros((2 * half, TAIL), jnp.float32)
    for e in range(local):
        label = (first_ref[0] + e).astype(jnp.float32)
        mask = jnp.max(jnp.where(tail == label, 1.0, 0.0), axis=1, keepdims=True)
        sums = sums + jax.nn.sigmoid(logits[:, e : e + 1]) * (mask * SCALE)
        marks = jnp.where(lane == e, mask, marks)
        masks.append(mask)
    row = lax.broadcasted_iota(jnp.int32, (2 * half, 2 * half), 0)
    col = lax.broadcasted_iota(jnp.int32, (2 * half, 2 * half), 1)
    before = jnp.where(col < row, 1.0, 0.0).astype(jnp.bfloat16)
    place = jnp.dot(before, marks.astype(jnp.bfloat16), preferred_element_type=jnp.float32)
    slot = lax.broadcasted_iota(jnp.int32, (2 * half, slots), 1).astype(jnp.float32)
    spread = jnp.concatenate(
        [jnp.where((slot == place[:, e : e + 1]) & (masks[e] > 0.0), 1.0, 0.0) for e in range(local)], axis=1
    ).astype(jnp.bfloat16)
    packed = lax.dot_general(
        spread, x, (((0,), (0,)), ((), ())), preferred_element_type=jnp.float32
    ).astype(jnp.bfloat16)
    scores = jax.nn.sigmoid(logits_of(packed)) * SCALE
    for e in range(local):
        mine = slice(e * slots, (e + 1) * slots)
        chosen = packed[mine]
        score = scores[mine, e : e + 1]
        for c in range(0, eff, STEP):
            gate = jnp.dot(chosen, up_ref[e, :, c : c + STEP], preferred_element_type=jnp.float32)
            up = jnp.dot(chosen, up_ref[e, :, eff + c : eff + c + STEP], preferred_element_type=jnp.float32)
            inner_ref[mine, c : c + STEP] = (gate / (1.0 + jnp.exp(-gate)) * up * score).astype(jnp.bfloat16)
    for e in range(local):
        mine = slice(e * slots, (e + 1) * slots)
        result_ref[mine, :] = jnp.dot(
            inner_ref[mine, :], down_ref[e], preferred_element_type=jnp.float32
        ).astype(jnp.bfloat16)
    for c in range(0, lat, STEP):
        part = jnp.dot(spread, result_ref[:, c : c + STEP], preferred_element_type=jnp.float32)
        put(slice(c, c + STEP), part)
    put(slice(lat, wide), jnp.where(lane == 0, sums, 0.0))


def tie_kernel(*refs):
    pass


def fold_kernel(mine_ref, came_a_ref, came_b_ref, *refs):
    keep_ref, send_ref = refs[-2:]
    rows = keep_ref.shape[0]
    keep_ref[...] = mine_ref[:rows] + came_a_ref[...].astype(jnp.float32)
    send_ref[...] = (mine_ref[rows:] + came_b_ref[...].astype(jnp.float32)).astype(jnp.bfloat16)


def add_kernel(mine_ref, came_ref, *refs):
    out_ref = refs[-1]
    out_ref[...] = (mine_ref[...] + came_ref[...].astype(jnp.float32)).astype(jnp.bfloat16)


def total_kernel(*refs):
    total_ref = refs[-1]
    total = refs[0][...]
    for ref in refs[1:-1]:
        total = total + ref[...].astype(jnp.float32)
    total_ref[...] = total


def finish_kernel(*refs):
    out_ref = refs[-1]
    lat = out_ref.shape[1]
    total = refs[0][...]
    for ref in refs[1:-1]:
        total = total + ref[...].astype(jnp.float32)
    out_ref[...] = (total[:, :lat] / total[:, lat : lat + 1]).astype(jnp.bfloat16)


def in_vmem(x):
    return pltpu.with_memory_space_constraint(x, pltpu.VMEM)


def in_hbm(x):
    return pltpu.with_memory_space_constraint(x, pltpu.HBM)


VMEM = pl.BlockSpec(memory_space=pltpu.VMEM)
ANY = pl.BlockSpec(memory_space=pl.ANY)


def call(kernel, outs, args, deps=(), smem=(), hbm=(), scratch=(), aliases=None):
    specs = [pl.BlockSpec(memory_space=pltpu.SMEM)] * len(smem) + [VMEM] * len(args)
    specs += [ANY] * (len(hbm) + len(deps))
    operands = list(smem) + [in_vmem(a) for a in args] + [in_hbm(h) for h in hbm] + [in_vmem(d) for d in deps]
    return pl.pallas_call(
        kernel,
        out_shape=outs,
        in_specs=specs,
        out_specs=[VMEM] * len(outs),
        scratch_shapes=list(scratch),
        compiler_params=pltpu.CompilerParams(vmem_limit_bytes=16 * 1024 * 1024),
        cost_estimate=pl.CostEstimate(flops=0, bytes_accessed=10_000, transcendentals=0),
        input_output_aliases=aliases or {},
        name=getattr(kernel, "func", kernel).__name__.removesuffix("_kernel"),
    )(*operands)


def on_device(latent_in, routes, router, gate_up, expert_down):
    n_dev = lax.axis_size("exp")
    local = gate_up.shape[0]
    eff = expert_down.shape[1]
    rows, lat = latent_in.shape
    wide = lat + TAIL
    first = (lax.axis_index("exp") * local).astype(jnp.int32).reshape(1)

    def swap(x, bits):
        return lax.ppermute(x, "exp", [(i, i ^ bits) for i in range(n_dev)])

    def space(height, dtype):
        return pltpu.VMEM((height, wide), dtype)

    def weights(dep):
        return call(
            load_kernel,
            [
                pltpu.VMEM((16, lat), jnp.bfloat16),
                pltpu.VMEM(gate_up.shape, gate_up.dtype),
                pltpu.VMEM(expert_down.shape, expert_down.dtype),
            ],
            [],
            deps=[dep],
            hbm=[router.T, gate_up, expert_down],
            scratch=[
                pltpu.VMEM((local, lat), jnp.bfloat16),
                pltpu.SemaphoreType.DMA((1 + local * (lat + eff) // PIECE,)),
            ],
        )

    bound = 2 * ((rows * routes.shape[1] + local * n_dev - 1) // (local * n_dev))
    slots = 4 * bound

    def experts(blocks, loaded, deps=()):
        return call(
            expert_kernel,
            [space(2 * rows, jnp.float32), space(rows, jnp.bfloat16), space(rows, jnp.bfloat16)],
            [*blocks, *loaded],
            deps,
            smem=[first],
            scratch=[
                pltpu.VMEM((local * slots, eff), jnp.bfloat16),
                pltpu.VMEM((local * slots, lat), jnp.bfloat16),
            ],
        )

    def tie(x, deps):
        return call(tie_kernel, [space(x.shape[0], x.dtype)], [x], deps, aliases={0: 0})[0]

    def fold(mine, came, deps=()):
        return call(
            fold_kernel, [space(rows, jnp.float32), space(rows, jnp.bfloat16)], [mine, *came], deps
        )

    def add(mine, came, deps=()):
        return call(add_kernel, [space(rows, jnp.bfloat16)], [mine, came], deps)[0]

    def group_pass(mine):
        loaded = weights(mine)
        z_2, z_1, y_0 = swap(mine, 8), swap(mine, 4), swap(mine, 2)
        block = {0: mine, 2: tie(z_2, [y_0, *loaded]), 1: z_1}
        block[3] = swap(block[2], 4)
        other = {0: y_0}
        keep, send, came, fold_keep, fold_send, y_came, z_send = {}, {}, {}, {}, {}, {}, {}

        def gather(k, deps):
            other[k] = tie(swap(block[k], 2), deps)

        def compute(k, deps=()):
            blocks = [block[k], other[k]]
            blocks += [swap(one, 1) for one in blocks]
            keep[k], *send[k] = experts(blocks, loaded, deps)
            came[k] = [swap(part, 1) for part in send[k]]

        def reduce_core(k, deps=()):
            fold_keep[k], fold_send[k] = fold(keep[k], came[k], deps)
            y_came[k] = swap(fold_send[k], 2)

        def reduce_y(k, deps=()):
            z_send[k] = add(fold_keep[k], y_came[k], deps)
            return swap(z_send[k], 4 * k)

        gather(2, [block[1], block[3], *loaded])
        compute(2)
        gather(3, send[2])
        gather(1, send[2])
        reduce_core(2)
        compute(3, [other[1], fold_send[2]])
        z_2 = reduce_y(2)
        reduce_core(3, [z_send[2]])
        compute(1, [fold_send[3]])
        z_3 = reduce_y(3)
        reduce_core(1, [z_send[3]])
        compute(0, [fold_send[1]])
        z_1 = reduce_y(1, [z_2])
        reduce_core(0, [z_send[1]])
        return fold_keep[0], y_came[0], z_1, z_2, z_3

    packet = call(
        pack_kernel,
        [space(rows, jnp.bfloat16)],
        [],
        hbm=[routes.T, latent_in],
        scratch=[pltpu.VMEM(routes.shape[::-1], routes.dtype), pltpu.SemaphoreType.DMA((2,))],
    )[0]

    def finish(parts):
        return pl.pallas_call(
            finish_kernel,
            out_shape=jax.ShapeDtypeStruct((rows, lat), jnp.bfloat16),
            in_specs=[VMEM] * len(parts),
            out_specs=VMEM,
            name="finish",
        )(*[in_vmem(p) for p in parts])

    if n_dev == GROUP:
        return finish(group_pass(packet))

    def next_group(x):
        return lax.ppermute(x, "exp", [(i, (i + GROUP) % n_dev) for i in range(n_dev)])

    def step(carry, _):
        mine, total = carry
        total = call(total_kernel, [space(rows, jnp.float32)], [total, *group_pass(mine)])[0]
        return (next_group(mine), next_group(total)), None

    start = (packet, jnp.zeros((rows, wide), jnp.float32))
    (_, total), _ = lax.scan(step, start, None, length=n_dev // GROUP)
    return finish([total])


def solution(mesh):
    placed = (
        P(("grp", "exp"), None),
        P(("grp", "exp"), None),
        P(None, "exp"),
        P("exp", None, None),
        P("exp", None, None),
    )
    return jax.shard_map(
        on_device, mesh=mesh, in_specs=placed, out_specs=P(("grp", "exp"), None), check_vma=False
    )
```

```python
import functools

import jax
import jax.numpy as jnp
from jax import lax
from jax.experimental import pallas as pl
from jax.experimental.pallas import tpu as pltpu
from jax.sharding import PartitionSpec as P

GROUP = 16
SCOPED = 2 * 1024 * 1024
TAIL = 128
SCALE = 2.0**40
STEP = 256
PIECE = 256


def pack_kernel(ids_hbm, row_hbm, out_ref, ids_ref, sems):
    rows, lat = row_hbm.shape
    top = ids_hbm.shape[0]
    get_ids = pltpu.make_async_copy(ids_hbm, ids_ref, sems.at[0])
    get_rows = pltpu.make_async_copy(row_hbm, out_ref.at[:, pl.ds(0, lat)], sems.at[1])
    get_ids.start()
    get_rows.start()
    get_ids.wait()
    ids = ids_ref[...].astype(jnp.float32)
    ids = jnp.concatenate([ids, jnp.full((top, TAIL - rows), -1.0, jnp.float32)], axis=1)
    ids = jnp.concatenate([ids, jnp.full((TAIL - top, TAIL), -1.0, jnp.float32)], axis=0)
    out_ref[:, lat:] = ids.T[:rows].astype(jnp.bfloat16)
    get_rows.wait()


def load_kernel(router_hbm, up_hbm, down_hbm, dep_ref, columns_ref, up_ref, down_ref, router_ref, sems):
    get_router = pltpu.make_async_copy(router_hbm, router_ref, sems.at[0])
    get_router.start()
    copies = []
    for src, dst in ((up_hbm, up_ref), (down_hbm, down_ref)):
        for e in range(src.shape[0]):
            for r in range(0, src.shape[1], PIECE):
                at = (e, pl.ds(r, PIECE))
                copies.append(pltpu.make_async_copy(src.at[at], dst.at[at], sems.at[1 + len(copies)]))
    for copy in copies:
        copy.start()
    columns_ref[...] = jnp.zeros_like(columns_ref)
    get_router.wait()
    columns_ref[: router_ref.shape[0], :] = router_ref[...]
    for copy in copies:
        copy.wait()


def expert_kernel(first_ref, a_ref, b_ref, c_ref, d_ref, columns_ref, up_ref, down_ref, *refs):
    inner_ref, result_ref = refs[-2:]
    keep_ref, send_refs = refs[-5], refs[-4:-2]
    blocks = (a_ref, b_ref, c_ref, d_ref)
    rows, wide = a_ref.shape
    half, lat = 2 * rows, wide - TAIL
    local, eff, _ = down_ref.shape
    slots = result_ref.shape[0] // local
    x = jnp.concatenate([ref[:, :lat] for ref in blocks], axis=0)
    tail = jnp.concatenate([ref[:, lat:] for ref in blocks], axis=0).astype(jnp.float32)

    def put(lanes, value):
        keep_ref[:, lanes] = value[:half]
        for i, ref in enumerate(send_refs):
            ref[:, lanes] = value[half + i * rows : half + (i + 1) * rows].astype(jnp.bfloat16)

    def logits_of(values):
        return lax.dot_general(
            values, columns_ref[...], (((1,), (1,)), ((), ())), preferred_element_type=jnp.float32
        )

    logits = logits_of(x)
    lane = lax.broadcasted_iota(jnp.int32, (2 * half, TAIL), 1)
    masks, sums = [], jnp.zeros((2 * half, 1), jnp.float32)
    marks = jnp.zeros((2 * half, TAIL), jnp.float32)
    for e in range(local):
        label = (first_ref[0] + e).astype(jnp.float32)
        mask = jnp.max(jnp.where(tail == label, 1.0, 0.0), axis=1, keepdims=True)
        sums = sums + jax.nn.sigmoid(logits[:, e : e + 1]) * (mask * SCALE)
        marks = jnp.where(lane == e, mask, marks)
        masks.append(mask)
    row = lax.broadcasted_iota(jnp.int32, (2 * half, 2 * half), 0)
    col = lax.broadcasted_iota(jnp.int32, (2 * half, 2 * half), 1)
    before = jnp.where(col < row, 1.0, 0.0).astype(jnp.bfloat16)
    place = jnp.dot(before, marks.astype(jnp.bfloat16), preferred_element_type=jnp.float32)
    slot = lax.broadcasted_iota(jnp.int32, (2 * half, slots), 1).astype(jnp.float32)
    spread = jnp.concatenate(
        [jnp.where((slot == place[:, e : e + 1]) & (masks[e] > 0.0), 1.0, 0.0) for e in range(local)], axis=1
    ).astype(jnp.bfloat16)
    packed = lax.dot_general(
        spread, x, (((0,), (0,)), ((), ())), preferred_element_type=jnp.float32
    ).astype(jnp.bfloat16)
    scores = jax.nn.sigmoid(logits_of(packed)) * SCALE
    for e in range(local):
        mine = slice(e * slots, (e + 1) * slots)
        chosen = packed[mine]
        score = scores[mine, e : e + 1]
        for c in range(0, eff, STEP):
            gate = jnp.dot(chosen, up_ref[e, :, c : c + STEP], preferred_element_type=jnp.float32)
            up = jnp.dot(chosen, up_ref[e, :, eff + c : eff + c + STEP], preferred_element_type=jnp.float32)
            inner_ref[mine, c : c + STEP] = (gate / (1.0 + jnp.exp(-gate)) * up * score).astype(jnp.bfloat16)
    for e in range(local):
        mine = slice(e * slots, (e + 1) * slots)
        result_ref[mine, :] = jnp.dot(
            inner_ref[mine, :], down_ref[e], preferred_element_type=jnp.float32
        ).astype(jnp.bfloat16)
    for c in range(0, lat, STEP):
        part = jnp.dot(spread, result_ref[:, c : c + STEP], preferred_element_type=jnp.float32)
        put(slice(c, c + STEP), part)
    put(slice(lat, wide), jnp.where(lane == 0, sums, 0.0))


def tie_kernel(*refs):
    pass


def fold_kernel(mine_ref, came_a_ref, came_b_ref, *refs):
    keep_ref, send_ref = refs[-2:]
    rows = keep_ref.shape[0]
    keep_ref[...] = mine_ref[:rows] + came_a_ref[...].astype(jnp.float32)
    send_ref[...] = (mine_ref[rows:] + came_b_ref[...].astype(jnp.float32)).astype(jnp.bfloat16)


def add_kernel(mine_ref, came_ref, *refs):
    out_ref = refs[-1]
    out_ref[...] = (mine_ref[...] + came_ref[...].astype(jnp.float32)).astype(jnp.bfloat16)


def total_kernel(*refs):
    total_ref = refs[-1]
    total = refs[0][...]
    for ref in refs[1:-1]:
        total = total + ref[...].astype(jnp.float32)
    total_ref[...] = total


def finish_kernel(*refs):
    out_ref = refs[-1]
    lat = out_ref.shape[1]
    total = refs[0][...]
    for ref in refs[1:-1]:
        total = total + ref[...].astype(jnp.float32)
    out_ref[...] = (total[:, :lat] / total[:, lat : lat + 1]).astype(jnp.bfloat16)


def in_vmem(x):
    return pltpu.with_memory_space_constraint(x, pltpu.VMEM)


def in_hbm(x):
    return pltpu.with_memory_space_constraint(x, pltpu.HBM)


VMEM = pl.BlockSpec(memory_space=pltpu.VMEM)
ANY = pl.BlockSpec(memory_space=pl.ANY)


def call(kernel, outs, args, deps=(), smem=(), hbm=(), scratch=(), aliases=None):
    specs = [pl.BlockSpec(memory_space=pltpu.SMEM)] * len(smem) + [VMEM] * len(args)
    specs += [ANY] * (len(hbm) + len(deps))
    operands = list(smem) + [in_vmem(a) for a in args] + [in_hbm(h) for h in hbm] + [in_vmem(d) for d in deps]
    return pl.pallas_call(
        kernel,
        out_shape=outs,
        in_specs=specs,
        out_specs=[VMEM] * len(outs),
        scratch_shapes=list(scratch),
        compiler_params=pltpu.CompilerParams(vmem_limit_bytes=SCOPED),
        cost_estimate=pl.CostEstimate(flops=0, bytes_accessed=10_000, transcendentals=0),
        input_output_aliases=aliases or {},
        name=getattr(kernel, "func", kernel).__name__.removesuffix("_kernel"),
    )(*operands)


def on_device(latent_in, routes, router, gate_up, expert_down):
    n_dev = lax.axis_size("exp")
    local = gate_up.shape[0]
    eff = expert_down.shape[1]
    rows, lat = latent_in.shape
    wide = lat + TAIL
    first = (lax.axis_index("exp") * local).astype(jnp.int32).reshape(1)

    def swap(x, bits):
        return lax.ppermute(x, "exp", [(i, i ^ bits) for i in range(n_dev)])

    def space(height, dtype):
        return pltpu.VMEM((height, wide), dtype)

    def weights(dep):
        return call(
            load_kernel,
            [
                pltpu.VMEM((16, lat), jnp.bfloat16),
                pltpu.VMEM(gate_up.shape, gate_up.dtype),
                pltpu.VMEM(expert_down.shape, expert_down.dtype),
            ],
            [],
            deps=[dep],
            hbm=[router.T, gate_up, expert_down],
            scratch=[
                pltpu.VMEM((local, lat), jnp.bfloat16),
                pltpu.SemaphoreType.DMA((1 + local * (lat + eff) // PIECE,)),
            ],
        )

    bound = 2 * ((rows * routes.shape[1] + local * n_dev - 1) // (local * n_dev))
    slots = 4 * bound

    def experts(blocks, loaded, deps=()):
        return call(
            expert_kernel,
            [space(2 * rows, jnp.float32), space(rows, jnp.bfloat16), space(rows, jnp.bfloat16)],
            [*blocks, *loaded],
            deps,
            smem=[first],
            scratch=[
                pltpu.VMEM((local * slots, eff), jnp.bfloat16),
                pltpu.VMEM((local * slots, lat), jnp.bfloat16),
            ],
        )

    def tie(x, deps):
        return call(tie_kernel, [space(x.shape[0], x.dtype)], [x], deps, aliases={0: 0})[0]

    def fold(mine, came, deps=()):
        return call(
            fold_kernel, [space(rows, jnp.float32), space(rows, jnp.bfloat16)], [mine, *came], deps
        )

    def add(mine, came, deps=()):
        return call(add_kernel, [space(rows, jnp.bfloat16)], [mine, came], deps)[0]

    def group_pass(mine):
        loaded = weights(mine)
        z_2, z_1, y_0 = swap(mine, 8), swap(mine, 4), swap(mine, 2)
        block = {0: mine, 2: tie(z_2, [y_0, *loaded]), 1: z_1}
        block[3] = swap(block[2], 4)
        other = {0: y_0}
        keep, send, came, fold_keep, fold_send, y_came, z_send = {}, {}, {}, {}, {}, {}, {}

        def gather(k, deps):
            other[k] = tie(swap(block[k], 2), deps)

        def compute(k, deps=()):
            blocks = [block[k], other[k]]
            blocks += [swap(one, 1) for one in blocks]
            keep[k], *send[k] = experts(blocks, loaded, deps)
            came[k] = [swap(part, 1) for part in send[k]]

        def reduce_core(k, deps=()):
            fold_keep[k], fold_send[k] = fold(keep[k], came[k], deps)
            y_came[k] = swap(fold_send[k], 2)

        def reduce_y(k, deps=()):
            z_send[k] = add(fold_keep[k], y_came[k], deps)
            return swap(z_send[k], 4 * k)

        gather(2, [block[1], block[3], *loaded])
        compute(2)
        gather(3, send[2])
        gather(1, send[2])
        reduce_core(2)
        compute(3, [other[1], fold_send[2]])
        z_2 = reduce_y(2)
        reduce_core(3, [z_send[2]])
        compute(1, [fold_send[3]])
        z_3 = reduce_y(3)
        reduce_core(1, [z_send[3]])
        compute(0, [fold_send[1]])
        z_1 = reduce_y(1, [z_2])
        reduce_core(0, [z_send[1]])
        return fold_keep[0], y_came[0], z_1, z_2, z_3

    packet = call(
        pack_kernel,
        [space(rows, jnp.bfloat16)],
        [],
        hbm=[routes.T, latent_in],
        scratch=[pltpu.VMEM(routes.shape[::-1], routes.dtype), pltpu.SemaphoreType.DMA((2,))],
    )[0]

    def finish(parts):
        return pl.pallas_call(
            finish_kernel,
            out_shape=jax.ShapeDtypeStruct((rows, lat), jnp.bfloat16),
            in_specs=[VMEM] * len(parts),
            out_specs=VMEM,
            compiler_params=pltpu.CompilerParams(vmem_limit_bytes=SCOPED),
            name="finish",
        )(*[in_vmem(p) for p in parts])

    if n_dev == GROUP:
        return finish(group_pass(packet))

    def next_group(x):
        return lax.ppermute(x, "exp", [(i, (i + GROUP) % n_dev) for i in range(n_dev)])

    def step(carry, _):
        mine, total = carry
        total = call(total_kernel, [space(rows, jnp.float32)], [total, *group_pass(mine)])[0]
        return (next_group(mine), next_group(total)), None

    start = (packet, jnp.zeros((rows, wide), jnp.float32))
    (_, total), _ = lax.scan(step, start, None, length=n_dev // GROUP)
    return finish([total])


def solution(mesh):
    placed = (
        P(("grp", "exp"), None),
        P(("grp", "exp"), None),
        P(None, "exp"),
        P("exp", None, None),
        P("exp", None, None),
    )
    return jax.shard_map(
        on_device, mesh=mesh, in_specs=placed, out_specs=P(("grp", "exp"), None), check_vma=False
    )
```

```python
import functools

import jax
import jax.numpy as jnp
from jax import lax
from jax.experimental import pallas as pl
from jax.experimental.pallas import tpu as pltpu
from jax.sharding import PartitionSpec as P

GROUP = 16
SCOPED = 2 * 1024 * 1024
TAIL = 128
SCALE = 2.0**40
STEP = 256
PIECE = 256


def pack_kernel(ids_hbm, row_hbm, out_ref, ids_ref, sems):
    rows, lat = row_hbm.shape
    top = ids_hbm.shape[0]
    get_ids = pltpu.make_async_copy(ids_hbm, ids_ref, sems.at[0])
    get_rows = pltpu.make_async_copy(row_hbm, out_ref.at[:, pl.ds(0, lat)], sems.at[1])
    get_ids.start()
    get_rows.start()
    get_ids.wait()
    ids = ids_ref[...].astype(jnp.float32)
    ids = jnp.concatenate([ids, jnp.full((top, TAIL - rows), -1.0, jnp.float32)], axis=1)
    ids = jnp.concatenate([ids, jnp.full((TAIL - top, TAIL), -1.0, jnp.float32)], axis=0)
    out_ref[:, lat:] = ids.T[:rows].astype(jnp.bfloat16)
    get_rows.wait()


def load_kernel(router_hbm, up_hbm, down_hbm, columns_ref, up_ref, down_ref, router_ref, sems):
    get_router = pltpu.make_async_copy(router_hbm, router_ref, sems.at[0])
    get_router.start()
    copies = []
    for src, dst in ((up_hbm, up_ref), (down_hbm, down_ref)):
        for e in range(src.shape[0]):
            for r in range(0, src.shape[1], PIECE):
                at = (e, pl.ds(r, PIECE))
                copies.append(pltpu.make_async_copy(src.at[at], dst.at[at], sems.at[1 + len(copies)]))
    for copy in copies:
        copy.start()
    columns_ref[...] = jnp.zeros_like(columns_ref)
    get_router.wait()
    columns_ref[: router_ref.shape[0], :] = router_ref[...]
    for copy in copies:
        copy.wait()


def expert_kernel(
    first_ref, a_ref, b_ref, c_ref, d_ref, columns_ref, up_ref, down_ref, keep_ref, *refs
):
    *send_refs, inner_ref, result_ref = refs
    blocks = (a_ref, b_ref, c_ref, d_ref)
    rows, wide = a_ref.shape
    half, lat = 2 * rows, wide - TAIL
    local, eff, _ = down_ref.shape
    slots = result_ref.shape[0] // local
    x = jnp.concatenate([ref[:, :lat] for ref in blocks], axis=0)
    tail = jnp.concatenate([ref[:, lat:] for ref in blocks], axis=0).astype(jnp.float32)

    def put(lanes, value):
        keep_ref[:, lanes] = value[:half]
        for i, ref in enumerate(send_refs):
            ref[:, lanes] = value[half + i * rows : half + (i + 1) * rows].astype(jnp.bfloat16)

    def logits_of(values):
        return lax.dot_general(
            values, columns_ref[...], (((1,), (1,)), ((), ())), preferred_element_type=jnp.float32
        )

    logits = logits_of(x)
    lane = lax.broadcasted_iota(jnp.int32, (2 * half, TAIL), 1)
    masks, sums = [], jnp.zeros((2 * half, 1), jnp.float32)
    marks = jnp.zeros((2 * half, TAIL), jnp.float32)
    for e in range(local):
        label = (first_ref[0] + e).astype(jnp.float32)
        mask = jnp.max(jnp.where(tail == label, 1.0, 0.0), axis=1, keepdims=True)
        sums = sums + jax.nn.sigmoid(logits[:, e : e + 1]) * (mask * SCALE)
        marks = jnp.where(lane == e, mask, marks)
        masks.append(mask)
    row = lax.broadcasted_iota(jnp.int32, (2 * half, 2 * half), 0)
    col = lax.broadcasted_iota(jnp.int32, (2 * half, 2 * half), 1)
    before = jnp.where(col < row, 1.0, 0.0).astype(jnp.bfloat16)
    place = jnp.dot(before, marks.astype(jnp.bfloat16), preferred_element_type=jnp.float32)
    slot = lax.broadcasted_iota(jnp.int32, (2 * half, slots), 1).astype(jnp.float32)
    spread = jnp.concatenate(
        [jnp.where((slot == place[:, e : e + 1]) & (masks[e] > 0.0), 1.0, 0.0) for e in range(local)], axis=1
    ).astype(jnp.bfloat16)
    packed = lax.dot_general(
        spread, x, (((0,), (0,)), ((), ())), preferred_element_type=jnp.float32
    ).astype(jnp.bfloat16)
    scores = jax.nn.sigmoid(logits_of(packed)) * SCALE
    for e in range(local):
        mine = slice(e * slots, (e + 1) * slots)
        chosen = packed[mine]
        score = scores[mine, e : e + 1]
        for c in range(0, eff, STEP):
            gate = jnp.dot(chosen, up_ref[e, :, c : c + STEP], preferred_element_type=jnp.float32)
            up = jnp.dot(chosen, up_ref[e, :, eff + c : eff + c + STEP], preferred_element_type=jnp.float32)
            inner_ref[mine, c : c + STEP] = (gate / (1.0 + jnp.exp(-gate)) * up * score).astype(jnp.bfloat16)
    for e in range(local):
        mine = slice(e * slots, (e + 1) * slots)
        result_ref[mine, :] = jnp.dot(
            inner_ref[mine, :], down_ref[e], preferred_element_type=jnp.float32
        ).astype(jnp.bfloat16)
    for c in range(0, lat, STEP):
        part = jnp.dot(spread, result_ref[:, c : c + STEP], preferred_element_type=jnp.float32)
        put(slice(c, c + STEP), part)
    put(slice(lat, wide), jnp.where(lane == 0, sums, 0.0))


def tie_kernel():
    pass


def fold_kernel(mine_ref, came_a_ref, came_b_ref, keep_ref, send_ref):
    rows = keep_ref.shape[0]
    keep_ref[...] = mine_ref[:rows] + came_a_ref[...].astype(jnp.float32)
    send_ref[...] = (mine_ref[rows:] + came_b_ref[...].astype(jnp.float32)).astype(jnp.bfloat16)


def add_kernel(mine_ref, came_ref, out_ref):
    out_ref[...] = (mine_ref[...] + came_ref[...].astype(jnp.float32)).astype(jnp.bfloat16)


def total_kernel(*refs):
    total_ref = refs[-1]
    total = refs[0][...]
    for ref in refs[1:-1]:
        total = total + ref[...].astype(jnp.float32)
    total_ref[...] = total


def finish_kernel(*refs):
    out_ref = refs[-1]
    lat = out_ref.shape[1]
    total = refs[0][...]
    for ref in refs[1:-1]:
        total = total + ref[...].astype(jnp.float32)
    out_ref[...] = (total[:, :lat] / total[:, lat : lat + 1]).astype(jnp.bfloat16)


def in_vmem(x):
    return pltpu.with_memory_space_constraint(x, pltpu.VMEM)


def in_hbm(x):
    return pltpu.with_memory_space_constraint(x, pltpu.HBM)


VMEM = pl.BlockSpec(memory_space=pltpu.VMEM)
ANY = pl.BlockSpec(memory_space=pl.ANY)


def call(kernel, outs, args=(), deps=(), chain=(), smem=(), hbm=(), scratch=()):
    n_in = len(smem) + len(args) + len(hbm)
    n_skip = n_in + len(deps)
    n_outs = n_skip + len(chain)

    def body(*refs):
        kernel(*refs[:n_in], *refs[n_outs : n_outs + len(outs)], *refs[n_outs + len(outs) + len(chain) :])

    def body_with_chain(*refs):
        kernel(
            *refs[:n_in],
            *refs[n_skip:n_outs],
            *refs[n_outs : n_outs + len(outs)],
            *refs[n_outs + len(outs) + len(chain) :],
        )

    specs = [pl.BlockSpec(memory_space=pltpu.SMEM)] * len(smem) + [VMEM] * len(args)
    specs += [ANY] * (len(hbm) + len(deps)) + [VMEM] * len(chain)
    operands = list(smem) + [in_vmem(a) for a in args] + [in_hbm(h) for h in hbm]
    operands += [in_vmem(x) for x in (*deps, *chain)]
    return pl.pallas_call(
        body_with_chain if kernel is expert_kernel else body,
        out_shape=list(outs) + [pltpu.VMEM(x.shape, x.dtype) for x in chain],
        in_specs=specs,
        out_specs=[VMEM] * (len(outs) + len(chain)),
        scratch_shapes=list(scratch),
        compiler_params=pltpu.CompilerParams(vmem_limit_bytes=SCOPED),
        cost_estimate=pl.CostEstimate(flops=0, bytes_accessed=10_000, transcendentals=0),
        input_output_aliases={n_skip + i: len(outs) + i for i in range(len(chain))},
        name=kernel.__name__.removesuffix("_kernel"),
    )(*operands)


def on_device(latent_in, routes, router, gate_up, expert_down):
    n_dev = lax.axis_size("exp")
    local = gate_up.shape[0]
    eff = expert_down.shape[1]
    rows, lat = latent_in.shape
    wide = lat + TAIL
    first = (lax.axis_index("exp") * local).astype(jnp.int32).reshape(1)

    def swap(x, bits):
        return lax.ppermute(x, "exp", [(i, i ^ bits) for i in range(n_dev)])

    def space(height, dtype):
        return pltpu.VMEM((height, wide), dtype)

    def weights(dep):
        return call(
            load_kernel,
            [
                pltpu.VMEM((16, lat), jnp.bfloat16),
                pltpu.VMEM(gate_up.shape, gate_up.dtype),
                pltpu.VMEM(expert_down.shape, expert_down.dtype),
            ],
            deps=[dep],
            hbm=[router.T, gate_up, expert_down],
            scratch=[
                pltpu.VMEM((local, lat), jnp.bfloat16),
                pltpu.SemaphoreType.DMA((1 + local * (lat + eff) // PIECE,)),
            ],
        )

    bound = 2 * ((rows * routes.shape[1] + local * n_dev - 1) // (local * n_dev))
    slots = 4 * bound

    def group_pass(mine):
        held = weights(mine)

        def step(kernel, outs, args=(), deps=(), hand_on=(), **more):
            nonlocal held
            result = call(kernel, outs, args, deps, [*held, *hand_on], **more)
            held = result[len(outs) : len(outs) + len(held)]
            return result[: len(outs)] + result[len(outs) + len(held) :]

        def tie(x, deps=()):
            return step(tie_kernel, [], deps=deps, hand_on=[x])[0]

        other, keep, send, came, fold_keep, fold_send, y_came, z_send = {}, {}, {}, {}, {}, {}, {}, {}

        def gather(k, deps=()):
            other[k] = tie(swap(block[k], 2), deps)

        def compute(k):
            blocks = [block[k], other[k]]
            blocks += [swap(one, 1) for one in blocks]
            keep[k], *send[k] = step(
                expert_kernel,
                [space(2 * rows, jnp.float32), space(rows, jnp.bfloat16), space(rows, jnp.bfloat16)],
                blocks,
                smem=[first],
                scratch=[
                    pltpu.VMEM((local * slots, eff), jnp.bfloat16),
                    pltpu.VMEM((local * slots, lat), jnp.bfloat16),
                ],
            )
            came[k] = [swap(part, 1) for part in send[k]]

        def reduce_core(k):
            fold_keep[k], fold_send[k] = step(
                fold_kernel, [space(rows, jnp.float32), space(rows, jnp.bfloat16)], [keep[k], *came[k]]
            )
            y_came[k] = swap(fold_send[k], 2)

        def reduce_y(k, deps=()):
            z_send[k] = step(add_kernel, [space(rows, jnp.bfloat16)], [fold_keep[k], y_came[k]], deps)[0]
            return swap(z_send[k], 4 * k)

        z_2, z_1, y_0 = swap(mine, 8), swap(mine, 4), swap(mine, 2)
        block = {0: mine, 2: tie(z_2, [y_0]), 1: z_1}
        block[3] = swap(block[2], 4)
        other[0] = y_0
        gather(2, [block[1], block[3]])
        compute(2)
        gather(3)
        gather(1)
        reduce_core(2)
        compute(3)
        z_2 = reduce_y(2)
        reduce_core(3)
        compute(1)
        z_3 = reduce_y(3)
        reduce_core(1)
        compute(0)
        z_1 = reduce_y(1, [z_2])
        reduce_core(0)
        return fold_keep[0], y_came[0], z_1, z_2, z_3

    packet = call(
        pack_kernel,
        [space(rows, jnp.bfloat16)],
        hbm=[routes.T, latent_in],
        scratch=[pltpu.VMEM(routes.shape[::-1], routes.dtype), pltpu.SemaphoreType.DMA((2,))],
    )[0]

    def finish(parts):
        return pl.pallas_call(
            finish_kernel,
            out_shape=jax.ShapeDtypeStruct((rows, lat), jnp.bfloat16),
            in_specs=[VMEM] * len(parts),
            out_specs=VMEM,
            compiler_params=pltpu.CompilerParams(vmem_limit_bytes=SCOPED),
            name="finish",
        )(*[in_vmem(p) for p in parts])

    if n_dev == GROUP:
        return finish(group_pass(packet))

    def next_group(x):
        return lax.ppermute(x, "exp", [(i, (i + GROUP) % n_dev) for i in range(n_dev)])

    def step(carry, _):
        mine, total = carry
        total = call(total_kernel, [space(rows, jnp.float32)], [total, *group_pass(mine)])[0]
        return (next_group(mine), next_group(total)), None

    start = (packet, jnp.zeros((rows, wide), jnp.float32))
    (_, total), _ = lax.scan(step, start, None, length=n_dev // GROUP)
    return finish([total])


def solution(mesh):
    placed = (
        P(("grp", "exp"), None),
        P(("grp", "exp"), None),
        P(None, "exp"),
        P("exp", None, None),
        P("exp", None, None),
    )
    return jax.shard_map(
        on_device, mesh=mesh, in_specs=placed, out_specs=P(("grp", "exp"), None), check_vma=False
    )
```

```python
import functools

import jax
import jax.numpy as jnp
from jax import lax
from jax.experimental import pallas as pl
from jax.experimental.pallas import tpu as pltpu
from jax.sharding import PartitionSpec as P

GROUP = 16
SCOPED = 2 * 1024 * 1024
TAIL = 128
SCALE = 2.0**40
STEP = 256
PIECE = 256


def pack_kernel(ids_hbm, row_hbm, out_ref, ids_ref, sems):
    rows, lat = row_hbm.shape
    top = ids_hbm.shape[0]
    get_ids = pltpu.make_async_copy(ids_hbm, ids_ref, sems.at[0])
    get_rows = pltpu.make_async_copy(row_hbm, out_ref.at[:, pl.ds(0, lat)], sems.at[1])
    get_ids.start()
    get_rows.start()
    get_ids.wait()
    ids = ids_ref[...].astype(jnp.float32)
    ids = jnp.concatenate([ids, jnp.full((top, TAIL - rows), -1.0, jnp.float32)], axis=1)
    ids = jnp.concatenate([ids, jnp.full((TAIL - top, TAIL), -1.0, jnp.float32)], axis=0)
    out_ref[:, lat:] = ids.T[:rows].astype(jnp.bfloat16)
    get_rows.wait()


def load_kernel(router_hbm, up_hbm, down_hbm, columns_ref, up_ref, down_ref, router_ref, sems):
    get_router = pltpu.make_async_copy(router_hbm, router_ref, sems.at[0])
    get_router.start()
    copies = []
    for src, dst in ((up_hbm, up_ref), (down_hbm, down_ref)):
        for e in range(src.shape[0]):
            for r in range(0, src.shape[1], PIECE):
                at = (e, pl.ds(r, PIECE))
                copies.append(pltpu.make_async_copy(src.at[at], dst.at[at], sems.at[1 + len(copies)]))
    for copy in copies:
        copy.start()
    columns_ref[...] = jnp.zeros_like(columns_ref)
    get_router.wait()
    columns_ref[: router_ref.shape[0], :] = router_ref[...]
    for copy in copies:
        copy.wait()


def expert_kernel(
    a_ref, b_ref, c_ref, d_ref, columns_ref, up_ref, down_ref, keep_ref, *refs
):
    *send_refs, inner_ref, result_ref = refs
    blocks = (a_ref, b_ref, c_ref, d_ref)
    rows, wide = a_ref.shape
    half, lat = 2 * rows, wide - TAIL
    local, eff, _ = down_ref.shape
    slots = result_ref.shape[0] // local
    x = jnp.concatenate([ref[:, :lat] for ref in blocks], axis=0)
    tail = jnp.concatenate([ref[:, lat:] for ref in blocks], axis=0).astype(jnp.float32)

    def put(lanes, value):
        keep_ref[:, lanes] = value[:half]
        for i, ref in enumerate(send_refs):
            ref[:, lanes] = value[half + i * rows : half + (i + 1) * rows].astype(jnp.bfloat16)

    def logits_of(values):
        return lax.dot_general(
            values, columns_ref[...], (((1,), (1,)), ((), ())), preferred_element_type=jnp.float32
        )

    logits = logits_of(x)
    lane = lax.broadcasted_iota(jnp.int32, (2 * half, TAIL), 1)
    masks, sums = [], jnp.zeros((2 * half, 1), jnp.float32)
    marks = jnp.zeros((2 * half, TAIL), jnp.float32)
    for e in range(local):
        label = (lax.axis_index("exp") * local + e).astype(jnp.float32)
        mask = jnp.max(jnp.where(tail == label, 1.0, 0.0), axis=1, keepdims=True)
        sums = sums + jax.nn.sigmoid(logits[:, e : e + 1]) * (mask * SCALE)
        marks = jnp.where(lane == e, mask, marks)
        masks.append(mask)
    row = lax.broadcasted_iota(jnp.int32, (2 * half, 2 * half), 0)
    col = lax.broadcasted_iota(jnp.int32, (2 * half, 2 * half), 1)
    before = jnp.where(col < row, 1.0, 0.0).astype(jnp.bfloat16)
    place = jnp.dot(before, marks.astype(jnp.bfloat16), preferred_element_type=jnp.float32)
    slot = lax.broadcasted_iota(jnp.int32, (2 * half, slots), 1).astype(jnp.float32)
    spread = jnp.concatenate(
        [jnp.where((slot == place[:, e : e + 1]) & (masks[e] > 0.0), 1.0, 0.0) for e in range(local)], axis=1
    ).astype(jnp.bfloat16)
    packed = lax.dot_general(
        spread, x, (((0,), (0,)), ((), ())), preferred_element_type=jnp.float32
    ).astype(jnp.bfloat16)
    scores = jax.nn.sigmoid(logits_of(packed)) * SCALE
    for e in range(local):
        mine = slice(e * slots, (e + 1) * slots)
        chosen = packed[mine]
        score = scores[mine, e : e + 1]
        for c in range(0, eff, STEP):
            gate = jnp.dot(chosen, up_ref[e, :, c : c + STEP], preferred_element_type=jnp.float32)
            up = jnp.dot(chosen, up_ref[e, :, eff + c : eff + c + STEP], preferred_element_type=jnp.float32)
            inner_ref[mine, c : c + STEP] = (gate / (1.0 + jnp.exp(-gate)) * up * score).astype(jnp.bfloat16)
    for e in range(local):
        mine = slice(e * slots, (e + 1) * slots)
        result_ref[mine, :] = jnp.dot(
            inner_ref[mine, :], down_ref[e], preferred_element_type=jnp.float32
        ).astype(jnp.bfloat16)
    for c in range(0, lat, STEP):
        part = jnp.dot(spread, result_ref[:, c : c + STEP], preferred_element_type=jnp.float32)
        put(slice(c, c + STEP), part)
    put(slice(lat, wide), jnp.where(lane == 0, sums, 0.0))


def tie_kernel():
    pass


def fold_kernel(mine_ref, came_a_ref, came_b_ref, keep_ref, send_ref):
    rows = keep_ref.shape[0]
    keep_ref[...] = mine_ref[:rows] + came_a_ref[...].astype(jnp.float32)
    send_ref[...] = (mine_ref[rows:] + came_b_ref[...].astype(jnp.float32)).astype(jnp.bfloat16)


def add_kernel(mine_ref, came_ref, out_ref):
    out_ref[...] = (mine_ref[...] + came_ref[...].astype(jnp.float32)).astype(jnp.bfloat16)


def total_kernel(*refs):
    total_ref = refs[-1]
    total = refs[0][...]
    for ref in refs[1:-1]:
        total = total + ref[...].astype(jnp.float32)
    total_ref[...] = total


def finish_kernel(*refs):
    out_ref = refs[-1]
    lat = out_ref.shape[1]
    total = refs[0][...]
    for ref in refs[1:-1]:
        total = total + ref[...].astype(jnp.float32)
    out_ref[...] = (total[:, :lat] / total[:, lat : lat + 1]).astype(jnp.bfloat16)


def in_vmem(x):
    return pltpu.with_memory_space_constraint(x, pltpu.VMEM)


def in_hbm(x):
    return pltpu.with_memory_space_constraint(x, pltpu.HBM)


VMEM = pl.BlockSpec(memory_space=pltpu.VMEM)
ANY = pl.BlockSpec(memory_space=pl.ANY)


def call(kernel, outs, args=(), deps=(), chain=(), hbm=(), scratch=()):
    n_in = len(args) + len(hbm)
    n_skip = n_in + len(deps)
    n_outs = n_skip + len(chain)

    def body(*refs):
        kernel(*refs[:n_in], *refs[n_outs : n_outs + len(outs)], *refs[n_outs + len(outs) + len(chain) :])

    def body_with_chain(*refs):
        kernel(
            *refs[:n_in],
            *refs[n_skip:n_outs],
            *refs[n_outs : n_outs + len(outs)],
            *refs[n_outs + len(outs) + len(chain) :],
        )

    specs = [VMEM] * len(args)
    specs += [ANY] * (len(hbm) + len(deps)) + [VMEM] * len(chain)
    operands = [in_vmem(a) for a in args] + [in_hbm(h) for h in hbm]
    operands += [in_vmem(x) for x in (*deps, *chain)]
    return pl.pallas_call(
        body_with_chain if kernel is expert_kernel else body,
        out_shape=list(outs) + [pltpu.VMEM(x.shape, x.dtype) for x in chain],
        in_specs=specs,
        out_specs=[VMEM] * (len(outs) + len(chain)),
        scratch_shapes=list(scratch),
        compiler_params=pltpu.CompilerParams(vmem_limit_bytes=SCOPED),
        cost_estimate=pl.CostEstimate(flops=0, bytes_accessed=10_000, transcendentals=0),
        input_output_aliases={n_skip + i: len(outs) + i for i in range(len(chain))},
        name=kernel.__name__.removesuffix("_kernel"),
    )(*operands)


def on_device(latent_in, routes, router, gate_up, expert_down):
    n_dev = lax.axis_size("exp")
    local = gate_up.shape[0]
    eff = expert_down.shape[1]
    rows, lat = latent_in.shape
    wide = lat + TAIL

    def swap(x, bits):
        return lax.ppermute(x, "exp", [(i, i ^ bits) for i in range(n_dev)])

    def space(height, dtype):
        return pltpu.VMEM((height, wide), dtype)

    def weights(dep):
        return call(
            load_kernel,
            [
                pltpu.VMEM((16, lat), jnp.bfloat16),
                pltpu.VMEM(gate_up.shape, gate_up.dtype),
                pltpu.VMEM(expert_down.shape, expert_down.dtype),
            ],
            deps=[dep],
            hbm=[router.T, gate_up, expert_down],
            scratch=[
                pltpu.VMEM((local, lat), jnp.bfloat16),
                pltpu.SemaphoreType.DMA((1 + local * (lat + eff) // PIECE,)),
            ],
        )

    bound = 2 * ((rows * routes.shape[1] + local * n_dev - 1) // (local * n_dev))
    slots = 4 * bound

    def group_pass(mine):
        held = weights(mine)

        def step(kernel, outs, args=(), deps=(), hand_on=(), **more):
            nonlocal held
            result = call(kernel, outs, args, deps, [*held, *hand_on], **more)
            held = result[len(outs) : len(outs) + len(held)]
            return result[: len(outs)] + result[len(outs) + len(held) :]

        def tie(x, deps=()):
            return step(tie_kernel, [], deps=deps, hand_on=[x])[0]

        other, keep, send, came, fold_keep, fold_send, y_came, z_send = {}, {}, {}, {}, {}, {}, {}, {}

        def gather(k, deps=()):
            other[k] = tie(swap(block[k], 2), deps)

        def compute(k):
            blocks = [block[k], other[k]]
            blocks += [swap(one, 1) for one in blocks]
            keep[k], *send[k] = step(
                expert_kernel,
                [space(2 * rows, jnp.float32), space(rows, jnp.bfloat16), space(rows, jnp.bfloat16)],
                blocks,
                scratch=[
                    pltpu.VMEM((local * slots, eff), jnp.bfloat16),
                    pltpu.VMEM((local * slots, lat), jnp.bfloat16),
                ],
            )
            came[k] = [swap(part, 1) for part in send[k]]

        def reduce_core(k):
            fold_keep[k], fold_send[k] = step(
                fold_kernel, [space(rows, jnp.float32), space(rows, jnp.bfloat16)], [keep[k], *came[k]]
            )
            y_came[k] = swap(fold_send[k], 2)

        def reduce_y(k, deps=()):
            z_send[k] = step(add_kernel, [space(rows, jnp.bfloat16)], [fold_keep[k], y_came[k]], deps)[0]
            return swap(z_send[k], 4 * k)

        z_2, z_1, y_0 = swap(mine, 8), swap(mine, 4), swap(mine, 2)
        block = {0: mine, 2: tie(z_2, [y_0]), 1: z_1}
        block[3] = swap(block[2], 4)
        other[0] = y_0
        gather(2, [block[1], block[3]])
        compute(2)
        gather(3)
        gather(1)
        reduce_core(2)
        compute(3)
        z_2 = reduce_y(2)
        reduce_core(3)
        compute(1)
        z_3 = reduce_y(3)
        reduce_core(1)
        compute(0)
        z_1 = reduce_y(1, [z_2])
        reduce_core(0)
        return fold_keep[0], y_came[0], z_1, z_2, z_3

    packet = call(
        pack_kernel,
        [space(rows, jnp.bfloat16)],
        hbm=[routes.T, latent_in],
        scratch=[pltpu.VMEM(routes.shape[::-1], routes.dtype), pltpu.SemaphoreType.DMA((2,))],
    )[0]

    def finish(parts):
        return pl.pallas_call(
            finish_kernel,
            out_shape=jax.ShapeDtypeStruct((rows, lat), jnp.bfloat16),
            in_specs=[VMEM] * len(parts),
            out_specs=VMEM,
            compiler_params=pltpu.CompilerParams(vmem_limit_bytes=SCOPED),
            name="finish",
        )(*[in_vmem(p) for p in parts])

    if n_dev == GROUP:
        return finish(group_pass(packet))

    def next_group(x):
        return lax.ppermute(x, "exp", [(i, (i + GROUP) % n_dev) for i in range(n_dev)])

    def step(carry, _):
        mine, total = carry
        total = call(total_kernel, [space(rows, jnp.float32)], [total, *group_pass(mine)])[0]
        return (next_group(mine), next_group(total)), None

    start = (packet, jnp.zeros((rows, wide), jnp.float32))
    (_, total), _ = lax.scan(step, start, None, length=n_dev // GROUP)
    return finish([total])


def solution(mesh):
    placed = (
        P(("grp", "exp"), None),
        P(("grp", "exp"), None),
        P(None, "exp"),
        P("exp", None, None),
        P("exp", None, None),
    )
    return jax.shard_map(
        on_device, mesh=mesh, in_specs=placed, out_specs=P(("grp", "exp"), None), check_vma=False
    )
```

```python
import functools

import jax
import jax.numpy as jnp
from jax import lax
from jax.experimental import pallas as pl
from jax.experimental.pallas import tpu as pltpu
from jax.sharding import PartitionSpec as P

GROUP = 16
SCOPED = 2 * 1024 * 1024
TAIL = 128
SCALE = 2.0**40
STEP = 256
PIECE = 256


def pack_kernel(ids_hbm, row_hbm, out_ref, ids_ref, sems):
    rows, lat = row_hbm.shape
    top = ids_hbm.shape[0]
    get_ids = pltpu.make_async_copy(ids_hbm, ids_ref, sems.at[0])
    get_rows = pltpu.make_async_copy(row_hbm, out_ref.at[:, pl.ds(0, lat)], sems.at[1])
    get_ids.start()
    get_rows.start()
    get_ids.wait()
    ids = ids_ref[...].astype(jnp.float32)
    ids = jnp.concatenate([ids, jnp.full((top, TAIL - rows), -1.0, jnp.float32)], axis=1)
    ids = jnp.concatenate([ids, jnp.full((TAIL - top, TAIL), -1.0, jnp.float32)], axis=0)
    out_ref[:, lat:] = ids.T[:rows].astype(jnp.bfloat16)
    get_rows.wait()


def load_kernel(router_hbm, up_hbm, down_hbm, columns_ref, up_ref, down_ref, router_ref, sems):
    get_router = pltpu.make_async_copy(router_hbm, router_ref, sems.at[0])
    get_router.start()
    copies = []
    for src, dst in ((up_hbm, up_ref), (down_hbm, down_ref)):
        for e in range(src.shape[0]):
            for r in range(0, src.shape[1], PIECE):
                at = (e, pl.ds(r, PIECE))
                copies.append(pltpu.make_async_copy(src.at[at], dst.at[at], sems.at[1 + len(copies)]))
    for copy in copies:
        copy.start()
    columns_ref[...] = jnp.zeros_like(columns_ref)
    get_router.wait()
    columns_ref[: router_ref.shape[0], :] = router_ref[...]
    for copy in copies:
        copy.wait()


def expert_kernel(
    a_ref, b_ref, c_ref, d_ref, columns_ref, up_ref, down_ref, keep_ref, *refs
):
    *send_refs, inner_ref, result_ref = refs
    blocks = (a_ref, b_ref, c_ref, d_ref)
    rows, wide = a_ref.shape
    half, lat = 2 * rows, wide - TAIL
    local, eff, _ = down_ref.shape
    slots = result_ref.shape[0] // local
    x = jnp.concatenate([ref[:, :lat] for ref in blocks], axis=0)
    tail = jnp.concatenate([ref[:, lat:] for ref in blocks], axis=0).astype(jnp.float32)

    def put(lanes, value):
        keep_ref[:, lanes] = value[:half]
        for i, ref in enumerate(send_refs):
            ref[:, lanes] = value[half + i * rows : half + (i + 1) * rows].astype(jnp.bfloat16)

    def logits_of(values):
        return lax.dot_general(
            values, columns_ref[...], (((1,), (1,)), ((), ())), preferred_element_type=jnp.float32
        )

    logits = logits_of(x)
    lane = lax.broadcasted_iota(jnp.int32, (2 * half, TAIL), 1)
    masks, sums = [], jnp.zeros((2 * half, 1), jnp.float32)
    marks = jnp.zeros((2 * half, TAIL), jnp.float32)
    for e in range(local):
        label = (lax.axis_index("exp") * local + e).astype(jnp.float32)
        mask = jnp.max(jnp.where(tail == label, 1.0, 0.0), axis=1, keepdims=True)
        sums = sums + jax.nn.sigmoid(logits[:, e : e + 1]) * (mask * SCALE)
        marks = jnp.where(lane == e, mask, marks)
        masks.append(mask)
    row = lax.broadcasted_iota(jnp.int32, (2 * half, 2 * half), 0)
    col = lax.broadcasted_iota(jnp.int32, (2 * half, 2 * half), 1)
    before = jnp.where(col < row, 1.0, 0.0).astype(jnp.bfloat16)
    place = jnp.dot(before, marks.astype(jnp.bfloat16), preferred_element_type=jnp.float32)
    slot = lax.broadcasted_iota(jnp.int32, (2 * half, slots), 1).astype(jnp.float32)
    spread = jnp.concatenate(
        [jnp.where((slot == place[:, e : e + 1]) & (masks[e] > 0.0), 1.0, 0.0) for e in range(local)], axis=1
    ).astype(jnp.bfloat16)
    packed = lax.dot_general(
        spread, x, (((0,), (0,)), ((), ())), preferred_element_type=jnp.float32
    ).astype(jnp.bfloat16)
    scores = jax.nn.sigmoid(logits_of(packed)) * SCALE
    for e in range(local):
        mine = slice(e * slots, (e + 1) * slots)
        chosen = packed[mine]
        score = scores[mine, e : e + 1]
        for c in range(0, eff, STEP):
            gate = jnp.dot(chosen, up_ref[e, :, c : c + STEP], preferred_element_type=jnp.float32)
            up = jnp.dot(chosen, up_ref[e, :, eff + c : eff + c + STEP], preferred_element_type=jnp.float32)
            inner_ref[mine, c : c + STEP] = (gate / (1.0 + jnp.exp(-gate)) * up * score).astype(jnp.bfloat16)
    for e in range(local):
        mine = slice(e * slots, (e + 1) * slots)
        result_ref[mine, :] = jnp.dot(
            inner_ref[mine, :], down_ref[e], preferred_element_type=jnp.float32
        ).astype(jnp.bfloat16)
    for c in range(0, lat, STEP):
        part = jnp.dot(spread, result_ref[:, c : c + STEP], preferred_element_type=jnp.float32)
        put(slice(c, c + STEP), part)
    put(slice(lat, wide), jnp.where(lane == 0, sums, 0.0))


def tie_kernel():
    pass


def fold_kernel(mine_ref, came_a_ref, came_b_ref, keep_ref, send_ref):
    rows = keep_ref.shape[0]
    keep_ref[...] = mine_ref[:rows] + came_a_ref[...].astype(jnp.float32)
    send_ref[...] = (mine_ref[rows:] + came_b_ref[...].astype(jnp.float32)).astype(jnp.bfloat16)


def add_kernel(mine_ref, came_ref, out_ref):
    out_ref[...] = (mine_ref[...] + came_ref[...].astype(jnp.float32)).astype(jnp.bfloat16)


def total_kernel(*refs):
    total_ref = refs[-1]
    total = refs[0][...]
    for ref in refs[1:-1]:
        total = total + ref[...].astype(jnp.float32)
    total_ref[...] = total


def finish_kernel(*refs):
    out_ref = refs[-1]
    lat = out_ref.shape[1]
    total = refs[0][...]
    for ref in refs[1:-1]:
        total = total + ref[...].astype(jnp.float32)
    out_ref[...] = (total[:, :lat] / total[:, lat : lat + 1]).astype(jnp.bfloat16)


def in_vmem(x):
    return pltpu.with_memory_space_constraint(x, pltpu.VMEM)


def in_hbm(x):
    return pltpu.with_memory_space_constraint(x, pltpu.HBM)


VMEM = pl.BlockSpec(memory_space=pltpu.VMEM)
ANY = pl.BlockSpec(memory_space=pl.ANY)


def call(kernel, outs, args=(), deps=(), chain=(), hbm=(), scratch=()):
    n_in = len(args) + len(hbm)
    n_skip = n_in + len(deps)
    n_outs = n_skip + len(chain)

    def body(*refs):
        kernel(*refs[:n_in], *refs[n_outs : n_outs + len(outs)], *refs[n_outs + len(outs) + len(chain) :])

    def body_with_chain(*refs):
        kernel(
            *refs[:n_in],
            *refs[n_skip:n_outs],
            *refs[n_outs : n_outs + len(outs)],
            *refs[n_outs + len(outs) + len(chain) :],
        )

    specs = [VMEM] * len(args)
    specs += [ANY] * (len(hbm) + len(deps)) + [VMEM] * len(chain)
    operands = [in_vmem(a) for a in args] + [in_hbm(h) for h in hbm]
    operands += [in_vmem(x) for x in (*deps, *chain)]
    return pl.pallas_call(
        body_with_chain if kernel is expert_kernel else body,
        out_shape=list(outs) + [pltpu.VMEM(x.shape, x.dtype) for x in chain],
        in_specs=specs,
        out_specs=[VMEM] * (len(outs) + len(chain)),
        scratch_shapes=list(scratch),
        compiler_params=pltpu.CompilerParams(vmem_limit_bytes=SCOPED),
        cost_estimate=pl.CostEstimate(flops=0, bytes_accessed=10_000, transcendentals=0),
        input_output_aliases={n_skip + i: len(outs) + i for i in range(len(chain))},
        name=kernel.__name__.removesuffix("_kernel"),
    )(*operands)


def on_device(latent_in, routes, router, gate_up, expert_down):
    n_dev = lax.axis_size("exp")
    local = gate_up.shape[0]
    eff = expert_down.shape[1]
    rows, lat = latent_in.shape
    wide = lat + TAIL

    def swap(x, bits):
        return lax.ppermute(x, "exp", [(i, i ^ bits) for i in range(n_dev)])

    def space(height, dtype):
        return pltpu.VMEM((height, wide), dtype)

    def weights(dep):
        return call(
            load_kernel,
            [
                pltpu.VMEM((16, lat), jnp.bfloat16),
                pltpu.VMEM(gate_up.shape, gate_up.dtype),
                pltpu.VMEM(expert_down.shape, expert_down.dtype),
            ],
            deps=[dep],
            hbm=[router.T, gate_up, expert_down],
            scratch=[
                pltpu.VMEM((local, lat), jnp.bfloat16),
                pltpu.SemaphoreType.DMA((1 + local * (lat + eff) // PIECE,)),
            ],
        )

    bound = 2 * ((rows * routes.shape[1] + local * n_dev - 1) // (local * n_dev))
    slots = 4 * bound

    def group_pass(mine):
        held = weights(mine)

        def step(kernel, outs, args=(), deps=(), hand_on=(), **more):
            nonlocal held
            result = call(kernel, outs, args, deps, [*held, *hand_on], **more)
            held = result[len(outs) : len(outs) + len(held)]
            return result[: len(outs)] + result[len(outs) + len(held) :]

        def tie(x, deps=()):
            return step(tie_kernel, [], deps=deps, hand_on=[x])[0]

        other, keep, send, came, fold_keep, fold_send, y_came, z_send = {}, {}, {}, {}, {}, {}, {}, {}

        def gather(k, deps=()):
            other[k] = tie(swap(block[k], 2), deps)

        def compute(k):
            blocks = [block[k], other[k]]
            blocks += [swap(one, 1) for one in blocks]
            keep[k], *send[k] = step(
                expert_kernel,
                [space(2 * rows, jnp.float32), space(rows, jnp.bfloat16), space(rows, jnp.bfloat16)],
                blocks,
                scratch=[
                    pltpu.VMEM((local * slots, eff), jnp.bfloat16),
                    pltpu.VMEM((local * slots, lat), jnp.bfloat16),
                ],
            )
            came[k] = [swap(part, 1) for part in send[k]]

        def reduce_core(k):
            fold_keep[k], fold_send[k] = step(
                fold_kernel, [space(rows, jnp.float32), space(rows, jnp.bfloat16)], [keep[k], *came[k]]
            )
            y_came[k] = swap(fold_send[k], 2)

        def reduce_y(k, deps=()):
            z_send[k] = step(add_kernel, [space(rows, jnp.bfloat16)], [fold_keep[k], y_came[k]], deps)[0]
            return swap(z_send[k], 4 * k)

        z_2, z_1, y_0 = swap(mine, 8), swap(mine, 4), swap(mine, 2)
        block = {0: mine, 2: tie(z_2, [y_0]), 1: z_1}
        block[3] = swap(block[2], 4)
        other[0] = y_0
        compute(0)
        gather(2, [block[1], block[3]])
        reduce_core(0)
        compute(2)
        gather(3)
        reduce_core(2)
        compute(3)
        gather(1)
        z_2 = reduce_y(2, [y_came[0]])
        reduce_core(3)
        compute(1)
        z_3 = reduce_y(3, [z_2])
        reduce_core(1)
        z_1 = reduce_y(1)
        return fold_keep[0], y_came[0], z_1, z_2, z_3

    packet = call(
        pack_kernel,
        [space(rows, jnp.bfloat16)],
        hbm=[routes.T, latent_in],
        scratch=[pltpu.VMEM(routes.shape[::-1], routes.dtype), pltpu.SemaphoreType.DMA((2,))],
    )[0]

    def finish(parts):
        return pl.pallas_call(
            finish_kernel,
            out_shape=jax.ShapeDtypeStruct((rows, lat), jnp.bfloat16),
            in_specs=[VMEM] * len(parts),
            out_specs=VMEM,
            compiler_params=pltpu.CompilerParams(vmem_limit_bytes=SCOPED),
            name="finish",
        )(*[in_vmem(p) for p in parts])

    if n_dev == GROUP:
        return finish(group_pass(packet))

    def next_group(x):
        return lax.ppermute(x, "exp", [(i, (i + GROUP) % n_dev) for i in range(n_dev)])

    def step(carry, _):
        mine, total = carry
        total = call(total_kernel, [space(rows, jnp.float32)], [total, *group_pass(mine)])[0]
        return (next_group(mine), next_group(total)), None

    start = (packet, jnp.zeros((rows, wide), jnp.float32))
    (_, total), _ = lax.scan(step, start, None, length=n_dev // GROUP)
    return finish([total])


def solution(mesh):
    placed = (
        P(("grp", "exp"), None),
        P(("grp", "exp"), None),
        P(None, "exp"),
        P("exp", None, None),
        P("exp", None, None),
    )
    return jax.shard_map(
        on_device, mesh=mesh, in_specs=placed, out_specs=P(("grp", "exp"), None), check_vma=False
    )
```

```python
import functools

import jax
import jax.numpy as jnp
from jax import lax
from jax.experimental import pallas as pl
from jax.experimental.pallas import tpu as pltpu
from jax.sharding import PartitionSpec as P

GROUP = 16
SCOPED = 2 * 1024 * 1024
TAIL = 128
SCALE = 2.0**40
STEP = 256
PIECE = 256


def pack_kernel(ids_hbm, row_hbm, out_ref, ids_ref, sems):
    rows, lat = row_hbm.shape
    top = ids_hbm.shape[0]
    get_ids = pltpu.make_async_copy(ids_hbm, ids_ref, sems.at[0])
    get_rows = pltpu.make_async_copy(row_hbm, out_ref.at[:, pl.ds(0, lat)], sems.at[1])
    get_ids.start()
    get_rows.start()
    get_ids.wait()
    ids = ids_ref[...].astype(jnp.float32)
    ids = jnp.concatenate([ids, jnp.full((top, TAIL - rows), -1.0, jnp.float32)], axis=1)
    ids = jnp.concatenate([ids, jnp.full((TAIL - top, TAIL), -1.0, jnp.float32)], axis=0)
    out_ref[:, lat:] = ids.T[:rows].astype(jnp.bfloat16)
    get_rows.wait()


def load_kernel(router_hbm, up_hbm, down_hbm, columns_ref, up_ref, down_ref, router_ref, sems):
    get_router = pltpu.make_async_copy(router_hbm, router_ref, sems.at[0])
    get_router.start()
    copies = []
    for src, dst in ((up_hbm, up_ref), (down_hbm, down_ref)):
        for e in range(src.shape[0]):
            for r in range(0, src.shape[1], PIECE):
                at = (e, pl.ds(r, PIECE))
                copies.append(pltpu.make_async_copy(src.at[at], dst.at[at], sems.at[1 + len(copies)]))
    for copy in copies:
        copy.start()
    columns_ref[...] = jnp.zeros_like(columns_ref)
    get_router.wait()
    columns_ref[: router_ref.shape[0], :] = router_ref[...]
    for copy in copies:
        copy.wait()


def expert_kernel(
    a_ref, b_ref, c_ref, d_ref, columns_ref, up_ref, down_ref, keep_ref, *refs
):
    *send_refs, inner_ref, result_ref = refs
    blocks = (a_ref, b_ref, c_ref, d_ref)
    rows, wide = a_ref.shape
    half, lat = 2 * rows, wide - TAIL
    local, eff, _ = down_ref.shape
    slots = result_ref.shape[0] // local
    x = jnp.concatenate([ref[:, :lat] for ref in blocks], axis=0)
    tail = jnp.concatenate([ref[:, lat:] for ref in blocks], axis=0).astype(jnp.float32)

    def put(lanes, value):
        keep_ref[:, lanes] = value[:half]
        for i, ref in enumerate(send_refs):
            ref[:, lanes] = value[half + i * rows : half + (i + 1) * rows].astype(jnp.bfloat16)

    def logits_of(values):
        return lax.dot_general(
            values, columns_ref[...], (((1,), (1,)), ((), ())), preferred_element_type=jnp.float32
        )

    logits = logits_of(x)
    lane = lax.broadcasted_iota(jnp.int32, (2 * half, TAIL), 1)
    masks, sums = [], jnp.zeros((2 * half, 1), jnp.float32)
    marks = jnp.zeros((2 * half, TAIL), jnp.float32)
    for e in range(local):
        label = (lax.axis_index("exp") * local + e).astype(jnp.float32)
        mask = jnp.max(jnp.where(tail == label, 1.0, 0.0), axis=1, keepdims=True)
        sums = sums + jax.nn.sigmoid(logits[:, e : e + 1]) * (mask * SCALE)
        marks = jnp.where(lane == e, mask, marks)
        masks.append(mask)
    row = lax.broadcasted_iota(jnp.int32, (2 * half, 2 * half), 0)
    col = lax.broadcasted_iota(jnp.int32, (2 * half, 2 * half), 1)
    before = jnp.where(col < row, 1.0, 0.0).astype(jnp.bfloat16)
    place = jnp.dot(before, marks.astype(jnp.bfloat16), preferred_element_type=jnp.float32)
    slot = lax.broadcasted_iota(jnp.int32, (2 * half, slots), 1).astype(jnp.float32)
    spread = jnp.concatenate(
        [jnp.where((slot == place[:, e : e + 1]) & (masks[e] > 0.0), 1.0, 0.0) for e in range(local)], axis=1
    ).astype(jnp.bfloat16)
    packed = lax.dot_general(
        spread, x, (((0,), (0,)), ((), ())), preferred_element_type=jnp.float32
    ).astype(jnp.bfloat16)
    scores = jax.nn.sigmoid(logits_of(packed)) * SCALE
    for e in range(local):
        mine = slice(e * slots, (e + 1) * slots)
        chosen = packed[mine]
        score = scores[mine, e : e + 1]
        for c in range(0, eff, STEP):
            gate = jnp.dot(chosen, up_ref[e, :, c : c + STEP], preferred_element_type=jnp.float32)
            up = jnp.dot(chosen, up_ref[e, :, eff + c : eff + c + STEP], preferred_element_type=jnp.float32)
            inner_ref[mine, c : c + STEP] = (gate / (1.0 + jnp.exp(-gate)) * up * score).astype(jnp.bfloat16)
    for e in range(local):
        mine = slice(e * slots, (e + 1) * slots)
        result_ref[mine, :] = jnp.dot(
            inner_ref[mine, :], down_ref[e], preferred_element_type=jnp.float32
        ).astype(jnp.bfloat16)
    for c in range(0, lat, STEP):
        part = jnp.dot(spread, result_ref[:, c : c + STEP], preferred_element_type=jnp.float32)
        put(slice(c, c + STEP), part)
    put(slice(lat, wide), jnp.where(lane == 0, sums, 0.0))


def tie_kernel():
    pass


def fold_kernel(mine_ref, came_a_ref, came_b_ref, keep_ref, send_ref):
    rows = keep_ref.shape[0]
    keep_ref[...] = mine_ref[:rows] + came_a_ref[...].astype(jnp.float32)
    send_ref[...] = (mine_ref[rows:] + came_b_ref[...].astype(jnp.float32)).astype(jnp.bfloat16)


def add_kernel(mine_ref, *refs):
    total = mine_ref[...]
    for ref in refs[:-1]:
        total = total + ref[...].astype(jnp.float32)
    refs[-1][...] = total.astype(jnp.bfloat16)


def total_kernel(*refs):
    total_ref = refs[-1]
    total = refs[0][...]
    for ref in refs[1:-1]:
        total = total + ref[...].astype(jnp.float32)
    total_ref[...] = total


def finish_kernel(*refs):
    out_ref = refs[-1]
    lat = out_ref.shape[1]
    total = refs[0][...]
    for ref in refs[1:-1]:
        total = total + ref[...].astype(jnp.float32)
    out_ref[...] = (total[:, :lat] / total[:, lat : lat + 1]).astype(jnp.bfloat16)


def in_vmem(x):
    return pltpu.with_memory_space_constraint(x, pltpu.VMEM)


def in_hbm(x):
    return pltpu.with_memory_space_constraint(x, pltpu.HBM)


VMEM = pl.BlockSpec(memory_space=pltpu.VMEM)
ANY = pl.BlockSpec(memory_space=pl.ANY)


def call(kernel, outs, args=(), deps=(), chain=(), hbm=(), scratch=()):
    n_in = len(args) + len(hbm)
    n_skip = n_in + len(deps)
    n_outs = n_skip + len(chain)

    def body(*refs):
        kernel(*refs[:n_in], *refs[n_outs : n_outs + len(outs)], *refs[n_outs + len(outs) + len(chain) :])

    def body_with_chain(*refs):
        kernel(
            *refs[:n_in],
            *refs[n_skip:n_outs],
            *refs[n_outs : n_outs + len(outs)],
            *refs[n_outs + len(outs) + len(chain) :],
        )

    specs = [VMEM] * len(args)
    specs += [ANY] * (len(hbm) + len(deps)) + [VMEM] * len(chain)
    operands = [in_vmem(a) for a in args] + [in_hbm(h) for h in hbm]
    operands += [in_vmem(x) for x in (*deps, *chain)]
    return pl.pallas_call(
        body_with_chain if kernel is expert_kernel else body,
        out_shape=list(outs) + [pltpu.VMEM(x.shape, x.dtype) for x in chain],
        in_specs=specs,
        out_specs=[VMEM] * (len(outs) + len(chain)),
        scratch_shapes=list(scratch),
        compiler_params=pltpu.CompilerParams(vmem_limit_bytes=SCOPED),
        cost_estimate=pl.CostEstimate(flops=0, bytes_accessed=10_000, transcendentals=0),
        input_output_aliases={n_skip + i: len(outs) + i for i in range(len(chain))},
        name=kernel.__name__.removesuffix("_kernel"),
    )(*operands)


def on_device(latent_in, routes, router, gate_up, expert_down):
    n_dev = lax.axis_size("exp")
    local = gate_up.shape[0]
    eff = expert_down.shape[1]
    rows, lat = latent_in.shape
    wide = lat + TAIL

    def swap(x, bits):
        return lax.ppermute(x, "exp", [(i, i ^ bits) for i in range(n_dev)])

    def space(height, dtype):
        return pltpu.VMEM((height, wide), dtype)

    def weights(dep):
        return call(
            load_kernel,
            [
                pltpu.VMEM((16, lat), jnp.bfloat16),
                pltpu.VMEM(gate_up.shape, gate_up.dtype),
                pltpu.VMEM(expert_down.shape, expert_down.dtype),
            ],
            deps=[dep],
            hbm=[router.T, gate_up, expert_down],
            scratch=[
                pltpu.VMEM((local, lat), jnp.bfloat16),
                pltpu.SemaphoreType.DMA((1 + local * (lat + eff) // PIECE,)),
            ],
        )

    bound = 2 * ((rows * routes.shape[1] + local * n_dev - 1) // (local * n_dev))
    slots = 4 * bound

    def group_pass(mine):
        held = weights(mine)

        def step(kernel, outs, args=(), deps=(), hand_on=(), **more):
            nonlocal held
            result = call(kernel, outs, args, deps, [*held, *hand_on], **more)
            held = result[len(outs) : len(outs) + len(held)]
            return result[: len(outs)] + result[len(outs) + len(held) :]

        def tie(x, deps=()):
            return step(tie_kernel, [], deps=deps, hand_on=[x])[0]

        other, keep, send, came, fold_keep, fold_send, y_came = {}, {}, {}, {}, {}, {}, {}

        def gather(k, deps=()):
            other[k] = tie(swap(block[k], 2), deps)

        def compute(k):
            blocks = [block[k], other[k]]
            blocks += [swap(one, 1) for one in blocks]
            keep[k], *send[k] = step(
                expert_kernel,
                [space(2 * rows, jnp.float32), space(rows, jnp.bfloat16), space(rows, jnp.bfloat16)],
                blocks,
                scratch=[
                    pltpu.VMEM((local * slots, eff), jnp.bfloat16),
                    pltpu.VMEM((local * slots, lat), jnp.bfloat16),
                ],
            )
            came[k] = [swap(part, 1) for part in send[k]]

        def reduce_core(k):
            fold_keep[k], fold_send[k] = step(
                fold_kernel, [space(rows, jnp.float32), space(rows, jnp.bfloat16)], [keep[k], *came[k]]
            )
            y_came[k] = swap(fold_send[k], 2)

        def reduce_y(k, *more):
            return step(add_kernel, [space(rows, jnp.bfloat16)], [fold_keep[k], y_came[k], *more])[0]

        z_2, z_1, y_0 = swap(mine, 8), swap(mine, 4), swap(mine, 2)
        block = {0: mine, 2: tie(z_2), 1: z_1}
        block[3] = swap(block[2], 4)
        other[0] = y_0
        gather(2, [block[1], block[3], y_0])
        compute(2)
        gather(3)
        reduce_core(2)
        compute(3)
        gather(1, [y_came[2]])
        reduce_core(3)
        compute(1)
        z_3 = swap(reduce_y(3), 4)
        reduce_core(1)
        compute(0)
        z_2 = swap(reduce_y(2, z_3), 8)
        z_1 = swap(reduce_y(1), 4)
        reduce_core(0)
        return fold_keep[0], z_2, z_1, y_came[0]

    packet = call(
        pack_kernel,
        [space(rows, jnp.bfloat16)],
        hbm=[routes.T, latent_in],
        scratch=[pltpu.VMEM(routes.shape[::-1], routes.dtype), pltpu.SemaphoreType.DMA((2,))],
    )[0]

    def finish(parts):
        return pl.pallas_call(
            finish_kernel,
            out_shape=jax.ShapeDtypeStruct((rows, lat), jnp.bfloat16),
            in_specs=[VMEM] * len(parts),
            out_specs=VMEM,
            compiler_params=pltpu.CompilerParams(vmem_limit_bytes=SCOPED),
            name="finish",
        )(*[in_vmem(p) for p in parts])

    if n_dev == GROUP:
        return finish(group_pass(packet))

    def next_group(x):
        return lax.ppermute(x, "exp", [(i, (i + GROUP) % n_dev) for i in range(n_dev)])

    def step(carry, _):
        mine, total = carry
        total = call(total_kernel, [space(rows, jnp.float32)], [total, *group_pass(mine)])[0]
        return (next_group(mine), next_group(total)), None

    start = (packet, jnp.zeros((rows, wide), jnp.float32))
    (_, total), _ = lax.scan(step, start, None, length=n_dev // GROUP)
    return finish([total])


def solution(mesh):
    placed = (
        P(("grp", "exp"), None),
        P(("grp", "exp"), None),
        P(None, "exp"),
        P("exp", None, None),
        P("exp", None, None),
    )
    return jax.shard_map(
        on_device, mesh=mesh, in_specs=placed, out_specs=P(("grp", "exp"), None), check_vma=False
    )
```

```python
import functools

import jax
import jax.numpy as jnp
from jax import lax
from jax.experimental import pallas as pl
from jax.experimental.pallas import tpu as pltpu
from jax.sharding import PartitionSpec as P

GROUP = 16
SCOPED = 8 * 1024 * 1024
TAIL = 128
SCALE = 2.0**40
STEP = 256
PIECE = 256


def pack_kernel(ids_hbm, row_hbm, out_ref, ids_ref, sems):
    rows, lat = row_hbm.shape
    top = ids_hbm.shape[0]
    get_ids = pltpu.make_async_copy(ids_hbm, ids_ref, sems.at[0])
    get_rows = pltpu.make_async_copy(row_hbm, out_ref.at[:, pl.ds(0, lat)], sems.at[1])
    get_ids.start()
    get_rows.start()
    get_ids.wait()
    ids = ids_ref[...].astype(jnp.float32)
    ids = jnp.concatenate([ids, jnp.full((top, TAIL - rows), -1.0, jnp.float32)], axis=1)
    ids = jnp.concatenate([ids, jnp.full((TAIL - top, TAIL), -1.0, jnp.float32)], axis=0)
    out_ref[:, lat:] = ids.T[:rows].astype(jnp.bfloat16)
    get_rows.wait()


def load_kernel(router_hbm, up_hbm, down_hbm, columns_ref, up_ref, down_ref, router_ref, sems):
    get_router = pltpu.make_async_copy(router_hbm, router_ref, sems.at[0])
    get_router.start()
    copies = []
    for src, dst in ((up_hbm, up_ref), (down_hbm, down_ref)):
        for e in range(src.shape[0]):
            for r in range(0, src.shape[1], PIECE):
                at = (e, pl.ds(r, PIECE))
                copies.append(pltpu.make_async_copy(src.at[at], dst.at[at], sems.at[1 + len(copies)]))
    for copy in copies:
        copy.start()
    columns_ref[...] = jnp.zeros_like(columns_ref)
    get_router.wait()
    columns_ref[: router_ref.shape[0], :] = router_ref[...]
    for copy in copies:
        copy.wait()


def expert_kernel(count, *refs):
    blocks, refs = refs[: 4 * count], refs[4 * count :]
    (columns_ref, up_ref, down_ref), refs = refs[:3], refs[3:]
    keep_refs, refs = refs[:count], refs[count:]
    send_refs, (packed_ref, inner_ref, result_ref) = refs[: 2 * count], refs[2 * count :]
    rows, wide = blocks[0].shape
    half, lat = 2 * rows, wide - TAIL
    local, eff, _ = down_ref.shape
    slots = packed_ref.shape[1] // count

    def put(i, lanes, value):
        keep_refs[i][:, lanes] = value[:half]
        for j, ref in enumerate(send_refs[2 * i : 2 * i + 2]):
            ref[:, lanes] = value[half + j * rows : half + (j + 1) * rows].astype(jnp.bfloat16)

    def logits_of(values):
        return lax.dot_general(
            values, columns_ref[...], (((1,), (1,)), ((), ())), preferred_element_type=jnp.float32
        )

    lane = lax.broadcasted_iota(jnp.int32, (2 * half, TAIL), 1)
    row = lax.broadcasted_iota(jnp.int32, (2 * half, 2 * half), 0)
    col = lax.broadcasted_iota(jnp.int32, (2 * half, 2 * half), 1)
    before = jnp.where(col < row, 1.0, 0.0).astype(jnp.bfloat16)
    slot = lax.broadcasted_iota(jnp.int32, (2 * half, slots), 1).astype(jnp.float32)
    spreads = []
    for i in range(count):
        batch = blocks[4 * i : 4 * i + 4]
        x = jnp.concatenate([ref[:, :lat] for ref in batch], axis=0)
        tail = jnp.concatenate([ref[:, lat:] for ref in batch], axis=0).astype(jnp.float32)
        logits = logits_of(x)
        masks, sums = [], jnp.zeros((2 * half, 1), jnp.float32)
        marks = jnp.zeros((2 * half, TAIL), jnp.float32)
        for e in range(local):
            label = (lax.axis_index("exp") * local + e).astype(jnp.float32)
            mask = jnp.max(jnp.where(tail == label, 1.0, 0.0), axis=1, keepdims=True)
            sums = sums + jax.nn.sigmoid(logits[:, e : e + 1]) * (mask * SCALE)
            marks = jnp.where(lane == e, mask, marks)
            masks.append(mask)
        put(i, slice(lat, wide), jnp.where(lane == 0, sums, 0.0))
        place = jnp.dot(before, marks.astype(jnp.bfloat16), preferred_element_type=jnp.float32)
        spread = jnp.concatenate(
            [jnp.where((slot == place[:, e : e + 1]) & (masks[e] > 0.0), 1.0, 0.0) for e in range(local)],
            axis=1,
        ).astype(jnp.bfloat16)
        packed = lax.dot_general(
            spread, x, (((0,), (0,)), ((), ())), preferred_element_type=jnp.float32
        ).astype(jnp.bfloat16)
        for e in range(local):
            packed_ref[e, i * slots : (i + 1) * slots, :] = packed[e * slots : (e + 1) * slots]
        spreads.append(spread)
    for e in range(local):
        chosen = packed_ref[e]
        score = jax.nn.sigmoid(logits_of(chosen)[:, e : e + 1]) * SCALE
        for c in range(0, eff, STEP):
            gate = jnp.dot(chosen, up_ref[e, :, c : c + STEP], preferred_element_type=jnp.float32)
            up = jnp.dot(chosen, up_ref[e, :, eff + c : eff + c + STEP], preferred_element_type=jnp.float32)
            inner_ref[e, :, c : c + STEP] = (gate / (1.0 + jnp.exp(-gate)) * up * score).astype(jnp.bfloat16)
    for e in range(local):
        result = jnp.dot(inner_ref[e], down_ref[e], preferred_element_type=jnp.float32).astype(jnp.bfloat16)
        for i in range(count):
            result_ref[i, e * slots : (e + 1) * slots, :] = result[i * slots : (i + 1) * slots]
    for i in range(count):
        for c in range(0, lat, STEP):
            part = jnp.dot(spreads[i], result_ref[i, :, c : c + STEP], preferred_element_type=jnp.float32)
            put(i, slice(c, c + STEP), part)


def tie_kernel():
    pass


def fold_kernel(mine_ref, came_a_ref, came_b_ref, keep_ref, send_ref):
    rows = keep_ref.shape[0]
    keep_ref[...] = mine_ref[:rows] + came_a_ref[...].astype(jnp.float32)
    send_ref[...] = (mine_ref[rows:] + came_b_ref[...].astype(jnp.float32)).astype(jnp.bfloat16)


def add_kernel(mine_ref, *refs):
    total = mine_ref[...]
    for ref in refs[:-1]:
        total = total + ref[...].astype(jnp.float32)
    refs[-1][...] = total.astype(jnp.bfloat16)


def total_kernel(*refs):
    total_ref = refs[-1]
    total = refs[0][...]
    for ref in refs[1:-1]:
        total = total + ref[...].astype(jnp.float32)
    total_ref[...] = total


def finish_kernel(*refs):
    out_ref = refs[-1]
    lat = out_ref.shape[1]
    total = refs[0][...]
    for ref in refs[1:-1]:
        total = total + ref[...].astype(jnp.float32)
    out_ref[...] = (total[:, :lat] / total[:, lat : lat + 1]).astype(jnp.bfloat16)


def in_vmem(x):
    return pltpu.with_memory_space_constraint(x, pltpu.VMEM)


def in_hbm(x):
    return pltpu.with_memory_space_constraint(x, pltpu.HBM)


VMEM = pl.BlockSpec(memory_space=pltpu.VMEM)
ANY = pl.BlockSpec(memory_space=pl.ANY)


def call(kernel, outs, args=(), deps=(), chain=(), hbm=(), scratch=()):
    plain = getattr(kernel, "func", kernel)
    reads_chain = plain is expert_kernel
    n_in = len(args) + len(hbm)
    n_skip = n_in + len(deps)
    n_outs = n_skip + len(chain)

    def body(*refs):
        kernel(*refs[:n_in], *refs[n_outs : n_outs + len(outs)], *refs[n_outs + len(outs) + len(chain) :])

    def body_with_chain(*refs):
        kernel(
            *refs[:n_in],
            *refs[n_skip:n_outs],
            *refs[n_outs : n_outs + len(outs)],
            *refs[n_outs + len(outs) + len(chain) :],
        )

    specs = [VMEM] * len(args)
    specs += [ANY] * (len(hbm) + len(deps)) + [VMEM] * len(chain)
    operands = [in_vmem(a) for a in args] + [in_hbm(h) for h in hbm]
    operands += [in_vmem(x) for x in (*deps, *chain)]
    return pl.pallas_call(
        body_with_chain if reads_chain else body,
        out_shape=list(outs) + [pltpu.VMEM(x.shape, x.dtype) for x in chain],
        in_specs=specs,
        out_specs=[VMEM] * (len(outs) + len(chain)),
        scratch_shapes=list(scratch),
        compiler_params=pltpu.CompilerParams(vmem_limit_bytes=SCOPED),
        cost_estimate=pl.CostEstimate(flops=0, bytes_accessed=10_000, transcendentals=0),
        input_output_aliases={n_skip + i: len(outs) + i for i in range(len(chain))},
        name=plain.__name__.removesuffix("_kernel"),
    )(*operands)


def on_device(latent_in, routes, router, gate_up, expert_down):
    n_dev = lax.axis_size("exp")
    local = gate_up.shape[0]
    eff = expert_down.shape[1]
    rows, lat = latent_in.shape
    wide = lat + TAIL

    def swap(x, bits):
        return lax.ppermute(x, "exp", [(i, i ^ bits) for i in range(n_dev)])

    def space(height, dtype):
        return pltpu.VMEM((height, wide), dtype)

    def weights(dep):
        return call(
            load_kernel,
            [
                pltpu.VMEM((16, lat), jnp.bfloat16),
                pltpu.VMEM(gate_up.shape, gate_up.dtype),
                pltpu.VMEM(expert_down.shape, expert_down.dtype),
            ],
            deps=[dep],
            hbm=[router.T, gate_up, expert_down],
            scratch=[
                pltpu.VMEM((local, lat), jnp.bfloat16),
                pltpu.SemaphoreType.DMA((1 + local * (lat + eff) // PIECE,)),
            ],
        )

    bound = 2 * ((rows * routes.shape[1] + local * n_dev - 1) // (local * n_dev))
    slots = 4 * bound

    def group_pass(mine):
        held = weights(mine)

        def step(kernel, outs, args=(), deps=(), hand_on=(), **more):
            nonlocal held
            result = call(kernel, outs, args, deps, [*held, *hand_on], **more)
            held = result[len(outs) : len(outs) + len(held)]
            return result[: len(outs)] + result[len(outs) + len(held) :]

        def tie(x, deps=()):
            return step(tie_kernel, [], deps=deps, hand_on=[x])[0]

        other, keep, send, came, fold_keep, fold_send, y_came = {}, {}, {}, {}, {}, {}, {}

        def gather(k, deps=()):
            other[k] = tie(swap(block[k], 2), deps)

        def compute(*ks):
            count = len(ks)
            blocks = []
            for k in ks:
                near = [block[k], other[k]]
                blocks += near + [swap(one, 1) for one in near]
            result = step(
                functools.partial(expert_kernel, count),
                [space(2 * rows, jnp.float32)] * count + [space(rows, jnp.bfloat16)] * (2 * count),
                blocks,
                scratch=[
                    pltpu.VMEM((local, count * slots, lat), jnp.bfloat16),
                    pltpu.VMEM((local, count * slots, eff), jnp.bfloat16),
                    pltpu.VMEM((count, local * slots, lat), jnp.bfloat16),
                ],
            )
            for i, k in enumerate(ks):
                keep[k] = result[i]
                came[k] = [swap(part, 1) for part in result[count + 2 * i : count + 2 * i + 2]]

        def reduce_core(k, deps=()):
            fold_keep[k], fold_send[k] = step(
                fold_kernel, [space(rows, jnp.float32), space(rows, jnp.bfloat16)], [keep[k], *came[k]], deps
            )
            y_came[k] = swap(fold_send[k], 2)

        def reduce_y(k, *more):
            return step(add_kernel, [space(rows, jnp.bfloat16)], [fold_keep[k], y_came[k], *more])[0]

        z_2, z_1, y_0 = swap(mine, 8), swap(mine, 4), swap(mine, 2)
        block = {0: mine, 2: tie(z_2), 1: z_1}
        block[3] = swap(block[2], 4)
        other[0] = y_0
        gather(2, [block[1], block[3], y_0])
        compute(2)
        gather(3)
        reduce_core(2)
        gather(1)
        compute(3)
        reduce_core(3, [y_came[2]])
        compute(1, 0)
        z_3 = swap(reduce_y(3), 4)
        reduce_core(1)
        reduce_core(0)
        z_2 = swap(reduce_y(2, z_3), 8)
        z_1 = swap(reduce_y(1), 4)
        return fold_keep[0], z_2, z_1, y_came[0]

    packet = call(
        pack_kernel,
        [space(rows, jnp.bfloat16)],
        hbm=[routes.T, latent_in],
        scratch=[pltpu.VMEM(routes.shape[::-1], routes.dtype), pltpu.SemaphoreType.DMA((2,))],
    )[0]

    def finish(parts):
        return pl.pallas_call(
            finish_kernel,
            out_shape=jax.ShapeDtypeStruct((rows, lat), jnp.bfloat16),
            in_specs=[VMEM] * len(parts),
            out_specs=VMEM,
            compiler_params=pltpu.CompilerParams(vmem_limit_bytes=SCOPED),
            name="finish",
        )(*[in_vmem(p) for p in parts])

    if n_dev == GROUP:
        return finish(group_pass(packet))

    def next_group(x):
        return lax.ppermute(x, "exp", [(i, (i + GROUP) % n_dev) for i in range(n_dev)])

    def step(carry, _):
        mine, total = carry
        total = call(total_kernel, [space(rows, jnp.float32)], [total, *group_pass(mine)])[0]
        return (next_group(mine), next_group(total)), None

    start = (packet, jnp.zeros((rows, wide), jnp.float32))
    (_, total), _ = lax.scan(step, start, None, length=n_dev // GROUP)
    return finish([total])


def solution(mesh):
    placed = (
        P(("grp", "exp"), None),
        P(("grp", "exp"), None),
        P(None, "exp"),
        P("exp", None, None),
        P("exp", None, None),
    )
    return jax.shard_map(
        on_device, mesh=mesh, in_specs=placed, out_specs=P(("grp", "exp"), None), check_vma=False
    )
```

```python
import functools

import jax
import jax.numpy as jnp
from jax import lax
from jax.experimental import pallas as pl
from jax.experimental.pallas import tpu as pltpu
from jax.sharding import PartitionSpec as P

GROUP = 16
SCOPED = 8 * 1024 * 1024
TAIL = 128
SCALE = 2.0**40
STEP = 256
PIECE = 256


def pack_kernel(ids_hbm, row_hbm, out_ref, ids_ref, sems):
    rows, lat = row_hbm.shape
    top = ids_hbm.shape[0]
    get_ids = pltpu.make_async_copy(ids_hbm, ids_ref, sems.at[0])
    get_rows = pltpu.make_async_copy(row_hbm, out_ref.at[:, pl.ds(0, lat)], sems.at[1])
    get_ids.start()
    get_rows.start()
    get_ids.wait()
    ids = ids_ref[...].astype(jnp.float32)
    ids = jnp.concatenate([ids, jnp.full((top, TAIL - rows), -1.0, jnp.float32)], axis=1)
    ids = jnp.concatenate([ids, jnp.full((TAIL - top, TAIL), -1.0, jnp.float32)], axis=0)
    out_ref[:, lat:] = ids.T[:rows].astype(jnp.bfloat16)
    get_rows.wait()


def load_kernel(router_hbm, up_hbm, down_hbm, columns_ref, up_ref, down_ref, router_ref, sems):
    get_router = pltpu.make_async_copy(router_hbm, router_ref, sems.at[0])
    get_router.start()
    copies = []
    for src, dst in ((up_hbm, up_ref), (down_hbm, down_ref)):
        for e in range(src.shape[0]):
            for r in range(0, src.shape[1], PIECE):
                at = (e, pl.ds(r, PIECE))
                copies.append(pltpu.make_async_copy(src.at[at], dst.at[at], sems.at[1 + len(copies)]))
    for copy in copies:
        copy.start()
    get_router.wait()
    local, lat = router_ref.shape
    wide = jnp.concatenate(
        [router_ref[...].astype(jnp.float32), jnp.zeros((TAIL - local, lat), jnp.float32)], axis=0
    )
    columns_ref[...] = wide.T.astype(jnp.bfloat16)
    for copy in copies:
        copy.wait()


def expert_kernel(count, *refs):
    blocks, refs = refs[: 4 * count], refs[4 * count :]
    (columns_ref, up_ref, down_ref), refs = refs[:3], refs[3:]
    keep_refs, refs = refs[:count], refs[count:]
    send_refs, (packed_ref, inner_ref, result_ref) = refs[: 2 * count], refs[2 * count :]
    rows, wide = blocks[0].shape
    half, lat = 2 * rows, wide - TAIL
    local, eff, _ = down_ref.shape
    slots = packed_ref.shape[1] // count

    def put(i, lanes, value):
        keep_refs[i][:, lanes] = value[:half]
        for j, ref in enumerate(send_refs[2 * i : 2 * i + 2]):
            ref[:, lanes] = value[half + j * rows : half + (j + 1) * rows].astype(jnp.bfloat16)

    def logits_of(values):
        return jnp.dot(values, columns_ref[...], preferred_element_type=jnp.float32)

    size = 2 * half
    row = lax.broadcasted_iota(jnp.int32, (size, size), 0)
    col = lax.broadcasted_iota(jnp.int32, (size, size), 1)
    before = jnp.where(col < row, 1.0, 0.0).astype(jnp.bfloat16)
    after = jnp.where(row < col, 1.0, 0.0).astype(jnp.bfloat16)
    lane = lax.broadcasted_iota(jnp.int32, (size, TAIL), 1)
    line = lax.broadcasted_iota(jnp.int32, (16, size), 0)
    slot = lax.broadcasted_iota(jnp.int32, (size, slots), 1).astype(jnp.float32)
    slot_t = lax.broadcasted_iota(jnp.int32, (slots, size), 0).astype(jnp.float32)
    labels = [(lax.axis_index("exp") * local + e).astype(jnp.float32) for e in range(local)]
    spreads = []
    for i in range(count):
        batch = blocks[4 * i : 4 * i + 4]
        x = jnp.concatenate([ref[:, :lat] for ref in batch], axis=0)
        tail = jnp.concatenate([ref[:, lat:] for ref in batch], axis=0).astype(jnp.float32)
        masks = [jnp.max(jnp.where(tail == label, 1.0, 0.0), axis=1, keepdims=True) for label in labels]
        tail_t = tail.T[:16]
        masks_t = [jnp.max(jnp.where(tail_t == label, 1.0, 0.0), axis=0, keepdims=True) for label in labels]
        marks, marks_t = jnp.zeros((size, TAIL), jnp.float32), jnp.zeros((16, size), jnp.float32)
        for e in range(local):
            marks = jnp.where(lane == e, masks[e], marks)
            marks_t = jnp.where(line == e, masks_t[e], marks_t)
        place_t = jnp.dot(marks_t.astype(jnp.bfloat16), after, preferred_element_type=jnp.float32)
        place = jnp.dot(before, marks.astype(jnp.bfloat16), preferred_element_type=jnp.float32)
        gather = jnp.concatenate(
            [
                jnp.where((slot_t == place_t[e : e + 1]) & (masks_t[e] > 0.0), 1.0, 0.0)
                for e in range(local)
            ],
            axis=0,
        ).astype(jnp.bfloat16)
        packed = jnp.dot(gather, x, preferred_element_type=jnp.float32).astype(jnp.bfloat16)
        spread = jnp.concatenate(
            [jnp.where((slot == place[:, e : e + 1]) & (masks[e] > 0.0), 1.0, 0.0) for e in range(local)],
            axis=1,
        ).astype(jnp.bfloat16)
        logits = logits_of(x)
        sums = jnp.zeros((size, 1), jnp.float32)
        for e in range(local):
            sums = sums + jax.nn.sigmoid(logits[:, e : e + 1]) * (masks[e] * SCALE)
        put(i, slice(lat, wide), jnp.where(lane == 0, sums, 0.0))
        for e in range(local):
            packed_ref[e, i * slots : (i + 1) * slots, :] = packed[e * slots : (e + 1) * slots]
        spreads.append(spread)
    for e in range(local):
        chosen = packed_ref[e]
        score = jax.nn.sigmoid(logits_of(chosen)[:, e : e + 1]) * SCALE
        for c in range(0, eff, STEP):
            gate = jnp.dot(chosen, up_ref[e, :, c : c + STEP], preferred_element_type=jnp.float32)
            up = jnp.dot(chosen, up_ref[e, :, eff + c : eff + c + STEP], preferred_element_type=jnp.float32)
            inner_ref[e, :, c : c + STEP] = (gate / (1.0 + jnp.exp(-gate)) * up * score).astype(jnp.bfloat16)
    for e in range(local):
        result = jnp.dot(inner_ref[e], down_ref[e], preferred_element_type=jnp.float32).astype(jnp.bfloat16)
        for i in range(count):
            result_ref[i, e * slots : (e + 1) * slots, :] = result[i * slots : (i + 1) * slots]
    for i in range(count):
        for c in range(0, lat, STEP):
            part = jnp.dot(spreads[i], result_ref[i, :, c : c + STEP], preferred_element_type=jnp.float32)
            put(i, slice(c, c + STEP), part)


def tie_kernel():
    pass


def fold_kernel(mine_ref, came_a_ref, came_b_ref, keep_ref, send_ref):
    rows = keep_ref.shape[0]
    keep_ref[...] = mine_ref[:rows] + came_a_ref[...].astype(jnp.float32)
    send_ref[...] = (mine_ref[rows:] + came_b_ref[...].astype(jnp.float32)).astype(jnp.bfloat16)


def add_kernel(mine_ref, *refs):
    total = mine_ref[...]
    for ref in refs[:-1]:
        total = total + ref[...].astype(jnp.float32)
    refs[-1][...] = total.astype(jnp.bfloat16)


def total_kernel(*refs):
    total_ref = refs[-1]
    total = refs[0][...]
    for ref in refs[1:-1]:
        total = total + ref[...].astype(jnp.float32)
    total_ref[...] = total


def finish_kernel(*refs):
    out_ref = refs[-1]
    lat = out_ref.shape[1]
    total = refs[0][...]
    for ref in refs[1:-1]:
        total = total + ref[...].astype(jnp.float32)
    out_ref[...] = (total[:, :lat] / total[:, lat : lat + 1]).astype(jnp.bfloat16)


def in_vmem(x):
    return pltpu.with_memory_space_constraint(x, pltpu.VMEM)


def in_hbm(x):
    return pltpu.with_memory_space_constraint(x, pltpu.HBM)


VMEM = pl.BlockSpec(memory_space=pltpu.VMEM)
ANY = pl.BlockSpec(memory_space=pl.ANY)


def call(kernel, outs, args=(), deps=(), chain=(), hbm=(), scratch=()):
    plain = getattr(kernel, "func", kernel)
    reads_chain = plain is expert_kernel
    n_in = len(args) + len(hbm)
    n_skip = n_in + len(deps)
    n_outs = n_skip + len(chain)

    def body(*refs):
        kernel(*refs[:n_in], *refs[n_outs : n_outs + len(outs)], *refs[n_outs + len(outs) + len(chain) :])

    def body_with_chain(*refs):
        kernel(
            *refs[:n_in],
            *refs[n_skip:n_outs],
            *refs[n_outs : n_outs + len(outs)],
            *refs[n_outs + len(outs) + len(chain) :],
        )

    specs = [VMEM] * len(args)
    specs += [ANY] * (len(hbm) + len(deps)) + [VMEM] * len(chain)
    operands = [in_vmem(a) for a in args] + [in_hbm(h) for h in hbm]
    operands += [in_vmem(x) for x in (*deps, *chain)]
    return pl.pallas_call(
        body_with_chain if reads_chain else body,
        out_shape=list(outs) + [pltpu.VMEM(x.shape, x.dtype) for x in chain],
        in_specs=specs,
        out_specs=[VMEM] * (len(outs) + len(chain)),
        scratch_shapes=list(scratch),
        compiler_params=pltpu.CompilerParams(vmem_limit_bytes=SCOPED),
        cost_estimate=pl.CostEstimate(flops=0, bytes_accessed=10_000, transcendentals=0),
        input_output_aliases={n_skip + i: len(outs) + i for i in range(len(chain))},
        name=plain.__name__.removesuffix("_kernel"),
    )(*operands)


def on_device(latent_in, routes, router, gate_up, expert_down):
    n_dev = lax.axis_size("exp")
    local = gate_up.shape[0]
    eff = expert_down.shape[1]
    rows, lat = latent_in.shape
    wide = lat + TAIL

    def swap(x, bits):
        return lax.ppermute(x, "exp", [(i, i ^ bits) for i in range(n_dev)])

    def space(height, dtype):
        return pltpu.VMEM((height, wide), dtype)

    def weights(dep):
        return call(
            load_kernel,
            [
                pltpu.VMEM((lat, TAIL), jnp.bfloat16),
                pltpu.VMEM(gate_up.shape, gate_up.dtype),
                pltpu.VMEM(expert_down.shape, expert_down.dtype),
            ],
            deps=[dep],
            hbm=[router.T, gate_up, expert_down],
            scratch=[
                pltpu.VMEM((local, lat), jnp.bfloat16),
                pltpu.SemaphoreType.DMA((1 + local * (lat + eff) // PIECE,)),
            ],
        )

    bound = 2 * ((rows * routes.shape[1] + local * n_dev - 1) // (local * n_dev))
    slots = 4 * bound

    def group_pass(mine):
        held = weights(mine)

        def step(kernel, outs, args=(), deps=(), hand_on=(), **more):
            nonlocal held
            result = call(kernel, outs, args, deps, [*held, *hand_on], **more)
            held = result[len(outs) : len(outs) + len(held)]
            return result[: len(outs)] + result[len(outs) + len(held) :]

        def tie(x, deps=()):
            return step(tie_kernel, [], deps=deps, hand_on=[x])[0]

        other, keep, send, came, fold_keep, fold_send, y_came = {}, {}, {}, {}, {}, {}, {}

        def gather(k, deps=()):
            other[k] = tie(swap(block[k], 2), deps)

        def compute(*ks):
            count = len(ks)
            blocks = []
            for k in ks:
                near = [block[k], other[k]]
                blocks += near + [swap(one, 1) for one in near]
            result = step(
                functools.partial(expert_kernel, count),
                [space(2 * rows, jnp.float32)] * count + [space(rows, jnp.bfloat16)] * (2 * count),
                blocks,
                scratch=[
                    pltpu.VMEM((local, count * slots, lat), jnp.bfloat16),
                    pltpu.VMEM((local, count * slots, eff), jnp.bfloat16),
                    pltpu.VMEM((count, local * slots, lat), jnp.bfloat16),
                ],
            )
            for i, k in enumerate(ks):
                keep[k] = result[i]
                came[k] = [swap(part, 1) for part in result[count + 2 * i : count + 2 * i + 2]]

        def reduce_core(k, deps=()):
            fold_keep[k], fold_send[k] = step(
                fold_kernel, [space(rows, jnp.float32), space(rows, jnp.bfloat16)], [keep[k], *came[k]], deps
            )
            y_came[k] = swap(fold_send[k], 2)

        def reduce_y(k, *more):
            return step(add_kernel, [space(rows, jnp.bfloat16)], [fold_keep[k], y_came[k], *more])[0]

        z_2, z_1, y_0 = swap(mine, 8), swap(mine, 4), swap(mine, 2)
        block = {0: mine, 2: tie(z_2), 1: z_1}
        block[3] = swap(block[2], 4)
        other[0] = y_0
        gather(2, [block[1], block[3], y_0])
        compute(2)
        gather(3)
        reduce_core(2)
        compute(3)
        gather(1)
        reduce_core(3, [y_came[2]])
        compute(1, 0)
        z_3 = swap(reduce_y(3), 4)
        reduce_core(1)
        reduce_core(0)
        z_2 = swap(reduce_y(2, z_3), 8)
        z_1 = swap(reduce_y(1), 4)
        return fold_keep[0], z_2, z_1, y_came[0]

    packet = call(
        pack_kernel,
        [space(rows, jnp.bfloat16)],
        hbm=[routes.T, latent_in],
        scratch=[pltpu.VMEM(routes.shape[::-1], routes.dtype), pltpu.SemaphoreType.DMA((2,))],
    )[0]

    def finish(parts):
        return pl.pallas_call(
            finish_kernel,
            out_shape=jax.ShapeDtypeStruct((rows, lat), jnp.bfloat16),
            in_specs=[VMEM] * len(parts),
            out_specs=VMEM,
            compiler_params=pltpu.CompilerParams(vmem_limit_bytes=SCOPED),
            name="finish",
        )(*[in_vmem(p) for p in parts])

    if n_dev == GROUP:
        return finish(group_pass(packet))

    def next_group(x):
        return lax.ppermute(x, "exp", [(i, (i + GROUP) % n_dev) for i in range(n_dev)])

    def step(carry, _):
        mine, total = carry
        total = call(total_kernel, [space(rows, jnp.float32)], [total, *group_pass(mine)])[0]
        return (next_group(mine), next_group(total)), None

    start = (packet, jnp.zeros((rows, wide), jnp.float32))
    (_, total), _ = lax.scan(step, start, None, length=n_dev // GROUP)
    return finish([total])


def solution(mesh):
    placed = (
        P(("grp", "exp"), None),
        P(("grp", "exp"), None),
        P(None, "exp"),
        P("exp", None, None),
        P("exp", None, None),
    )
    return jax.shard_map(
        on_device, mesh=mesh, in_specs=placed, out_specs=P(("grp", "exp"), None), check_vma=False
    )
```

```python
import functools

import jax
import jax.numpy as jnp
from jax import lax
from jax.experimental import pallas as pl
from jax.experimental.pallas import tpu as pltpu
from jax.sharding import PartitionSpec as P

GROUP = 16
SCOPED = 8 * 1024 * 1024
TAIL = 128
SCALE = 2.0**40
STEP = 256
PIECE = 256


def pack_kernel(ids_hbm, row_hbm, out_ref, ids_ref, sems):
    rows, lat = row_hbm.shape
    top = ids_hbm.shape[0]
    get_ids = pltpu.make_async_copy(ids_hbm, ids_ref, sems.at[0])
    get_rows = pltpu.make_async_copy(row_hbm, out_ref.at[:, pl.ds(0, lat)], sems.at[1])
    get_ids.start()
    get_rows.start()
    get_ids.wait()
    ids = ids_ref[...].astype(jnp.float32)
    ids = jnp.concatenate([ids, jnp.full((top, TAIL - rows), -1.0, jnp.float32)], axis=1)
    ids = jnp.concatenate([ids, jnp.full((TAIL - top, TAIL), -1.0, jnp.float32)], axis=0)
    out_ref[:, lat:] = ids.T[:rows].astype(jnp.bfloat16)
    get_rows.wait()


def load_kernel(router_hbm, up_hbm, down_hbm, columns_ref, up_ref, down_ref, router_ref, sems):
    get_router = pltpu.make_async_copy(router_hbm, router_ref, sems.at[0])
    get_router.start()
    copies = []
    for src, dst in ((up_hbm, up_ref), (down_hbm, down_ref)):
        for e in range(src.shape[0]):
            for r in range(0, src.shape[1], PIECE):
                at = (e, pl.ds(r, PIECE))
                copies.append(pltpu.make_async_copy(src.at[at], dst.at[at], sems.at[1 + len(copies)]))
    for copy in copies:
        copy.start()
    get_router.wait()
    local, lat = router_ref.shape
    wide = jnp.concatenate(
        [router_ref[...].astype(jnp.float32), jnp.zeros((TAIL - local, lat), jnp.float32)], axis=0
    )
    columns_ref[...] = wide.T.astype(jnp.bfloat16)
    for copy in copies:
        copy.wait()


def expert_kernel(count, *refs):
    blocks, refs = refs[: 4 * count], refs[4 * count :]
    (columns_ref, up_ref, down_ref), refs = refs[:3], refs[3:]
    keep_refs, refs = refs[:count], refs[count:]
    send_refs, (packed_ref, inner_ref, result_ref) = refs[: 2 * count], refs[2 * count :]
    rows, wide = blocks[0].shape
    half, lat = 2 * rows, wide - TAIL
    local, eff, _ = down_ref.shape
    slots = packed_ref.shape[1] // count

    def put(i, lanes, value):
        keep_refs[i][:, lanes] = value[:half]
        for j, ref in enumerate(send_refs[2 * i : 2 * i + 2]):
            ref[:, lanes] = value[half + j * rows : half + (j + 1) * rows].astype(jnp.bfloat16)

    def logits_of(values):
        return jnp.dot(values, columns_ref[...], preferred_element_type=jnp.float32)

    size = 2 * half
    row = lax.broadcasted_iota(jnp.int32, (size, size), 0)
    col = lax.broadcasted_iota(jnp.int32, (size, size), 1)
    before = jnp.where(col < row, 1.0, 0.0).astype(jnp.bfloat16)
    after = jnp.where(row < col, 1.0, 0.0).astype(jnp.bfloat16)
    lane = lax.broadcasted_iota(jnp.int32, (size, TAIL), 1)
    line = lax.broadcasted_iota(jnp.int32, (16, size), 0)
    slot = lax.broadcasted_iota(jnp.int32, (size, slots), 1).astype(jnp.float32)
    slot_t = lax.broadcasted_iota(jnp.int32, (slots, size), 0).astype(jnp.float32)
    labels = [(lax.axis_index("exp") * local + e).astype(jnp.float32) for e in range(local)]
    spreads = []
    for i in range(count):
        batch = blocks[4 * i : 4 * i + 4]
        x = jnp.concatenate([ref[:, :lat] for ref in batch], axis=0)
        tail = jnp.concatenate([ref[:, lat:] for ref in batch], axis=0).astype(jnp.float32)
        masks = [jnp.max(jnp.where(tail == label, 1.0, 0.0), axis=1, keepdims=True) for label in labels]
        tail_t = tail.T[:16]
        masks_t = [jnp.max(jnp.where(tail_t == label, 1.0, 0.0), axis=0, keepdims=True) for label in labels]
        marks, marks_t = jnp.zeros((size, TAIL), jnp.float32), jnp.zeros((16, size), jnp.float32)
        for e in range(local):
            marks = jnp.where(lane == e, masks[e], marks)
            marks_t = jnp.where(line == e, masks_t[e], marks_t)
        place_t = jnp.dot(marks_t.astype(jnp.bfloat16), after, preferred_element_type=jnp.float32)
        place = jnp.dot(before, marks.astype(jnp.bfloat16), preferred_element_type=jnp.float32)
        gather = jnp.concatenate(
            [
                jnp.where((slot_t == place_t[e : e + 1]) & (masks_t[e] > 0.0), 1.0, 0.0)
                for e in range(local)
            ],
            axis=0,
        ).astype(jnp.bfloat16)
        packed = jnp.dot(gather, x, preferred_element_type=jnp.float32).astype(jnp.bfloat16)
        spread = jnp.concatenate(
            [jnp.where((slot == place[:, e : e + 1]) & (masks[e] > 0.0), 1.0, 0.0) for e in range(local)],
            axis=1,
        ).astype(jnp.bfloat16)
        logits = logits_of(x)
        sums = jnp.zeros((size, 1), jnp.float32)
        for e in range(local):
            sums = sums + jax.nn.sigmoid(logits[:, e : e + 1]) * (masks[e] * SCALE)
        put(i, slice(lat, wide), jnp.where(lane == 0, sums, 0.0))
        for e in range(local):
            packed_ref[e, i * slots : (i + 1) * slots, :] = packed[e * slots : (e + 1) * slots]
        spreads.append(spread)
    for e in range(local):
        chosen = packed_ref[e]
        score = jax.nn.sigmoid(logits_of(chosen)[:, e : e + 1]) * SCALE
        for c in range(0, eff, STEP):
            gate = jnp.dot(chosen, up_ref[e, :, c : c + STEP], preferred_element_type=jnp.float32)
            up = jnp.dot(chosen, up_ref[e, :, eff + c : eff + c + STEP], preferred_element_type=jnp.float32)
            inner_ref[e, :, c : c + STEP] = (gate / (1.0 + jnp.exp(-gate)) * up * score).astype(jnp.bfloat16)
    for e in range(local):
        result = jnp.dot(inner_ref[e], down_ref[e], preferred_element_type=jnp.float32).astype(jnp.bfloat16)
        for i in range(count):
            result_ref[i, e * slots : (e + 1) * slots, :] = result[i * slots : (i + 1) * slots]
    for i in range(count):
        for c in range(0, lat, STEP):
            part = jnp.dot(spreads[i], result_ref[i, :, c : c + STEP], preferred_element_type=jnp.float32)
            put(i, slice(c, c + STEP), part)


def tie_kernel():
    pass


def fold_kernel(mine_ref, came_a_ref, came_b_ref, keep_ref, send_ref):
    rows = keep_ref.shape[0]
    keep_ref[...] = mine_ref[:rows] + came_a_ref[...].astype(jnp.float32)
    send_ref[...] = (mine_ref[rows:] + came_b_ref[...].astype(jnp.float32)).astype(jnp.bfloat16)


def add_kernel(mine_ref, *refs):
    total = mine_ref[...]
    for ref in refs[:-1]:
        total = total + ref[...].astype(jnp.float32)
    refs[-1][...] = total.astype(jnp.bfloat16)


def total_kernel(*refs):
    total_ref = refs[-1]
    total = refs[0][...]
    for ref in refs[1:-1]:
        total = total + ref[...].astype(jnp.float32)
    total_ref[...] = total


def finish_kernel(*refs):
    out_ref = refs[-1]
    lat = out_ref.shape[1]
    total = refs[0][...]
    for ref in refs[1:-1]:
        total = total + ref[...].astype(jnp.float32)
    out_ref[...] = (total[:, :lat] / total[:, lat : lat + 1]).astype(jnp.bfloat16)


def in_vmem(x):
    return pltpu.with_memory_space_constraint(x, pltpu.VMEM)


def in_hbm(x):
    return pltpu.with_memory_space_constraint(x, pltpu.HBM)


VMEM = pl.BlockSpec(memory_space=pltpu.VMEM)
ANY = pl.BlockSpec(memory_space=pl.ANY)


def call(kernel, outs, args=(), deps=(), chain=(), hbm=(), scratch=()):
    plain = getattr(kernel, "func", kernel)
    reads_chain = plain is expert_kernel
    n_in = len(args) + len(hbm)
    n_skip = n_in + len(deps)
    n_outs = n_skip + len(chain)

    def body(*refs):
        kernel(*refs[:n_in], *refs[n_outs : n_outs + len(outs)], *refs[n_outs + len(outs) + len(chain) :])

    def body_with_chain(*refs):
        kernel(
            *refs[:n_in],
            *refs[n_skip:n_outs],
            *refs[n_outs : n_outs + len(outs)],
            *refs[n_outs + len(outs) + len(chain) :],
        )

    specs = [VMEM] * len(args)
    specs += [ANY] * (len(hbm) + len(deps)) + [VMEM] * len(chain)
    operands = [in_vmem(a) for a in args] + [in_hbm(h) for h in hbm]
    operands += [in_vmem(x) for x in (*deps, *chain)]
    return pl.pallas_call(
        body_with_chain if reads_chain else body,
        out_shape=list(outs) + [pltpu.VMEM(x.shape, x.dtype) for x in chain],
        in_specs=specs,
        out_specs=[VMEM] * (len(outs) + len(chain)),
        scratch_shapes=list(scratch),
        compiler_params=pltpu.CompilerParams(vmem_limit_bytes=SCOPED),
        cost_estimate=pl.CostEstimate(flops=0, bytes_accessed=10_000, transcendentals=0),
        input_output_aliases={n_skip + i: len(outs) + i for i in range(len(chain))},
        name=plain.__name__.removesuffix("_kernel"),
    )(*operands)


def on_device(latent_in, routes, router, gate_up, expert_down):
    n_dev = lax.axis_size("exp")
    local = gate_up.shape[0]
    eff = expert_down.shape[1]
    rows, lat = latent_in.shape
    wide = lat + TAIL

    def swap(x, bits):
        return lax.ppermute(x, "exp", [(i, i ^ bits) for i in range(n_dev)])

    def space(height, dtype):
        return pltpu.VMEM((height, wide), dtype)

    def weights(dep):
        return call(
            load_kernel,
            [
                pltpu.VMEM((lat, TAIL), jnp.bfloat16),
                pltpu.VMEM(gate_up.shape, gate_up.dtype),
                pltpu.VMEM(expert_down.shape, expert_down.dtype),
            ],
            deps=[dep],
            hbm=[router.T, gate_up, expert_down],
            scratch=[
                pltpu.VMEM((local, lat), jnp.bfloat16),
                pltpu.SemaphoreType.DMA((1 + local * (lat + eff) // PIECE,)),
            ],
        )

    bound = 2 * ((rows * routes.shape[1] + local * n_dev - 1) // (local * n_dev))
    slots = 4 * bound

    def group_pass(mine):
        held = weights(mine)

        def step(kernel, outs, args=(), deps=(), hand_on=(), **more):
            nonlocal held
            result = call(kernel, outs, args, deps, [*held, *hand_on], **more)
            held = result[len(outs) : len(outs) + len(held)]
            return result[: len(outs)] + result[len(outs) + len(held) :]

        def tie(x, deps=()):
            return step(tie_kernel, [], deps=deps, hand_on=[x])[0]

        other, keep, send, came, fold_keep, fold_send, y_came = {}, {}, {}, {}, {}, {}, {}

        def gather(k, deps=()):
            other[k] = tie(swap(block[k], 2), deps)

        def compute(*ks):
            count = len(ks)
            blocks = []
            for k in ks:
                near = [block[k], other[k]]
                blocks += near + [swap(one, 1) for one in near]
            result = step(
                functools.partial(expert_kernel, count),
                [space(2 * rows, jnp.float32)] * count + [space(rows, jnp.bfloat16)] * (2 * count),
                blocks,
                scratch=[
                    pltpu.VMEM((local, count * slots, lat), jnp.bfloat16),
                    pltpu.VMEM((local, count * slots, eff), jnp.bfloat16),
                    pltpu.VMEM((count, local * slots, lat), jnp.bfloat16),
                ],
            )
            for i, k in enumerate(ks):
                keep[k] = result[i]
                came[k] = [swap(part, 1) for part in result[count + 2 * i : count + 2 * i + 2]]

        def reduce_core(k, deps=()):
            fold_keep[k], fold_send[k] = step(
                fold_kernel, [space(rows, jnp.float32), space(rows, jnp.bfloat16)], [keep[k], *came[k]], deps
            )
            y_came[k] = swap(fold_send[k], 2)

        def reduce_y(k, *more):
            return step(add_kernel, [space(rows, jnp.bfloat16)], [fold_keep[k], y_came[k], *more])[0]

        z_2, z_1, y_0 = swap(mine, 8), swap(mine, 4), swap(mine, 2)
        block = {0: mine, 2: tie(z_2), 1: z_1}
        block[3] = swap(block[2], 4)
        other[0] = y_0
        gather(2, [block[1], block[3], y_0])
        gather(1)
        compute(2)
        gather(3)
        reduce_core(2)
        compute(3)
        reduce_core(3, [y_came[2]])
        compute(1, 0)
        z_3 = swap(reduce_y(3), 4)
        reduce_core(1)
        reduce_core(0)
        z_2 = swap(reduce_y(2, z_3), 8)
        z_1 = swap(reduce_y(1), 4)
        return fold_keep[0], z_2, z_1, y_came[0]

    packet = call(
        pack_kernel,
        [space(rows, jnp.bfloat16)],
        hbm=[routes.T, latent_in],
        scratch=[pltpu.VMEM(routes.shape[::-1], routes.dtype), pltpu.SemaphoreType.DMA((2,))],
    )[0]

    def finish(parts):
        return pl.pallas_call(
            finish_kernel,
            out_shape=jax.ShapeDtypeStruct((rows, lat), jnp.bfloat16),
            in_specs=[VMEM] * len(parts),
            out_specs=VMEM,
            compiler_params=pltpu.CompilerParams(vmem_limit_bytes=SCOPED),
            name="finish",
        )(*[in_vmem(p) for p in parts])

    if n_dev == GROUP:
        return finish(group_pass(packet))

    def next_group(x):
        return lax.ppermute(x, "exp", [(i, (i + GROUP) % n_dev) for i in range(n_dev)])

    def step(carry, _):
        mine, total = carry
        total = call(total_kernel, [space(rows, jnp.float32)], [total, *group_pass(mine)])[0]
        return (next_group(mine), next_group(total)), None

    start = (packet, jnp.zeros((rows, wide), jnp.float32))
    (_, total), _ = lax.scan(step, start, None, length=n_dev // GROUP)
    return finish([total])


def solution(mesh):
    placed = (
        P(("grp", "exp"), None),
        P(("grp", "exp"), None),
        P(None, "exp"),
        P("exp", None, None),
        P("exp", None, None),
    )
    return jax.shard_map(
        on_device, mesh=mesh, in_specs=placed, out_specs=P(("grp", "exp"), None), check_vma=False
    )
```

```python
import functools

import jax
import jax.numpy as jnp
from jax import lax
from jax.experimental import pallas as pl
from jax.experimental.pallas import tpu as pltpu
from jax.sharding import PartitionSpec as P

GROUP = 16
SCOPED = 8 * 1024 * 1024
TAIL = 128
SCALE = 2.0**40
STEP = 256
PIECE = 256


def pack_kernel(ids_hbm, row_hbm, out_ref, ids_ref, sems):
    rows, lat = row_hbm.shape
    top = ids_hbm.shape[0]
    get_ids = pltpu.make_async_copy(ids_hbm, ids_ref, sems.at[0])
    get_rows = pltpu.make_async_copy(row_hbm, out_ref.at[:, pl.ds(0, lat)], sems.at[1])
    get_ids.start()
    get_rows.start()
    get_ids.wait()
    ids = ids_ref[...].astype(jnp.float32)
    ids = jnp.concatenate([ids, jnp.full((top, TAIL - rows), -1.0, jnp.float32)], axis=1)
    ids = jnp.concatenate([ids, jnp.full((TAIL - top, TAIL), -1.0, jnp.float32)], axis=0)
    out_ref[:, lat:] = ids.T[:rows].astype(jnp.bfloat16)
    get_rows.wait()


def load_kernel(router_hbm, up_hbm, down_hbm, columns_ref, up_ref, down_ref, router_ref, sems):
    get_router = pltpu.make_async_copy(router_hbm, router_ref, sems.at[0])
    get_router.start()
    copies = []
    for src, dst in ((up_hbm, up_ref), (down_hbm, down_ref)):
        for e in range(src.shape[0]):
            for r in range(0, src.shape[1], PIECE):
                at = (e, pl.ds(r, PIECE))
                copies.append(pltpu.make_async_copy(src.at[at], dst.at[at], sems.at[1 + len(copies)]))
    for copy in copies:
        copy.start()
    get_router.wait()
    local, lat = router_ref.shape
    wide = jnp.concatenate(
        [router_ref[...].astype(jnp.float32), jnp.zeros((TAIL - local, lat), jnp.float32)], axis=0
    )
    columns_ref[...] = wide.T.astype(jnp.bfloat16)
    for copy in copies:
        copy.wait()


def expert_kernel(count, *refs):
    blocks, refs = refs[: 4 * count], refs[4 * count :]
    (columns_ref, up_ref, down_ref), refs = refs[:3], refs[3:]
    keep_refs, refs = refs[:count], refs[count:]
    send_refs, (packed_ref, inner_ref, result_ref) = refs[: 2 * count], refs[2 * count :]
    rows, wide = blocks[0].shape
    half, lat = 2 * rows, wide - TAIL
    local, eff, _ = down_ref.shape
    slots = packed_ref.shape[1] // count

    def put(i, lanes, value):
        keep_refs[i][:, lanes] = value[:half]
        for j, ref in enumerate(send_refs[2 * i : 2 * i + 2]):
            ref[:, lanes] = value[half + j * rows : half + (j + 1) * rows].astype(jnp.bfloat16)

    def logits_of(values):
        return jnp.dot(values, columns_ref[...], preferred_element_type=jnp.float32)

    size = 2 * half
    row = lax.broadcasted_iota(jnp.int32, (size, size), 0)
    col = lax.broadcasted_iota(jnp.int32, (size, size), 1)
    before = jnp.where(col < row, 1.0, 0.0).astype(jnp.bfloat16)
    after = jnp.where(row < col, 1.0, 0.0).astype(jnp.bfloat16)
    lane = lax.broadcasted_iota(jnp.int32, (size, TAIL), 1)
    line = lax.broadcasted_iota(jnp.int32, (16, size), 0)
    slot = lax.broadcasted_iota(jnp.int32, (size, slots), 1).astype(jnp.float32)
    slot_t = lax.broadcasted_iota(jnp.int32, (slots, size), 0).astype(jnp.float32)
    labels = [(lax.axis_index("exp") * local + e).astype(jnp.float32) for e in range(local)]
    spreads = []
    for i in range(count):
        batch = blocks[4 * i : 4 * i + 4]
        x = jnp.concatenate([ref[:, :lat] for ref in batch], axis=0)
        tail = jnp.concatenate([ref[:, lat:] for ref in batch], axis=0).astype(jnp.float32)
        masks = [jnp.max(jnp.where(tail == label, 1.0, 0.0), axis=1, keepdims=True) for label in labels]
        tail_t = tail.T[:16]
        masks_t = [jnp.max(jnp.where(tail_t == label, 1.0, 0.0), axis=0, keepdims=True) for label in labels]
        marks, marks_t = jnp.zeros((size, TAIL), jnp.float32), jnp.zeros((16, size), jnp.float32)
        for e in range(local):
            marks = jnp.where(lane == e, masks[e], marks)
            marks_t = jnp.where(line == e, masks_t[e], marks_t)
        place_t = jnp.dot(marks_t.astype(jnp.bfloat16), after, preferred_element_type=jnp.float32)
        place = jnp.dot(before, marks.astype(jnp.bfloat16), preferred_element_type=jnp.float32)
        gather = jnp.concatenate(
            [
                jnp.where((slot_t == place_t[e : e + 1]) & (masks_t[e] > 0.0), 1.0, 0.0)
                for e in range(local)
            ],
            axis=0,
        ).astype(jnp.bfloat16)
        packed = jnp.dot(gather, x, preferred_element_type=jnp.float32).astype(jnp.bfloat16)
        spread = jnp.concatenate(
            [jnp.where((slot == place[:, e : e + 1]) & (masks[e] > 0.0), 1.0, 0.0) for e in range(local)],
            axis=1,
        ).astype(jnp.bfloat16)
        logits = logits_of(x)
        sums = jnp.zeros((size, 1), jnp.float32)
        for e in range(local):
            sums = sums + jax.nn.sigmoid(logits[:, e : e + 1]) * (masks[e] * SCALE)
        put(i, slice(lat, wide), jnp.where(lane == 0, sums, 0.0))
        for e in range(local):
            packed_ref[e, i * slots : (i + 1) * slots, :] = packed[e * slots : (e + 1) * slots]
        spreads.append(spread)
    for e in range(local):
        chosen = packed_ref[e]
        score = jax.nn.sigmoid(logits_of(chosen)[:, e : e + 1]) * SCALE
        for c in range(0, eff, STEP):
            gate = jnp.dot(chosen, up_ref[e, :, c : c + STEP], preferred_element_type=jnp.float32)
            up = jnp.dot(chosen, up_ref[e, :, eff + c : eff + c + STEP], preferred_element_type=jnp.float32)
            inner_ref[e, :, c : c + STEP] = (gate / (1.0 + jnp.exp(-gate)) * up * score).astype(jnp.bfloat16)
    for e in range(local):
        result = jnp.dot(inner_ref[e], down_ref[e], preferred_element_type=jnp.float32).astype(jnp.bfloat16)
        for i in range(count):
            result_ref[i, e * slots : (e + 1) * slots, :] = result[i * slots : (i + 1) * slots]
    for i in range(count):
        for c in range(0, lat, STEP):
            part = jnp.dot(spreads[i], result_ref[i, :, c : c + STEP], preferred_element_type=jnp.float32)
            put(i, slice(c, c + STEP), part)


def tie_kernel():
    pass


def fold_kernel(mine_ref, came_a_ref, came_b_ref, keep_ref, send_ref):
    rows = keep_ref.shape[0]
    keep_ref[...] = mine_ref[:rows] + came_a_ref[...].astype(jnp.float32)
    send_ref[...] = (mine_ref[rows:] + came_b_ref[...].astype(jnp.float32)).astype(jnp.bfloat16)


def add_kernel(mine_ref, *refs):
    total = mine_ref[...]
    for ref in refs[:-1]:
        total = total + ref[...].astype(jnp.float32)
    refs[-1][...] = total.astype(jnp.bfloat16)


def total_kernel(*refs):
    total_ref = refs[-1]
    total = refs[0][...]
    for ref in refs[1:-1]:
        total = total + ref[...].astype(jnp.float32)
    total_ref[...] = total


def finish_kernel(*refs):
    out_ref = refs[-1]
    lat = out_ref.shape[1]
    total = refs[0][...]
    for ref in refs[1:-1]:
        total = total + ref[...].astype(jnp.float32)
    out_ref[...] = (total[:, :lat] / total[:, lat : lat + 1]).astype(jnp.bfloat16)


def in_vmem(x):
    return pltpu.with_memory_space_constraint(x, pltpu.VMEM)


def in_hbm(x):
    return pltpu.with_memory_space_constraint(x, pltpu.HBM)


VMEM = pl.BlockSpec(memory_space=pltpu.VMEM)
ANY = pl.BlockSpec(memory_space=pl.ANY)


def call(kernel, outs, args=(), deps=(), chain=(), hbm=(), scratch=()):
    plain = getattr(kernel, "func", kernel)
    reads_chain = plain is expert_kernel
    n_in = len(args) + len(hbm)
    n_skip = n_in + len(deps)
    n_outs = n_skip + len(chain)

    def body(*refs):
        kernel(*refs[:n_in], *refs[n_outs : n_outs + len(outs)], *refs[n_outs + len(outs) + len(chain) :])

    def body_with_chain(*refs):
        kernel(
            *refs[:n_in],
            *refs[n_skip:n_outs],
            *refs[n_outs : n_outs + len(outs)],
            *refs[n_outs + len(outs) + len(chain) :],
        )

    specs = [VMEM] * len(args)
    specs += [ANY] * (len(hbm) + len(deps)) + [VMEM] * len(chain)
    operands = [in_vmem(a) for a in args] + [in_hbm(h) for h in hbm]
    operands += [in_vmem(x) for x in (*deps, *chain)]
    return pl.pallas_call(
        body_with_chain if reads_chain else body,
        out_shape=list(outs) + [pltpu.VMEM(x.shape, x.dtype) for x in chain],
        in_specs=specs,
        out_specs=[VMEM] * (len(outs) + len(chain)),
        scratch_shapes=list(scratch),
        compiler_params=pltpu.CompilerParams(vmem_limit_bytes=SCOPED),
        cost_estimate=pl.CostEstimate(flops=0, bytes_accessed=10_000, transcendentals=0),
        input_output_aliases={n_skip + i: len(outs) + i for i in range(len(chain))},
        name=plain.__name__.removesuffix("_kernel"),
    )(*operands)


def on_device(latent_in, routes, router, gate_up, expert_down):
    n_dev = lax.axis_size("exp")
    local = gate_up.shape[0]
    eff = expert_down.shape[1]
    rows, lat = latent_in.shape
    wide = lat + TAIL

    def swap(x, bits):
        return lax.ppermute(x, "exp", [(i, i ^ bits) for i in range(n_dev)])

    def space(height, dtype):
        return pltpu.VMEM((height, wide), dtype)

    def weights(dep):
        return call(
            load_kernel,
            [
                pltpu.VMEM((lat, TAIL), jnp.bfloat16),
                pltpu.VMEM(gate_up.shape, gate_up.dtype),
                pltpu.VMEM(expert_down.shape, expert_down.dtype),
            ],
            deps=[dep],
            hbm=[router.T, gate_up, expert_down],
            scratch=[
                pltpu.VMEM((local, lat), jnp.bfloat16),
                pltpu.SemaphoreType.DMA((1 + local * (lat + eff) // PIECE,)),
            ],
        )

    bound = 2 * ((rows * routes.shape[1] + local * n_dev - 1) // (local * n_dev))
    slots = 4 * bound

    def group_pass(mine):
        held = weights(mine)

        def step(kernel, outs, args=(), deps=(), hand_on=(), **more):
            nonlocal held
            result = call(kernel, outs, args, deps, [*held, *hand_on], **more)
            held = result[len(outs) : len(outs) + len(held)]
            return result[: len(outs)] + result[len(outs) + len(held) :]

        def tie(x, deps=()):
            return step(tie_kernel, [], deps=deps, hand_on=[x])[0]

        other, keep, send, came, fold_keep, fold_send, y_came = {}, {}, {}, {}, {}, {}, {}

        def gather(k, deps=()):
            other[k] = tie(swap(block[k], 2), deps)

        def compute(*ks):
            count = len(ks)
            blocks = []
            for k in ks:
                near = [block[k], other[k]]
                blocks += near + [swap(one, 1) for one in near]
            result = step(
                functools.partial(expert_kernel, count),
                [space(2 * rows, jnp.float32)] * count + [space(rows, jnp.bfloat16)] * (2 * count),
                blocks,
                scratch=[
                    pltpu.VMEM((local, count * slots, lat), jnp.bfloat16),
                    pltpu.VMEM((local, count * slots, eff), jnp.bfloat16),
                    pltpu.VMEM((count, local * slots, lat), jnp.bfloat16),
                ],
            )
            for i, k in enumerate(ks):
                keep[k] = result[i]
                came[k] = [swap(part, 1) for part in result[count + 2 * i : count + 2 * i + 2]]

        def reduce_core(k, deps=()):
            fold_keep[k], fold_send[k] = step(
                fold_kernel, [space(rows, jnp.float32), space(rows, jnp.bfloat16)], [keep[k], *came[k]], deps
            )
            y_came[k] = swap(fold_send[k], 2)

        def reduce_y(k, deps=()):
            sums = step(add_kernel, [space(rows, jnp.bfloat16)], [fold_keep[k], y_came[k]], deps)[0]
            return swap(sums, 4 * k)

        z_2, z_1, y_0 = swap(mine, 8), swap(mine, 4), swap(mine, 2)
        block = {0: mine, 2: tie(z_2), 1: z_1}
        block[3] = swap(block[2], 4)
        other[0] = y_0
        gather(2, [block[1], block[3], y_0])
        gather(1)
        compute(2)
        gather(3)
        reduce_core(2)
        compute(3)
        z_2 = reduce_y(2)
        reduce_core(3)
        compute(1, 0)
        z_3 = reduce_y(3, [z_2])
        reduce_core(1)
        z_1 = reduce_y(1)
        reduce_core(0)
        return fold_keep[0], z_3, z_1, y_came[0], z_2

    packet = call(
        pack_kernel,
        [space(rows, jnp.bfloat16)],
        hbm=[routes.T, latent_in],
        scratch=[pltpu.VMEM(routes.shape[::-1], routes.dtype), pltpu.SemaphoreType.DMA((2,))],
    )[0]

    def finish(parts):
        return pl.pallas_call(
            finish_kernel,
            out_shape=jax.ShapeDtypeStruct((rows, lat), jnp.bfloat16),
            in_specs=[VMEM] * len(parts),
            out_specs=VMEM,
            compiler_params=pltpu.CompilerParams(vmem_limit_bytes=SCOPED),
            name="finish",
        )(*[in_vmem(p) for p in parts])

    if n_dev == GROUP:
        return finish(group_pass(packet))

    def next_group(x):
        return lax.ppermute(x, "exp", [(i, (i + GROUP) % n_dev) for i in range(n_dev)])

    def step(carry, _):
        mine, total = carry
        total = call(total_kernel, [space(rows, jnp.float32)], [total, *group_pass(mine)])[0]
        return (next_group(mine), next_group(total)), None

    start = (packet, jnp.zeros((rows, wide), jnp.float32))
    (_, total), _ = lax.scan(step, start, None, length=n_dev // GROUP)
    return finish([total])


def solution(mesh):
    placed = (
        P(("grp", "exp"), None),
        P(("grp", "exp"), None),
        P(None, "exp"),
        P("exp", None, None),
        P("exp", None, None),
    )
    return jax.shard_map(
        on_device, mesh=mesh, in_specs=placed, out_specs=P(("grp", "exp"), None), check_vma=False
    )
```

```python
import functools

import jax
import jax.numpy as jnp
from jax import lax
from jax.experimental import pallas as pl
from jax.experimental.pallas import tpu as pltpu
from jax.sharding import PartitionSpec as P

GROUP = 16
SCOPED = 8 * 1024 * 1024
TAIL = 128
SCALE = 2.0**40
STEP = 256
PIECE = 256


def pack_kernel(ids_hbm, row_hbm, out_ref, ids_ref, sems):
    rows, lat = row_hbm.shape
    top = ids_hbm.shape[0]
    get_ids = pltpu.make_async_copy(ids_hbm, ids_ref, sems.at[0])
    get_rows = pltpu.make_async_copy(row_hbm, out_ref.at[:, pl.ds(0, lat)], sems.at[1])
    get_ids.start()
    get_rows.start()
    get_ids.wait()
    ids = ids_ref[...].astype(jnp.float32)
    ids = jnp.concatenate([ids, jnp.full((top, TAIL - rows), -1.0, jnp.float32)], axis=1)
    ids = jnp.concatenate([ids, jnp.full((TAIL - top, TAIL), -1.0, jnp.float32)], axis=0)
    out_ref[:, lat:] = ids.T[:rows].astype(jnp.bfloat16)
    get_rows.wait()


def load_kernel(router_hbm, up_hbm, down_hbm, columns_ref, up_ref, down_ref, router_ref, sems):
    get_router = pltpu.make_async_copy(router_hbm, router_ref, sems.at[0])
    get_router.start()
    copies = []
    for src, dst in ((up_hbm, up_ref), (down_hbm, down_ref)):
        for e in range(src.shape[0]):
            for r in range(0, src.shape[1], PIECE):
                at = (e, pl.ds(r, PIECE))
                copies.append(pltpu.make_async_copy(src.at[at], dst.at[at], sems.at[1 + len(copies)]))
    for copy in copies:
        copy.start()
    get_router.wait()
    local, lat = router_ref.shape
    wide = jnp.concatenate(
        [router_ref[...].astype(jnp.float32), jnp.zeros((TAIL - local, lat), jnp.float32)], axis=0
    )
    columns_ref[...] = wide.T.astype(jnp.bfloat16)
    for copy in copies:
        copy.wait()


def expert_kernel(count, *refs):
    blocks, refs = refs[: 4 * count], refs[4 * count :]
    (columns_ref, up_ref, down_ref), refs = refs[:3], refs[3:]
    keep_refs, refs = refs[:count], refs[count:]
    send_refs, (packed_ref, inner_ref, result_ref) = refs[: 2 * count], refs[2 * count :]
    rows, wide = blocks[0].shape
    half, lat = 2 * rows, wide - TAIL
    local, eff, _ = down_ref.shape
    slots = packed_ref.shape[1] // count

    def put(i, lanes, value):
        keep_refs[i][:, lanes] = value[:half]
        for j, ref in enumerate(send_refs[2 * i : 2 * i + 2]):
            ref[:, lanes] = value[half + j * rows : half + (j + 1) * rows].astype(jnp.bfloat16)

    def logits_of(values):
        return jnp.dot(values, columns_ref[...], preferred_element_type=jnp.float32)

    size = 2 * half
    row = lax.broadcasted_iota(jnp.int32, (size, size), 0)
    col = lax.broadcasted_iota(jnp.int32, (size, size), 1)
    before = jnp.where(col < row, 1.0, 0.0).astype(jnp.bfloat16)
    after = jnp.where(row < col, 1.0, 0.0).astype(jnp.bfloat16)
    lane = lax.broadcasted_iota(jnp.int32, (size, TAIL), 1)
    line = lax.broadcasted_iota(jnp.int32, (16, size), 0)
    slot = lax.broadcasted_iota(jnp.int32, (size, slots), 1).astype(jnp.float32)
    slot_t = lax.broadcasted_iota(jnp.int32, (slots, size), 0).astype(jnp.float32)
    labels = [(lax.axis_index("exp") * local + e).astype(jnp.float32) for e in range(local)]
    spreads = []
    for i in range(count):
        batch = blocks[4 * i : 4 * i + 4]
        x = jnp.concatenate([ref[:, :lat] for ref in batch], axis=0)
        tail = jnp.concatenate([ref[:, lat:] for ref in batch], axis=0).astype(jnp.float32)
        masks = [jnp.max(jnp.where(tail == label, 1.0, 0.0), axis=1, keepdims=True) for label in labels]
        tail_t = tail.T[:16]
        masks_t = [jnp.max(jnp.where(tail_t == label, 1.0, 0.0), axis=0, keepdims=True) for label in labels]
        marks, marks_t = jnp.zeros((size, TAIL), jnp.float32), jnp.zeros((16, size), jnp.float32)
        for e in range(local):
            marks = jnp.where(lane == e, masks[e], marks)
            marks_t = jnp.where(line == e, masks_t[e], marks_t)
        place_t = jnp.dot(marks_t.astype(jnp.bfloat16), after, preferred_element_type=jnp.float32)
        place = jnp.dot(before, marks.astype(jnp.bfloat16), preferred_element_type=jnp.float32)
        gather = jnp.concatenate(
            [
                jnp.where((slot_t == place_t[e : e + 1]) & (masks_t[e] > 0.0), 1.0, 0.0)
                for e in range(local)
            ],
            axis=0,
        ).astype(jnp.bfloat16)
        packed = jnp.dot(gather, x, preferred_element_type=jnp.float32).astype(jnp.bfloat16)
        spread = jnp.concatenate(
            [jnp.where((slot == place[:, e : e + 1]) & (masks[e] > 0.0), 1.0, 0.0) for e in range(local)],
            axis=1,
        ).astype(jnp.bfloat16)
        logits = logits_of(x)
        sums = jnp.zeros((size, 1), jnp.float32)
        for e in range(local):
            sums = sums + jax.nn.sigmoid(logits[:, e : e + 1]) * (masks[e] * SCALE)
        put(i, slice(lat, wide), jnp.where(lane == 0, sums, 0.0))
        for e in range(local):
            packed_ref[e, i * slots : (i + 1) * slots, :] = packed[e * slots : (e + 1) * slots]
        spreads.append(spread)
    for e in range(local):
        chosen = packed_ref[e]
        score = jax.nn.sigmoid(logits_of(chosen)[:, e : e + 1]) * SCALE
        for c in range(0, eff, STEP):
            gate = jnp.dot(chosen, up_ref[e, :, c : c + STEP], preferred_element_type=jnp.float32)
            up = jnp.dot(chosen, up_ref[e, :, eff + c : eff + c + STEP], preferred_element_type=jnp.float32)
            inner_ref[e, :, c : c + STEP] = (gate / (1.0 + jnp.exp(-gate)) * up * score).astype(jnp.bfloat16)
    for e in range(local):
        result = jnp.dot(inner_ref[e], down_ref[e], preferred_element_type=jnp.float32).astype(jnp.bfloat16)
        for i in range(count):
            result_ref[i, e * slots : (e + 1) * slots, :] = result[i * slots : (i + 1) * slots]
    for i in range(count):
        for c in range(0, lat, STEP):
            part = jnp.dot(spreads[i], result_ref[i, :, c : c + STEP], preferred_element_type=jnp.float32)
            put(i, slice(c, c + STEP), part)


def tie_kernel():
    pass


def fold_kernel(mine_ref, came_a_ref, came_b_ref, keep_ref, send_ref):
    rows = keep_ref.shape[0]
    keep_ref[...] = mine_ref[:rows] + came_a_ref[...].astype(jnp.float32)
    send_ref[...] = (mine_ref[rows:] + came_b_ref[...].astype(jnp.float32)).astype(jnp.bfloat16)


def add_kernel(mine_ref, *refs):
    total = mine_ref[...]
    for ref in refs[:-1]:
        total = total + ref[...].astype(jnp.float32)
    refs[-1][...] = total.astype(jnp.bfloat16)


def total_kernel(*refs):
    total_ref = refs[-1]
    total = refs[0][...]
    for ref in refs[1:-1]:
        total = total + ref[...].astype(jnp.float32)
    total_ref[...] = total


def finish_kernel(*refs):
    out_ref = refs[-1]
    lat = out_ref.shape[1]
    total = refs[0][...]
    for ref in refs[1:-1]:
        total = total + ref[...].astype(jnp.float32)
    out_ref[...] = (total[:, :lat] / total[:, lat : lat + 1]).astype(jnp.bfloat16)


def in_vmem(x):
    return pltpu.with_memory_space_constraint(x, pltpu.VMEM)


def in_hbm(x):
    return pltpu.with_memory_space_constraint(x, pltpu.HBM)


VMEM = pl.BlockSpec(memory_space=pltpu.VMEM)
ANY = pl.BlockSpec(memory_space=pl.ANY)


def call(kernel, outs, args=(), deps=(), chain=(), hbm=(), scratch=()):
    plain = getattr(kernel, "func", kernel)
    reads_chain = plain is expert_kernel
    n_in = len(args) + len(hbm)
    n_skip = n_in + len(deps)
    n_outs = n_skip + len(chain)

    def body(*refs):
        kernel(*refs[:n_in], *refs[n_outs : n_outs + len(outs)], *refs[n_outs + len(outs) + len(chain) :])

    def body_with_chain(*refs):
        kernel(
            *refs[:n_in],
            *refs[n_skip:n_outs],
            *refs[n_outs : n_outs + len(outs)],
            *refs[n_outs + len(outs) + len(chain) :],
        )

    specs = [VMEM] * len(args)
    specs += [ANY] * (len(hbm) + len(deps)) + [VMEM] * len(chain)
    operands = [in_vmem(a) for a in args] + [in_hbm(h) for h in hbm]
    operands += [in_vmem(x) for x in (*deps, *chain)]
    return pl.pallas_call(
        body_with_chain if reads_chain else body,
        out_shape=list(outs) + [pltpu.VMEM(x.shape, x.dtype) for x in chain],
        in_specs=specs,
        out_specs=[VMEM] * (len(outs) + len(chain)),
        scratch_shapes=list(scratch),
        compiler_params=pltpu.CompilerParams(vmem_limit_bytes=SCOPED),
        cost_estimate=pl.CostEstimate(flops=0, bytes_accessed=10_000, transcendentals=0),
        input_output_aliases={n_skip + i: len(outs) + i for i in range(len(chain))},
        name=plain.__name__.removesuffix("_kernel"),
    )(*operands)


def on_device(latent_in, routes, router, gate_up, expert_down):
    n_dev = lax.axis_size("exp")
    local = gate_up.shape[0]
    eff = expert_down.shape[1]
    rows, lat = latent_in.shape
    wide = lat + TAIL

    def swap(x, bits):
        return lax.ppermute(x, "exp", [(i, i ^ bits) for i in range(n_dev)])

    def space(height, dtype):
        return pltpu.VMEM((height, wide), dtype)

    def weights(dep):
        return call(
            load_kernel,
            [
                pltpu.VMEM((lat, TAIL), jnp.bfloat16),
                pltpu.VMEM(gate_up.shape, gate_up.dtype),
                pltpu.VMEM(expert_down.shape, expert_down.dtype),
            ],
            deps=[dep],
            hbm=[router.T, gate_up, expert_down],
            scratch=[
                pltpu.VMEM((local, lat), jnp.bfloat16),
                pltpu.SemaphoreType.DMA((1 + local * (lat + eff) // PIECE,)),
            ],
        )

    bound = 2 * ((rows * routes.shape[1] + local * n_dev - 1) // (local * n_dev))
    slots = 4 * bound

    def group_pass(mine):
        held = weights(mine)

        def step(kernel, outs, args=(), deps=(), hand_on=(), **more):
            nonlocal held
            result = call(kernel, outs, args, deps, [*held, *hand_on], **more)
            held = result[len(outs) : len(outs) + len(held)]
            return result[: len(outs)] + result[len(outs) + len(held) :]

        def tie(x, deps=()):
            return step(tie_kernel, [], deps=deps, hand_on=[x])[0]

        other, keep, send, came, fold_keep, fold_send, y_came = {}, {}, {}, {}, {}, {}, {}

        def gather(k, deps=()):
            other[k] = tie(swap(block[k], 2), deps)

        def compute(*ks):
            count = len(ks)
            blocks = []
            for k in ks:
                near = [block[k], other[k]]
                blocks += near + [swap(one, 1) for one in near]
            result = step(
                functools.partial(expert_kernel, count),
                [space(2 * rows, jnp.float32)] * count + [space(rows, jnp.bfloat16)] * (2 * count),
                blocks,
                scratch=[
                    pltpu.VMEM((local, count * slots, lat), jnp.bfloat16),
                    pltpu.VMEM((local, count * slots, eff), jnp.bfloat16),
                    pltpu.VMEM((count, local * slots, lat), jnp.bfloat16),
                ],
            )
            for i, k in enumerate(ks):
                keep[k] = result[i]
                came[k] = [swap(part, 1) for part in result[count + 2 * i : count + 2 * i + 2]]

        def reduce_core(k, deps=()):
            fold_keep[k], fold_send[k] = step(
                fold_kernel, [space(rows, jnp.float32), space(rows, jnp.bfloat16)], [keep[k], *came[k]], deps
            )
            y_came[k] = swap(fold_send[k], 2)

        def reduce_y(k, deps=()):
            sums = step(add_kernel, [space(rows, jnp.bfloat16)], [fold_keep[k], y_came[k]], deps)[0]
            return swap(sums, 4 * k)

        z_2, z_1, y_0 = swap(mine, 8), swap(mine, 4), swap(mine, 2)
        block = {0: mine, 2: tie(z_2), 1: z_1}
        block[3] = swap(block[2], 4)
        other[0] = tie(y_0)
        compute(0)
        gather(2, [block[1], block[3]])
        gather(1)
        reduce_core(0)
        compute(2)
        gather(3)
        reduce_core(2)
        compute(3, 1)
        z_2 = reduce_y(2, [y_came[0]])
        reduce_core(3)
        reduce_core(1)
        z_3 = reduce_y(3, [z_2])
        z_1 = reduce_y(1)
        return fold_keep[0], y_came[0], z_2, z_3, z_1

    packet = call(
        pack_kernel,
        [space(rows, jnp.bfloat16)],
        hbm=[routes.T, latent_in],
        scratch=[pltpu.VMEM(routes.shape[::-1], routes.dtype), pltpu.SemaphoreType.DMA((2,))],
    )[0]

    def finish(parts):
        return pl.pallas_call(
            finish_kernel,
            out_shape=jax.ShapeDtypeStruct((rows, lat), jnp.bfloat16),
            in_specs=[VMEM] * len(parts),
            out_specs=VMEM,
            compiler_params=pltpu.CompilerParams(vmem_limit_bytes=SCOPED),
            name="finish",
        )(*[in_vmem(p) for p in parts])

    if n_dev == GROUP:
        return finish(group_pass(packet))

    def next_group(x):
        return lax.ppermute(x, "exp", [(i, (i + GROUP) % n_dev) for i in range(n_dev)])

    def step(carry, _):
        mine, total = carry
        total = call(total_kernel, [space(rows, jnp.float32)], [total, *group_pass(mine)])[0]
        return (next_group(mine), next_group(total)), None

    start = (packet, jnp.zeros((rows, wide), jnp.float32))
    (_, total), _ = lax.scan(step, start, None, length=n_dev // GROUP)
    return finish([total])


def solution(mesh):
    placed = (
        P(("grp", "exp"), None),
        P(("grp", "exp"), None),
        P(None, "exp"),
        P("exp", None, None),
        P("exp", None, None),
    )
    return jax.shard_map(
        on_device, mesh=mesh, in_specs=placed, out_specs=P(("grp", "exp"), None), check_vma=False
    )
```

```python
import functools

import jax
import jax.numpy as jnp
from jax import lax
from jax.experimental import pallas as pl
from jax.experimental.pallas import tpu as pltpu
from jax.sharding import PartitionSpec as P

GROUP = 16
SCOPED = 8 * 1024 * 1024
TAIL = 128
SCALE = 2.0**40
STEP = 256
PIECE = 256


def pack_kernel(ids_hbm, row_hbm, out_ref, ids_ref, sems):
    rows, lat = row_hbm.shape
    top = ids_hbm.shape[0]
    get_ids = pltpu.make_async_copy(ids_hbm, ids_ref, sems.at[0])
    get_rows = pltpu.make_async_copy(row_hbm, out_ref.at[:, pl.ds(0, lat)], sems.at[1])
    get_ids.start()
    get_rows.start()
    get_ids.wait()
    ids = ids_ref[...].astype(jnp.float32)
    ids = jnp.concatenate([ids, jnp.full((top, TAIL - rows), -1.0, jnp.float32)], axis=1)
    ids = jnp.concatenate([ids, jnp.full((TAIL - top, TAIL), -1.0, jnp.float32)], axis=0)
    out_ref[:, lat:] = ids.T[:rows].astype(jnp.bfloat16)
    get_rows.wait()


def load_kernel(router_hbm, up_hbm, down_hbm, columns_ref, up_ref, down_ref, router_ref, sems):
    get_router = pltpu.make_async_copy(router_hbm, router_ref, sems.at[0])
    get_router.start()
    copies = []
    for src, dst in ((up_hbm, up_ref), (down_hbm, down_ref)):
        for e in range(src.shape[0]):
            for r in range(0, src.shape[1], PIECE):
                at = (e, pl.ds(r, PIECE))
                copies.append(pltpu.make_async_copy(src.at[at], dst.at[at], sems.at[1 + len(copies)]))
    for copy in copies:
        copy.start()
    get_router.wait()
    local, lat = router_ref.shape
    wide = jnp.concatenate(
        [router_ref[...].astype(jnp.float32), jnp.zeros((TAIL - local, lat), jnp.float32)], axis=0
    )
    columns_ref[...] = wide.T.astype(jnp.bfloat16)
    for copy in copies:
        copy.wait()


def expert_kernel(count, *refs):
    blocks, refs = refs[: 4 * count], refs[4 * count :]
    (columns_ref, up_ref, down_ref), refs = refs[:3], refs[3:]
    keep_refs, refs = refs[:count], refs[count:]
    send_refs, (packed_ref, inner_ref, result_ref) = refs[: 2 * count], refs[2 * count :]
    rows, wide = blocks[0].shape
    half, lat = 2 * rows, wide - TAIL
    local, eff, _ = down_ref.shape
    slots = packed_ref.shape[1] // count

    def put(i, lanes, value):
        keep_refs[i][:, lanes] = value[:half]
        for j, ref in enumerate(send_refs[2 * i : 2 * i + 2]):
            ref[:, lanes] = value[half + j * rows : half + (j + 1) * rows].astype(jnp.bfloat16)

    def logits_of(values):
        return jnp.dot(values, columns_ref[...], preferred_element_type=jnp.float32)

    size = 2 * half
    row = lax.broadcasted_iota(jnp.int32, (size, size), 0)
    col = lax.broadcasted_iota(jnp.int32, (size, size), 1)
    before = jnp.where(col < row, 1.0, 0.0).astype(jnp.bfloat16)
    after = jnp.where(row < col, 1.0, 0.0).astype(jnp.bfloat16)
    lane = lax.broadcasted_iota(jnp.int32, (size, TAIL), 1)
    line = lax.broadcasted_iota(jnp.int32, (16, size), 0)
    slot = lax.broadcasted_iota(jnp.int32, (size, slots), 1).astype(jnp.float32)
    slot_t = lax.broadcasted_iota(jnp.int32, (slots, size), 0).astype(jnp.float32)
    labels = [(lax.axis_index("exp") * local + e).astype(jnp.float32) for e in range(local)]
    spreads = []
    for i in range(count):
        batch = blocks[4 * i : 4 * i + 4]
        x = jnp.concatenate([ref[:, :lat] for ref in batch], axis=0)
        tail = jnp.concatenate([ref[:, lat:] for ref in batch], axis=0).astype(jnp.float32)
        masks = [jnp.max(jnp.where(tail == label, 1.0, 0.0), axis=1, keepdims=True) for label in labels]
        tail_t = tail.T[:16]
        masks_t = [jnp.max(jnp.where(tail_t == label, 1.0, 0.0), axis=0, keepdims=True) for label in labels]
        marks, marks_t = jnp.zeros((size, TAIL), jnp.float32), jnp.zeros((16, size), jnp.float32)
        for e in range(local):
            marks = jnp.where(lane == e, masks[e], marks)
            marks_t = jnp.where(line == e, masks_t[e], marks_t)
        place_t = jnp.dot(marks_t.astype(jnp.bfloat16), after, preferred_element_type=jnp.float32)
        place = jnp.dot(before, marks.astype(jnp.bfloat16), preferred_element_type=jnp.float32)
        gather = jnp.concatenate(
            [
                jnp.where((slot_t == place_t[e : e + 1]) & (masks_t[e] > 0.0), 1.0, 0.0)
                for e in range(local)
            ],
            axis=0,
        ).astype(jnp.bfloat16)
        packed = jnp.dot(gather, x, preferred_element_type=jnp.float32).astype(jnp.bfloat16)
        spread = jnp.concatenate(
            [jnp.where((slot == place[:, e : e + 1]) & (masks[e] > 0.0), 1.0, 0.0) for e in range(local)],
            axis=1,
        ).astype(jnp.bfloat16)
        logits = logits_of(x)
        sums = jnp.zeros((size, 1), jnp.float32)
        for e in range(local):
            sums = sums + jax.nn.sigmoid(logits[:, e : e + 1]) * (masks[e] * SCALE)
        put(i, slice(lat, wide), jnp.where(lane == 0, sums, 0.0))
        for e in range(local):
            packed_ref[e, i * slots : (i + 1) * slots, :] = packed[e * slots : (e + 1) * slots]
        spreads.append(spread)
    for e in range(local):
        chosen = packed_ref[e]
        score = jax.nn.sigmoid(logits_of(chosen)[:, e : e + 1]) * SCALE
        for c in range(0, eff, STEP):
            gate = jnp.dot(chosen, up_ref[e, :, c : c + STEP], preferred_element_type=jnp.float32)
            up = jnp.dot(chosen, up_ref[e, :, eff + c : eff + c + STEP], preferred_element_type=jnp.float32)
            inner_ref[e, :, c : c + STEP] = (gate / (1.0 + jnp.exp(-gate)) * up * score).astype(jnp.bfloat16)
    for e in range(local):
        result = jnp.dot(inner_ref[e], down_ref[e], preferred_element_type=jnp.float32).astype(jnp.bfloat16)
        for i in range(count):
            result_ref[i, e * slots : (e + 1) * slots, :] = result[i * slots : (i + 1) * slots]
    for i in range(count):
        for c in range(0, lat, STEP):
            part = jnp.dot(spreads[i], result_ref[i, :, c : c + STEP], preferred_element_type=jnp.float32)
            put(i, slice(c, c + STEP), part)


def tie_kernel():
    pass


def fold_kernel(mine_ref, came_a_ref, came_b_ref, keep_ref, send_ref):
    rows = keep_ref.shape[0]
    keep_ref[...] = mine_ref[:rows] + came_a_ref[...].astype(jnp.float32)
    send_ref[...] = (mine_ref[rows:] + came_b_ref[...].astype(jnp.float32)).astype(jnp.bfloat16)


def add_kernel(mine_ref, *refs):
    total = mine_ref[...]
    for ref in refs[:-1]:
        total = total + ref[...].astype(jnp.float32)
    refs[-1][...] = total.astype(jnp.bfloat16)


def total_kernel(*refs):
    total_ref = refs[-1]
    total = refs[0][...]
    for ref in refs[1:-1]:
        total = total + ref[...].astype(jnp.float32)
    total_ref[...] = total


def finish_kernel(*refs):
    out_ref = refs[-1]
    lat = out_ref.shape[1]
    total = refs[0][...]
    for ref in refs[1:-1]:
        total = total + ref[...].astype(jnp.float32)
    out_ref[...] = (total[:, :lat] / total[:, lat : lat + 1]).astype(jnp.bfloat16)


def in_vmem(x):
    return pltpu.with_memory_space_constraint(x, pltpu.VMEM)


def in_hbm(x):
    return pltpu.with_memory_space_constraint(x, pltpu.HBM)


VMEM = pl.BlockSpec(memory_space=pltpu.VMEM)
ANY = pl.BlockSpec(memory_space=pl.ANY)


def call(kernel, outs, args=(), deps=(), chain=(), hbm=(), scratch=()):
    plain = getattr(kernel, "func", kernel)
    reads_chain = plain is expert_kernel
    n_in = len(args) + len(hbm)
    n_skip = n_in + len(deps)
    n_outs = n_skip + len(chain)

    def body(*refs):
        kernel(*refs[:n_in], *refs[n_outs : n_outs + len(outs)], *refs[n_outs + len(outs) + len(chain) :])

    def body_with_chain(*refs):
        kernel(
            *refs[:n_in],
            *refs[n_skip:n_outs],
            *refs[n_outs : n_outs + len(outs)],
            *refs[n_outs + len(outs) + len(chain) :],
        )

    specs = [VMEM] * len(args)
    specs += [ANY] * (len(hbm) + len(deps)) + [VMEM] * len(chain)
    operands = [in_vmem(a) for a in args] + [in_hbm(h) for h in hbm]
    operands += [in_vmem(x) for x in (*deps, *chain)]
    return pl.pallas_call(
        body_with_chain if reads_chain else body,
        out_shape=list(outs) + [pltpu.VMEM(x.shape, x.dtype) for x in chain],
        in_specs=specs,
        out_specs=[VMEM] * (len(outs) + len(chain)),
        scratch_shapes=list(scratch),
        compiler_params=pltpu.CompilerParams(vmem_limit_bytes=SCOPED),
        cost_estimate=pl.CostEstimate(flops=0, bytes_accessed=10_000, transcendentals=0),
        input_output_aliases={n_skip + i: len(outs) + i for i in range(len(chain))},
        name=plain.__name__.removesuffix("_kernel"),
    )(*operands)


def on_device(latent_in, routes, router, gate_up, expert_down):
    n_dev = lax.axis_size("exp")
    local = gate_up.shape[0]
    eff = expert_down.shape[1]
    rows, lat = latent_in.shape
    wide = lat + TAIL

    def swap(x, bits):
        return lax.ppermute(x, "exp", [(i, i ^ bits) for i in range(n_dev)])

    def space(height, dtype):
        return pltpu.VMEM((height, wide), dtype)

    def weights(dep):
        return call(
            load_kernel,
            [
                pltpu.VMEM((lat, TAIL), jnp.bfloat16),
                pltpu.VMEM(gate_up.shape, gate_up.dtype),
                pltpu.VMEM(expert_down.shape, expert_down.dtype),
            ],
            deps=[dep],
            hbm=[router.T, gate_up, expert_down],
            scratch=[
                pltpu.VMEM((local, lat), jnp.bfloat16),
                pltpu.SemaphoreType.DMA((1 + local * (lat + eff) // PIECE,)),
            ],
        )

    bound = 2 * ((rows * routes.shape[1] + local * n_dev - 1) // (local * n_dev))
    slots = 4 * bound

    def group_pass(mine):
        held = weights(mine)

        def step(kernel, outs, args=(), deps=(), hand_on=(), **more):
            nonlocal held
            result = call(kernel, outs, args, deps, [*held, *hand_on], **more)
            held = result[len(outs) : len(outs) + len(held)]
            return result[: len(outs)] + result[len(outs) + len(held) :]

        def tie(x, deps=()):
            return step(tie_kernel, [], deps=deps, hand_on=[x])[0]

        other, keep, send, came, fold_keep, fold_send, y_came = {}, {}, {}, {}, {}, {}, {}

        def gather(k, deps=()):
            other[k] = tie(swap(block[k], 2), deps)

        def compute(*ks):
            count = len(ks)
            blocks = []
            for k in ks:
                near = [block[k], other[k]]
                blocks += near + [swap(one, 1) for one in near]
            result = step(
                functools.partial(expert_kernel, count),
                [space(2 * rows, jnp.float32)] * count + [space(rows, jnp.bfloat16)] * (2 * count),
                blocks,
                scratch=[
                    pltpu.VMEM((local, count * slots, lat), jnp.bfloat16),
                    pltpu.VMEM((local, count * slots, eff), jnp.bfloat16),
                    pltpu.VMEM((count, local * slots, lat), jnp.bfloat16),
                ],
            )
            for i, k in enumerate(ks):
                keep[k] = result[i]
                came[k] = [swap(part, 1) for part in result[count + 2 * i : count + 2 * i + 2]]

        def reduce_core(k, deps=()):
            fold_keep[k], fold_send[k] = step(
                fold_kernel, [space(rows, jnp.float32), space(rows, jnp.bfloat16)], [keep[k], *came[k]], deps
            )
            y_came[k] = swap(fold_send[k], 2)

        def reduce_y(k, deps=()):
            sums = step(add_kernel, [space(rows, jnp.bfloat16)], [fold_keep[k], y_came[k]], deps)[0]
            return swap(sums, 4 * k)

        z_2, z_1, y_0 = swap(mine, 8), swap(mine, 4), swap(mine, 2)
        block = {0: mine, 2: tie(z_2, [z_1]), 1: z_1}
        block[3] = swap(block[2], 4)
        other[0] = tie(y_0)
        compute(0)
        gather(2, [block[1], block[3]])
        reduce_core(0)
        compute(2)
        gather(1)
        gather(3)
        reduce_core(2)
        compute(3, 1)
        z_2 = reduce_y(2)
        reduce_core(3, [y_came[0]])
        reduce_core(1)
        z_3 = reduce_y(3)
        z_1 = reduce_y(1, [z_2])
        return fold_keep[0], y_came[0], z_2, z_3, z_1

    packet = call(
        pack_kernel,
        [space(rows, jnp.bfloat16)],
        hbm=[routes.T, latent_in],
        scratch=[pltpu.VMEM(routes.shape[::-1], routes.dtype), pltpu.SemaphoreType.DMA((2,))],
    )[0]

    def finish(parts):
        return pl.pallas_call(
            finish_kernel,
            out_shape=jax.ShapeDtypeStruct((rows, lat), jnp.bfloat16),
            in_specs=[VMEM] * len(parts),
            out_specs=VMEM,
            compiler_params=pltpu.CompilerParams(vmem_limit_bytes=SCOPED),
            name="finish",
        )(*[in_vmem(p) for p in parts])

    if n_dev == GROUP:
        return finish(group_pass(packet))

    def next_group(x):
        return lax.ppermute(x, "exp", [(i, (i + GROUP) % n_dev) for i in range(n_dev)])

    def step(carry, _):
        mine, total = carry
        total = call(total_kernel, [space(rows, jnp.float32)], [total, *group_pass(mine)])[0]
        return (next_group(mine), next_group(total)), None

    start = (packet, jnp.zeros((rows, wide), jnp.float32))
    (_, total), _ = lax.scan(step, start, None, length=n_dev // GROUP)
    return finish([total])


def solution(mesh):
    placed = (
        P(("grp", "exp"), None),
        P(("grp", "exp"), None),
        P(None, "exp"),
        P("exp", None, None),
        P("exp", None, None),
    )
    return jax.shard_map(
        on_device, mesh=mesh, in_specs=placed, out_specs=P(("grp", "exp"), None), check_vma=False
    )
```

```python
import functools

import jax
import jax.numpy as jnp
from jax import lax
from jax.experimental import pallas as pl
from jax.experimental.pallas import tpu as pltpu
from jax.sharding import PartitionSpec as P

GROUP = 16
SCOPED = 8 * 1024 * 1024
TAIL = 128
SCALE = 2.0**40
STEP = 256
PIECE = 256


def pack_kernel(ids_hbm, row_hbm, out_ref, ids_ref, sems):
    rows, lat = row_hbm.shape
    top = ids_hbm.shape[0]
    get_ids = pltpu.make_async_copy(ids_hbm, ids_ref, sems.at[0])
    get_rows = pltpu.make_async_copy(row_hbm, out_ref.at[:, pl.ds(0, lat)], sems.at[1])
    get_ids.start()
    get_rows.start()
    get_ids.wait()
    ids = ids_ref[...].astype(jnp.float32)
    ids = jnp.concatenate([ids, jnp.full((top, TAIL - rows), -1.0, jnp.float32)], axis=1)
    ids = jnp.concatenate([ids, jnp.full((TAIL - top, TAIL), -1.0, jnp.float32)], axis=0)
    out_ref[:, lat:] = ids.T[:rows].astype(jnp.bfloat16)
    get_rows.wait()


def load_kernel(router_hbm, up_hbm, down_hbm, columns_ref, up_ref, down_ref, router_ref, sems):
    get_router = pltpu.make_async_copy(router_hbm, router_ref, sems.at[0])
    get_router.start()
    copies = []
    for src, dst in ((up_hbm, up_ref), (down_hbm, down_ref)):
        for e in range(src.shape[0]):
            for r in range(0, src.shape[1], PIECE):
                at = (e, pl.ds(r, PIECE))
                copies.append(pltpu.make_async_copy(src.at[at], dst.at[at], sems.at[1 + len(copies)]))
    for copy in copies:
        copy.start()
    get_router.wait()
    local, lat = router_ref.shape
    wide = jnp.concatenate(
        [router_ref[...].astype(jnp.float32), jnp.zeros((TAIL - local, lat), jnp.float32)], axis=0
    )
    columns_ref[...] = wide.T.astype(jnp.bfloat16)
    for copy in copies:
        copy.wait()


def expert_kernel(count, *refs):
    blocks, refs = refs[: 4 * count], refs[4 * count :]
    (columns_ref, up_ref, down_ref), refs = refs[:3], refs[3:]
    keep_refs, refs = refs[:count], refs[count:]
    send_refs, (packed_ref, inner_ref, result_ref) = refs[: 2 * count], refs[2 * count :]
    rows, wide = blocks[0].shape
    half, lat = 2 * rows, wide - TAIL
    local, eff, _ = down_ref.shape
    slots = packed_ref.shape[1] // count

    def put(i, lanes, value):
        keep_refs[i][:, lanes] = value[:half]
        for j, ref in enumerate(send_refs[2 * i : 2 * i + 2]):
            ref[:, lanes] = value[half + j * rows : half + (j + 1) * rows].astype(jnp.bfloat16)

    def logits_of(values):
        return jnp.dot(values, columns_ref[...], preferred_element_type=jnp.float32)

    size = 2 * half
    row = lax.broadcasted_iota(jnp.int32, (size, size), 0)
    col = lax.broadcasted_iota(jnp.int32, (size, size), 1)
    before = jnp.where(col < row, 1.0, 0.0).astype(jnp.bfloat16)
    after = jnp.where(row < col, 1.0, 0.0).astype(jnp.bfloat16)
    lane = lax.broadcasted_iota(jnp.int32, (size, TAIL), 1)
    line = lax.broadcasted_iota(jnp.int32, (16, size), 0)
    slot = lax.broadcasted_iota(jnp.int32, (size, slots), 1).astype(jnp.float32)
    slot_t = lax.broadcasted_iota(jnp.int32, (slots, size), 0).astype(jnp.float32)
    labels = [(lax.axis_index("exp") * local + e).astype(jnp.float32) for e in range(local)]
    spreads = []
    for i in range(count):
        batch = blocks[4 * i : 4 * i + 4]
        x = jnp.concatenate([ref[:, :lat] for ref in batch], axis=0)
        tail = jnp.concatenate([ref[:, lat:] for ref in batch], axis=0).astype(jnp.float32)
        masks = [jnp.max(jnp.where(tail == label, 1.0, 0.0), axis=1, keepdims=True) for label in labels]
        tail_t = tail.T[:16]
        masks_t = [jnp.max(jnp.where(tail_t == label, 1.0, 0.0), axis=0, keepdims=True) for label in labels]
        marks, marks_t = jnp.zeros((size, TAIL), jnp.float32), jnp.zeros((16, size), jnp.float32)
        for e in range(local):
            marks = jnp.where(lane == e, masks[e], marks)
            marks_t = jnp.where(line == e, masks_t[e], marks_t)
        place_t = jnp.dot(marks_t.astype(jnp.bfloat16), after, preferred_element_type=jnp.float32)
        place = jnp.dot(before, marks.astype(jnp.bfloat16), preferred_element_type=jnp.float32)
        gather = jnp.concatenate(
            [
                jnp.where((slot_t == place_t[e : e + 1]) & (masks_t[e] > 0.0), 1.0, 0.0)
                for e in range(local)
            ],
            axis=0,
        ).astype(jnp.bfloat16)
        packed = jnp.dot(gather, x, preferred_element_type=jnp.float32).astype(jnp.bfloat16)
        spread = jnp.concatenate(
            [jnp.where((slot == place[:, e : e + 1]) & (masks[e] > 0.0), 1.0, 0.0) for e in range(local)],
            axis=1,
        ).astype(jnp.bfloat16)
        logits = logits_of(x)
        sums = jnp.zeros((size, 1), jnp.float32)
        for e in range(local):
            sums = sums + jax.nn.sigmoid(logits[:, e : e + 1]) * (masks[e] * SCALE)
        put(i, slice(lat, wide), jnp.where(lane == 0, sums, 0.0))
        for e in range(local):
            packed_ref[e, i * slots : (i + 1) * slots, :] = packed[e * slots : (e + 1) * slots]
        spreads.append(spread)
    for e in range(local):
        chosen = packed_ref[e]
        score = jax.nn.sigmoid(logits_of(chosen)[:, e : e + 1]) * SCALE
        for c in range(0, eff, STEP):
            gate = jnp.dot(chosen, up_ref[e, :, c : c + STEP], preferred_element_type=jnp.float32)
            up = jnp.dot(chosen, up_ref[e, :, eff + c : eff + c + STEP], preferred_element_type=jnp.float32)
            inner_ref[e, :, c : c + STEP] = (gate / (1.0 + jnp.exp(-gate)) * up * score).astype(jnp.bfloat16)
    for e in range(local):
        result = jnp.dot(inner_ref[e], down_ref[e], preferred_element_type=jnp.float32).astype(jnp.bfloat16)
        for i in range(count):
            result_ref[i, e * slots : (e + 1) * slots, :] = result[i * slots : (i + 1) * slots]
    for i in range(count):
        for c in range(0, lat, STEP):
            part = jnp.dot(spreads[i], result_ref[i, :, c : c + STEP], preferred_element_type=jnp.float32)
            put(i, slice(c, c + STEP), part)


def tie_kernel():
    pass


def fold_kernel(mine_ref, came_a_ref, came_b_ref, keep_ref, send_ref):
    rows = keep_ref.shape[0]
    keep_ref[...] = mine_ref[:rows] + came_a_ref[...].astype(jnp.float32)
    send_ref[...] = (mine_ref[rows:] + came_b_ref[...].astype(jnp.float32)).astype(jnp.bfloat16)


def add_kernel(mine_ref, *refs):
    total = mine_ref[...]
    for ref in refs[:-1]:
        total = total + ref[...].astype(jnp.float32)
    refs[-1][...] = total.astype(jnp.bfloat16)


def total_kernel(*refs):
    total_ref = refs[-1]
    total = refs[0][...]
    for ref in refs[1:-1]:
        total = total + ref[...].astype(jnp.float32)
    total_ref[...] = total


def finish_kernel(*refs):
    out_ref = refs[-1]
    lat = out_ref.shape[1]
    total = refs[0][...]
    for ref in refs[1:-1]:
        total = total + ref[...].astype(jnp.float32)
    out_ref[...] = (total[:, :lat] / total[:, lat : lat + 1]).astype(jnp.bfloat16)


def in_vmem(x):
    return pltpu.with_memory_space_constraint(x, pltpu.VMEM)


def in_hbm(x):
    return pltpu.with_memory_space_constraint(x, pltpu.HBM)


VMEM = pl.BlockSpec(memory_space=pltpu.VMEM)
ANY = pl.BlockSpec(memory_space=pl.ANY)


def call(kernel, outs, args=(), deps=(), chain=(), hbm=(), scratch=()):
    plain = getattr(kernel, "func", kernel)
    reads_chain = plain is expert_kernel
    n_in = len(args) + len(hbm)
    n_skip = n_in + len(deps)
    n_outs = n_skip + len(chain)

    def body(*refs):
        kernel(*refs[:n_in], *refs[n_outs : n_outs + len(outs)], *refs[n_outs + len(outs) + len(chain) :])

    def body_with_chain(*refs):
        kernel(
            *refs[:n_in],
            *refs[n_skip:n_outs],
            *refs[n_outs : n_outs + len(outs)],
            *refs[n_outs + len(outs) + len(chain) :],
        )

    specs = [VMEM] * len(args)
    specs += [ANY] * (len(hbm) + len(deps)) + [VMEM] * len(chain)
    operands = [in_vmem(a) for a in args] + [in_hbm(h) for h in hbm]
    operands += [in_vmem(x) for x in (*deps, *chain)]
    return pl.pallas_call(
        body_with_chain if reads_chain else body,
        out_shape=list(outs) + [pltpu.VMEM(x.shape, x.dtype) for x in chain],
        in_specs=specs,
        out_specs=[VMEM] * (len(outs) + len(chain)),
        scratch_shapes=list(scratch),
        compiler_params=pltpu.CompilerParams(vmem_limit_bytes=SCOPED),
        cost_estimate=pl.CostEstimate(flops=0, bytes_accessed=10_000, transcendentals=0),
        input_output_aliases={n_skip + i: len(outs) + i for i in range(len(chain))},
        name=plain.__name__.removesuffix("_kernel"),
    )(*operands)


def on_device(latent_in, routes, router, gate_up, expert_down):
    n_dev = lax.axis_size("exp")
    local = gate_up.shape[0]
    eff = expert_down.shape[1]
    rows, lat = latent_in.shape
    wide = lat + TAIL

    def swap(x, bits):
        return lax.ppermute(x, "exp", [(i, i ^ bits) for i in range(n_dev)])

    def space(height, dtype):
        return pltpu.VMEM((height, wide), dtype)

    def weights(dep):
        return call(
            load_kernel,
            [
                pltpu.VMEM((lat, TAIL), jnp.bfloat16),
                pltpu.VMEM(gate_up.shape, gate_up.dtype),
                pltpu.VMEM(expert_down.shape, expert_down.dtype),
            ],
            deps=[dep],
            hbm=[router.T, gate_up, expert_down],
            scratch=[
                pltpu.VMEM((local, lat), jnp.bfloat16),
                pltpu.SemaphoreType.DMA((1 + local * (lat + eff) // PIECE,)),
            ],
        )

    bound = 2 * ((rows * routes.shape[1] + local * n_dev - 1) // (local * n_dev))
    slots = 4 * bound

    def group_pass(mine):
        block, other = {0: mine}, {0: swap(mine, 2)}
        held = weights(other[0])

        def step(kernel, outs, args=(), deps=(), hand_on=(), **more):
            nonlocal held
            result = call(kernel, outs, args, deps, [*held, *hand_on], **more)
            held = result[len(outs) : len(outs) + len(held)]
            return result[: len(outs)] + result[len(outs) + len(held) :]

        def tie(x, deps=()):
            return step(tie_kernel, [], deps=deps, hand_on=[x])[0]

        keep, send, came, fold_keep, fold_send, y_came = {}, {}, {}, {}, {}, {}

        def compute(*ks):
            count = len(ks)
            blocks = []
            for k in ks:
                near = [block[k], other[k]]
                blocks += near + [swap(one, 1) for one in near]
            result = step(
                functools.partial(expert_kernel, count),
                [space(2 * rows, jnp.float32)] * count + [space(rows, jnp.bfloat16)] * (2 * count),
                blocks,
                scratch=[
                    pltpu.VMEM((local, count * slots, lat), jnp.bfloat16),
                    pltpu.VMEM((local, count * slots, eff), jnp.bfloat16),
                    pltpu.VMEM((count, local * slots, lat), jnp.bfloat16),
                ],
            )
            for i, k in enumerate(ks):
                keep[k] = result[i]
                came[k] = [swap(part, 1) for part in result[count + 2 * i : count + 2 * i + 2]]

        def reduce_core(k, deps=()):
            fold_keep[k], fold_send[k] = step(
                fold_kernel, [space(rows, jnp.float32), space(rows, jnp.bfloat16)], [keep[k], *came[k]], deps
            )
            y_came[k] = swap(fold_send[k], 2)

        def reduce_y(k, deps=()):
            sums = step(add_kernel, [space(rows, jnp.bfloat16)], [fold_keep[k], y_came[k]], deps)[0]
            return swap(sums, 4 * k)

        block[1], block[2] = swap(mine, 4), swap(mine, 8)
        other[1], other[2] = swap(other[0], 4), swap(other[0], 8)
        block[2] = tie(block[2])
        block[3] = swap(block[2], 4)
        compute(0)
        other[1] = tie(other[1], [other[2], block[3]])
        other[3] = swap(other[2], 4)
        reduce_core(0)
        compute(2)
        other[3] = tie(other[3])
        reduce_core(2, [y_came[0]])
        compute(3, 1)
        z_2 = reduce_y(2)
        reduce_core(3)
        reduce_core(1)
        z_3 = reduce_y(3)
        z_1 = reduce_y(1, [z_2])
        return fold_keep[0], y_came[0], z_2, z_3, z_1

    packet = call(
        pack_kernel,
        [space(rows, jnp.bfloat16)],
        hbm=[routes.T, latent_in],
        scratch=[pltpu.VMEM(routes.shape[::-1], routes.dtype), pltpu.SemaphoreType.DMA((2,))],
    )[0]

    def finish(parts):
        return pl.pallas_call(
            finish_kernel,
            out_shape=jax.ShapeDtypeStruct((rows, lat), jnp.bfloat16),
            in_specs=[VMEM] * len(parts),
            out_specs=VMEM,
            compiler_params=pltpu.CompilerParams(vmem_limit_bytes=SCOPED),
            name="finish",
        )(*[in_vmem(p) for p in parts])

    if n_dev == GROUP:
        return finish(group_pass(packet))

    def next_group(x):
        return lax.ppermute(x, "exp", [(i, (i + GROUP) % n_dev) for i in range(n_dev)])

    def step(carry, _):
        mine, total = carry
        total = call(total_kernel, [space(rows, jnp.float32)], [total, *group_pass(mine)])[0]
        return (next_group(mine), next_group(total)), None

    start = (packet, jnp.zeros((rows, wide), jnp.float32))
    (_, total), _ = lax.scan(step, start, None, length=n_dev // GROUP)
    return finish([total])


def solution(mesh):
    placed = (
        P(("grp", "exp"), None),
        P(("grp", "exp"), None),
        P(None, "exp"),
        P("exp", None, None),
        P("exp", None, None),
    )
    return jax.shard_map(
        on_device, mesh=mesh, in_specs=placed, out_specs=P(("grp", "exp"), None), check_vma=False
    )
```

```python
import functools

import jax
import jax.numpy as jnp
from jax import lax
from jax.experimental import pallas as pl
from jax.experimental.pallas import tpu as pltpu
from jax.sharding import PartitionSpec as P

GROUP = 16
SCOPED = 8 * 1024 * 1024
TAIL = 128
SCALE = 2.0**40
STEP = 256
PIECE = 256


def pack_kernel(ids_hbm, row_hbm, out_ref, ids_ref, sems):
    rows, lat = row_hbm.shape
    top = ids_hbm.shape[0]
    get_ids = pltpu.make_async_copy(ids_hbm, ids_ref, sems.at[0])
    get_rows = pltpu.make_async_copy(row_hbm, out_ref.at[:, pl.ds(0, lat)], sems.at[1])
    get_ids.start()
    get_rows.start()
    get_ids.wait()
    ids = ids_ref[...].astype(jnp.float32)
    ids = jnp.concatenate([ids, jnp.full((top, TAIL - rows), -1.0, jnp.float32)], axis=1)
    ids = jnp.concatenate([ids, jnp.full((TAIL - top, TAIL), -1.0, jnp.float32)], axis=0)
    out_ref[:, lat:] = ids.T[:rows].astype(jnp.bfloat16)
    get_rows.wait()


def load_kernel(router_hbm, up_hbm, down_hbm, columns_ref, up_ref, down_ref, router_ref, sems):
    get_router = pltpu.make_async_copy(router_hbm, router_ref, sems.at[0])
    get_router.start()
    copies = []
    for src, dst in ((up_hbm, up_ref), (down_hbm, down_ref)):
        for e in range(src.shape[0]):
            for r in range(0, src.shape[1], PIECE):
                at = (e, pl.ds(r, PIECE))
                copies.append(pltpu.make_async_copy(src.at[at], dst.at[at], sems.at[1 + len(copies)]))
    for copy in copies:
        copy.start()
    get_router.wait()
    local, lat = router_ref.shape
    wide = jnp.concatenate(
        [router_ref[...].astype(jnp.float32), jnp.zeros((TAIL - local, lat), jnp.float32)], axis=0
    )
    columns_ref[...] = wide.T.astype(jnp.bfloat16)
    for copy in copies:
        copy.wait()


def expert_kernel(count, *refs):
    blocks, refs = refs[: 4 * count], refs[4 * count :]
    (columns_ref, up_ref, down_ref), refs = refs[:3], refs[3:]
    keep_refs, refs = refs[:count], refs[count:]
    send_refs, (packed_ref, inner_ref, result_ref) = refs[: 2 * count], refs[2 * count :]
    rows, wide = blocks[0].shape
    half, lat = 2 * rows, wide - TAIL
    local, eff, _ = down_ref.shape
    slots = packed_ref.shape[1] // count

    def put(i, lanes, value):
        keep_refs[i][:, lanes] = value[:half]
        for j, ref in enumerate(send_refs[2 * i : 2 * i + 2]):
            ref[:, lanes] = value[half + j * rows : half + (j + 1) * rows].astype(jnp.bfloat16)

    def logits_of(values):
        return jnp.dot(values, columns_ref[...], preferred_element_type=jnp.float32)

    size = 2 * half
    row = lax.broadcasted_iota(jnp.int32, (size, size), 0)
    col = lax.broadcasted_iota(jnp.int32, (size, size), 1)
    before = jnp.where(col < row, 1.0, 0.0).astype(jnp.bfloat16)
    after = jnp.where(row < col, 1.0, 0.0).astype(jnp.bfloat16)
    lane = lax.broadcasted_iota(jnp.int32, (size, TAIL), 1)
    line = lax.broadcasted_iota(jnp.int32, (16, size), 0)
    slot = lax.broadcasted_iota(jnp.int32, (size, slots), 1).astype(jnp.float32)
    slot_t = lax.broadcasted_iota(jnp.int32, (slots, size), 0).astype(jnp.float32)
    labels = [(lax.axis_index("exp") * local + e).astype(jnp.float32) for e in range(local)]
    spreads = []
    for i in range(count):
        batch = blocks[4 * i : 4 * i + 4]
        x = jnp.concatenate([ref[:, :lat] for ref in batch], axis=0)
        tail = jnp.concatenate([ref[:, lat:] for ref in batch], axis=0).astype(jnp.float32)
        masks = [jnp.max(jnp.where(tail == label, 1.0, 0.0), axis=1, keepdims=True) for label in labels]
        tail_t = tail.T[:16]
        masks_t = [jnp.max(jnp.where(tail_t == label, 1.0, 0.0), axis=0, keepdims=True) for label in labels]
        marks, marks_t = jnp.zeros((size, TAIL), jnp.float32), jnp.zeros((16, size), jnp.float32)
        for e in range(local):
            marks = jnp.where(lane == e, masks[e], marks)
            marks_t = jnp.where(line == e, masks_t[e], marks_t)
        place_t = jnp.dot(marks_t.astype(jnp.bfloat16), after, preferred_element_type=jnp.float32)
        place = jnp.dot(before, marks.astype(jnp.bfloat16), preferred_element_type=jnp.float32)
        gather = jnp.concatenate(
            [
                jnp.where((slot_t == place_t[e : e + 1]) & (masks_t[e] > 0.0), 1.0, 0.0)
                for e in range(local)
            ],
            axis=0,
        ).astype(jnp.bfloat16)
        packed = jnp.dot(gather, x, preferred_element_type=jnp.float32).astype(jnp.bfloat16)
        spread = jnp.concatenate(
            [jnp.where((slot == place[:, e : e + 1]) & (masks[e] > 0.0), 1.0, 0.0) for e in range(local)],
            axis=1,
        ).astype(jnp.bfloat16)
        logits = logits_of(x)
        sums = jnp.zeros((size, 1), jnp.float32)
        for e in range(local):
            sums = sums + jax.nn.sigmoid(logits[:, e : e + 1]) * (masks[e] * SCALE)
        put(i, slice(lat, wide), jnp.where(lane == 0, sums, 0.0))
        for e in range(local):
            packed_ref[e, i * slots : (i + 1) * slots, :] = packed[e * slots : (e + 1) * slots]
        spreads.append(spread)
    for e in range(local):
        chosen = packed_ref[e]
        score = jax.nn.sigmoid(logits_of(chosen)[:, e : e + 1]) * SCALE
        for c in range(0, eff, STEP):
            gate = jnp.dot(chosen, up_ref[e, :, c : c + STEP], preferred_element_type=jnp.float32)
            up = jnp.dot(chosen, up_ref[e, :, eff + c : eff + c + STEP], preferred_element_type=jnp.float32)
            inner_ref[e, :, c : c + STEP] = (gate / (1.0 + jnp.exp(-gate)) * up * score).astype(jnp.bfloat16)
    for e in range(local):
        result = jnp.dot(inner_ref[e], down_ref[e], preferred_element_type=jnp.float32).astype(jnp.bfloat16)
        for i in range(count):
            result_ref[i, e * slots : (e + 1) * slots, :] = result[i * slots : (i + 1) * slots]
    for i in range(count):
        for c in range(0, lat, STEP):
            part = jnp.dot(spreads[i], result_ref[i, :, c : c + STEP], preferred_element_type=jnp.float32)
            put(i, slice(c, c + STEP), part)


def tie_kernel():
    pass


def fold_kernel(mine_ref, came_a_ref, came_b_ref, keep_ref, send_ref):
    rows = keep_ref.shape[0]
    keep_ref[...] = mine_ref[:rows] + came_a_ref[...].astype(jnp.float32)
    send_ref[...] = (mine_ref[rows:] + came_b_ref[...].astype(jnp.float32)).astype(jnp.bfloat16)


def add_kernel(mine_ref, *refs):
    total = mine_ref[...]
    for ref in refs[:-1]:
        total = total + ref[...].astype(jnp.float32)
    refs[-1][...] = total.astype(jnp.bfloat16)


def total_kernel(*refs):
    total_ref = refs[-1]
    total = refs[0][...]
    for ref in refs[1:-1]:
        total = total + ref[...].astype(jnp.float32)
    total_ref[...] = total


def finish_kernel(*refs):
    out_ref = refs[-1]
    lat = out_ref.shape[1]
    total = refs[0][...]
    for ref in refs[1:-1]:
        total = total + ref[...].astype(jnp.float32)
    out_ref[...] = (total[:, :lat] / total[:, lat : lat + 1]).astype(jnp.bfloat16)


def in_vmem(x):
    return pltpu.with_memory_space_constraint(x, pltpu.VMEM)


def in_hbm(x):
    return pltpu.with_memory_space_constraint(x, pltpu.HBM)


VMEM = pl.BlockSpec(memory_space=pltpu.VMEM)
ANY = pl.BlockSpec(memory_space=pl.ANY)


def call(kernel, outs, args=(), deps=(), chain=(), hbm=(), scratch=()):
    plain = getattr(kernel, "func", kernel)
    reads_chain = plain is expert_kernel
    n_in = len(args) + len(hbm)
    n_skip = n_in + len(deps)
    n_outs = n_skip + len(chain)

    def body(*refs):
        kernel(*refs[:n_in], *refs[n_outs : n_outs + len(outs)], *refs[n_outs + len(outs) + len(chain) :])

    def body_with_chain(*refs):
        kernel(
            *refs[:n_in],
            *refs[n_skip:n_outs],
            *refs[n_outs : n_outs + len(outs)],
            *refs[n_outs + len(outs) + len(chain) :],
        )

    specs = [VMEM] * len(args)
    specs += [ANY] * (len(hbm) + len(deps)) + [VMEM] * len(chain)
    operands = [in_vmem(a) for a in args] + [in_hbm(h) for h in hbm]
    operands += [in_vmem(x) for x in (*deps, *chain)]
    return pl.pallas_call(
        body_with_chain if reads_chain else body,
        out_shape=list(outs) + [pltpu.VMEM(x.shape, x.dtype) for x in chain],
        in_specs=specs,
        out_specs=[VMEM] * (len(outs) + len(chain)),
        scratch_shapes=list(scratch),
        compiler_params=pltpu.CompilerParams(vmem_limit_bytes=SCOPED),
        cost_estimate=pl.CostEstimate(flops=0, bytes_accessed=10_000, transcendentals=0),
        input_output_aliases={n_skip + i: len(outs) + i for i in range(len(chain))},
        name=plain.__name__.removesuffix("_kernel"),
    )(*operands)


def on_device(latent_in, routes, router, gate_up, expert_down):
    n_dev = lax.axis_size("exp")
    local = gate_up.shape[0]
    eff = expert_down.shape[1]
    rows, lat = latent_in.shape
    wide = lat + TAIL

    def swap(x, bits):
        return lax.ppermute(x, "exp", [(i, i ^ bits) for i in range(n_dev)])

    def space(height, dtype):
        return pltpu.VMEM((height, wide), dtype)

    def weights(dep):
        return call(
            load_kernel,
            [
                pltpu.VMEM((lat, TAIL), jnp.bfloat16),
                pltpu.VMEM(gate_up.shape, gate_up.dtype),
                pltpu.VMEM(expert_down.shape, expert_down.dtype),
            ],
            deps=[dep],
            hbm=[router.T, gate_up, expert_down],
            scratch=[
                pltpu.VMEM((local, lat), jnp.bfloat16),
                pltpu.SemaphoreType.DMA((1 + local * (lat + eff) // PIECE,)),
            ],
        )

    bound = 2 * ((rows * routes.shape[1] + local * n_dev - 1) // (local * n_dev))
    slots = 4 * bound

    def group_pass(mine):
        held = weights(mine)

        def step(kernel, outs, args=(), deps=(), hand_on=(), **more):
            nonlocal held
            result = call(kernel, outs, args, deps, [*held, *hand_on], **more)
            held = result[len(outs) : len(outs) + len(held)]
            return result[: len(outs)] + result[len(outs) + len(held) :]

        def tie(x, deps=()):
            return step(tie_kernel, [], deps=deps, hand_on=[x])[0]

        other, keep, send, came, fold_keep, fold_send, y_came = {}, {}, {}, {}, {}, {}, {}

        def gather(k, deps=()):
            other[k] = tie(swap(block[k], 2), deps)

        def compute(*ks):
            count = len(ks)
            blocks = []
            for k in ks:
                near = [block[k], other[k]]
                blocks += near + [swap(one, 1) for one in near]
            result = step(
                functools.partial(expert_kernel, count),
                [space(2 * rows, jnp.float32)] * count + [space(rows, jnp.bfloat16)] * (2 * count),
                blocks,
                scratch=[
                    pltpu.VMEM((local, count * slots, lat), jnp.bfloat16),
                    pltpu.VMEM((local, count * slots, eff), jnp.bfloat16),
                    pltpu.VMEM((count, local * slots, lat), jnp.bfloat16),
                ],
            )
            for i, k in enumerate(ks):
                keep[k] = result[i]
                came[k] = [swap(part, 1) for part in result[count + 2 * i : count + 2 * i + 2]]

        def reduce_core(k, deps=()):
            fold_keep[k], fold_send[k] = step(
                fold_kernel, [space(rows, jnp.float32), space(rows, jnp.bfloat16)], [keep[k], *came[k]], deps
            )
            y_came[k] = swap(fold_send[k], 2)

        def reduce_y(k, *more):
            return step(add_kernel, [space(rows, jnp.bfloat16)], [fold_keep[k], y_came[k], *more])[0]

        z_2, z_1, y_0 = swap(mine, 8), swap(mine, 4), swap(mine, 2)
        block = {0: mine, 2: tie(z_2), 1: z_1}
        block[3] = swap(block[2], 4)
        other[0] = y_0
        gather(2, [block[1], block[3], y_0])
        gather(1)
        compute(2)
        gather(3)
        reduce_core(2)
        compute(3)
        other[0] = tie(other[0], [y_came[2]])
        reduce_core(3)
        compute(1)
        z_3 = swap(reduce_y(3), 4)
        compute(0)
        reduce_core(1)
        z_2 = swap(reduce_y(2, z_3), 8)
        reduce_core(0)
        z_1 = swap(reduce_y(1), 4)
        return fold_keep[0], z_2, z_1, y_came[0]

    packet = call(
        pack_kernel,
        [space(rows, jnp.bfloat16)],
        hbm=[routes.T, latent_in],
        scratch=[pltpu.VMEM(routes.shape[::-1], routes.dtype), pltpu.SemaphoreType.DMA((2,))],
    )[0]

    def finish(parts):
        return pl.pallas_call(
            finish_kernel,
            out_shape=jax.ShapeDtypeStruct((rows, lat), jnp.bfloat16),
            in_specs=[VMEM] * len(parts),
            out_specs=VMEM,
            compiler_params=pltpu.CompilerParams(vmem_limit_bytes=SCOPED),
            name="finish",
        )(*[in_vmem(p) for p in parts])

    if n_dev == GROUP:
        return finish(group_pass(packet))

    def next_group(x):
        return lax.ppermute(x, "exp", [(i, (i + GROUP) % n_dev) for i in range(n_dev)])

    def step(carry, _):
        mine, total = carry
        total = call(total_kernel, [space(rows, jnp.float32)], [total, *group_pass(mine)])[0]
        return (next_group(mine), next_group(total)), None

    start = (packet, jnp.zeros((rows, wide), jnp.float32))
    (_, total), _ = lax.scan(step, start, None, length=n_dev // GROUP)
    return finish([total])


def solution(mesh):
    placed = (
        P(("grp", "exp"), None),
        P(("grp", "exp"), None),
        P(None, "exp"),
        P("exp", None, None),
        P("exp", None, None),
    )
    return jax.shard_map(
        on_device, mesh=mesh, in_specs=placed, out_specs=P(("grp", "exp"), None), check_vma=False
    )
```

```python
import functools

import jax
import jax.numpy as jnp
from jax import lax
from jax.experimental import pallas as pl
from jax.experimental.pallas import tpu as pltpu
from jax.sharding import PartitionSpec as P

GROUP = 16
SCOPED = 8 * 1024 * 1024
TAIL = 128
LINE = 16
SCALE = 2.0**40
STEP = 256
PIECE = 256


def pack_kernel(ids_hbm, row_hbm, router_hbm, out_ref, ids_ref, router_ref, sems):
    rows, lat = row_hbm.shape
    local = router_hbm.shape[0]
    top = ids_hbm.shape[0]
    copies = [
        pltpu.make_async_copy(ids_hbm, ids_ref, sems.at[0]),
        pltpu.make_async_copy(router_hbm, router_ref, sems.at[1]),
        pltpu.make_async_copy(row_hbm, out_ref.at[:, pl.ds(0, lat)], sems.at[2]),
    ]
    for copy in copies:
        copy.start()
    copies[0].wait()
    copies[1].wait()
    ids = ids_ref[...].astype(jnp.float32)
    router = router_ref[...].astype(jnp.float32)
    lines = [jnp.concatenate([ids, jnp.full((top, TAIL - rows), -1.0, jnp.float32)], axis=1)]
    lines.append(jnp.full((LINE - top, TAIL), -1.0, jnp.float32))
    for e in range(local):
        for c in range(0, lat, TAIL):
            lines.append(router[e : e + 1, c : c + TAIL])
    lines.append(jnp.full((rows - LINE - local * lat // TAIL, TAIL), -1.0, jnp.float32))
    out_ref[:, lat:] = jnp.concatenate(lines, axis=0).astype(jnp.bfloat16)
    copies[2].wait()


def load_kernel(router_hbm, up_hbm, down_hbm, columns_ref, up_ref, down_ref, router_ref, sems):
    get_router = pltpu.make_async_copy(router_hbm, router_ref, sems.at[0])
    get_router.start()
    copies = []
    for src, dst in ((up_hbm, up_ref), (down_hbm, down_ref)):
        for e in range(src.shape[0]):
            for r in range(0, src.shape[1], PIECE):
                at = (e, pl.ds(r, PIECE))
                copies.append(pltpu.make_async_copy(src.at[at], dst.at[at], sems.at[1 + len(copies)]))
    for copy in copies:
        copy.start()
    get_router.wait()
    local, lat = router_ref.shape
    wide = jnp.concatenate(
        [router_ref[...].astype(jnp.float32), jnp.zeros((TAIL - local, lat), jnp.float32)], axis=0
    )
    columns_ref[...] = wide.T.astype(jnp.bfloat16)
    for copy in copies:
        copy.wait()


def expert_kernel(count, *refs):
    blocks, refs = refs[: 4 * count], refs[4 * count :]
    (columns_ref, up_ref, down_ref), refs = refs[:3], refs[3:]
    keep_refs, refs = refs[:count], refs[count:]
    send_refs, (packed_ref, inner_ref, result_ref) = refs[: 2 * count], refs[2 * count :]
    rows, lat = blocks[0].shape[0], blocks[0].shape[1] - TAIL
    half = 2 * rows
    local, eff, _ = down_ref.shape
    slots = packed_ref.shape[1] // count

    def put(i, lanes, value):
        keep_refs[i][:, lanes] = value[:half]
        for j, ref in enumerate(send_refs[2 * i : 2 * i + 2]):
            ref[:, lanes] = value[half + j * rows : half + (j + 1) * rows].astype(jnp.bfloat16)

    def logits_of(values):
        return jnp.dot(values, columns_ref[...], preferred_element_type=jnp.float32)

    size = 2 * half
    row = lax.broadcasted_iota(jnp.int32, (size, size), 0)
    col = lax.broadcasted_iota(jnp.int32, (size, size), 1)
    before = jnp.where(col < row, 1.0, 0.0).astype(jnp.bfloat16)
    after = jnp.where(row < col, 1.0, 0.0).astype(jnp.bfloat16)
    line = lax.broadcasted_iota(jnp.int32, (LINE, size), 0)
    slot = lax.broadcasted_iota(jnp.int32, (size, slots), 1).astype(jnp.float32)
    slot_t = lax.broadcasted_iota(jnp.int32, (slots, size), 0).astype(jnp.float32)
    labels = [(lax.axis_index("exp") * local + e).astype(jnp.float32) for e in range(local)]
    spreads = []
    for i in range(count):
        batch = blocks[4 * i : 4 * i + 4]
        x = jnp.concatenate([ref[:, :lat] for ref in batch], axis=0)
        ids_t = jnp.concatenate([ref[:LINE, lat:].astype(jnp.float32)[:, :rows] for ref in batch], axis=1)
        masks_t = [jnp.max(jnp.where(ids_t == label, 1.0, 0.0), axis=0, keepdims=True) for label in labels]
        marks_t = jnp.zeros((LINE, size), jnp.float32)
        for e in range(local):
            marks_t = jnp.where(line == e, masks_t[e], marks_t)
        marks = jnp.concatenate([marks_t, jnp.zeros((TAIL - LINE, size), jnp.float32)], axis=0).T
        place_t = jnp.dot(marks_t.astype(jnp.bfloat16), after, preferred_element_type=jnp.float32)
        place = jnp.dot(before, marks.astype(jnp.bfloat16), preferred_element_type=jnp.float32)
        gather = jnp.concatenate(
            [
                jnp.where((slot_t == place_t[e : e + 1]) & (masks_t[e] > 0.0), 1.0, 0.0)
                for e in range(local)
            ],
            axis=0,
        ).astype(jnp.bfloat16)
        packed = jnp.dot(gather, x, preferred_element_type=jnp.float32).astype(jnp.bfloat16)
        spread = jnp.concatenate(
            [jnp.where((slot == place[:, e : e + 1]) & (marks[:, e : e + 1] > 0.0), 1.0, 0.0) for e in range(local)],
            axis=1,
        ).astype(jnp.bfloat16)
        for e in range(local):
            packed_ref[e, i * slots : (i + 1) * slots, :] = packed[e * slots : (e + 1) * slots]
        spreads.append(spread)
    for e in range(local):
        chosen = packed_ref[e]
        score = jax.nn.sigmoid(logits_of(chosen)[:, e : e + 1]) * SCALE
        for c in range(0, eff, STEP):
            gate = jnp.dot(chosen, up_ref[e, :, c : c + STEP], preferred_element_type=jnp.float32)
            up = jnp.dot(chosen, up_ref[e, :, eff + c : eff + c + STEP], preferred_element_type=jnp.float32)
            inner_ref[e, :, c : c + STEP] = (gate / (1.0 + jnp.exp(-gate)) * up * score).astype(jnp.bfloat16)
    for e in range(local):
        result = jnp.dot(inner_ref[e], down_ref[e], preferred_element_type=jnp.float32).astype(jnp.bfloat16)
        for i in range(count):
            result_ref[i, e * slots : (e + 1) * slots, :] = result[i * slots : (i + 1) * slots]
    for i in range(count):
        for c in range(0, lat, STEP):
            part = jnp.dot(spreads[i], result_ref[i, :, c : c + STEP], preferred_element_type=jnp.float32)
            put(i, slice(c, c + STEP), part)


def tie_kernel():
    pass


def fold_kernel(mine_ref, came_a_ref, came_b_ref, keep_ref, send_ref):
    rows = keep_ref.shape[0]
    keep_ref[...] = mine_ref[:rows] + came_a_ref[...].astype(jnp.float32)
    send_ref[...] = (mine_ref[rows:] + came_b_ref[...].astype(jnp.float32)).astype(jnp.bfloat16)


def add_kernel(mine_ref, *refs):
    total = mine_ref[...]
    for ref in refs[:-1]:
        total = total + ref[...].astype(jnp.float32)
    refs[-1][...] = total.astype(jnp.bfloat16)


def total_kernel(*refs):
    total_ref = refs[-1]
    total = refs[0][...]
    for ref in refs[1:-1]:
        total = total + ref[...].astype(jnp.float32)
    total_ref[...] = total


def scores_kernel(mine_ref, *refs):
    *packet_refs, out_ref, lines_ref = refs
    rows, lat = mine_ref.shape[0], mine_ref.shape[1] - TAIL
    chunks = lat // TAIL
    height = lines_ref.shape[0] // len(packet_refs)
    local = height // chunks
    for i, ref in enumerate(packet_refs):
        lines_ref[i * height : (i + 1) * height, :] = ref[LINE : LINE + height, lat:].astype(jnp.float32)
    number = len(packet_refs) * local
    logits = jnp.zeros((number, rows), jnp.float32)
    for c in range(chunks):
        columns = lines_ref[pl.ds(c, number, stride=chunks), :].astype(jnp.bfloat16)
        logits = logits + lax.dot_general(
            columns,
            mine_ref[:, c * TAIL : (c + 1) * TAIL],
            (((1,), (1,)), ((), ())),
            preferred_element_type=jnp.float32,
        )
    at = lax.broadcasted_iota(jnp.int32, (number, rows), 0)
    label = ((lax.axis_index("exp") ^ (at // local)) * local + at % local).astype(jnp.float32)
    ids = mine_ref[:LINE, lat:].astype(jnp.float32)[:, :rows]
    mask = jnp.zeros((number, rows), jnp.float32)
    for k in range(LINE):
        mask = jnp.where(ids[k : k + 1] == label, 1.0, mask)
    total = jnp.sum(jax.nn.sigmoid(logits) * (mask * SCALE), axis=0, keepdims=True)
    total = jnp.broadcast_to(total, (TAIL, rows))
    total = jnp.concatenate([total, jnp.ones((TAIL, TAIL - rows), jnp.float32)], axis=1)
    out_ref[...] = total.T[:rows]


def finish_kernel(scores_ref, *refs):
    total = refs[0][...]
    for ref in refs[1:-1]:
        total = total + ref[...].astype(jnp.float32)
    refs[-1][...] = (total / scores_ref[:, :1]).astype(jnp.bfloat16)


def in_vmem(x):
    return pltpu.with_memory_space_constraint(x, pltpu.VMEM)


def in_hbm(x):
    return pltpu.with_memory_space_constraint(x, pltpu.HBM)


VMEM = pl.BlockSpec(memory_space=pltpu.VMEM)
ANY = pl.BlockSpec(memory_space=pl.ANY)


def call(kernel, outs, args=(), deps=(), chain=(), hbm=(), scratch=()):
    plain = getattr(kernel, "func", kernel)
    reads_chain = plain is expert_kernel
    n_in = len(args) + len(hbm)
    n_skip = n_in + len(deps)
    n_outs = n_skip + len(chain)

    def body(*refs):
        kernel(*refs[:n_in], *refs[n_outs : n_outs + len(outs)], *refs[n_outs + len(outs) + len(chain) :])

    def body_with_chain(*refs):
        kernel(
            *refs[:n_in],
            *refs[n_skip:n_outs],
            *refs[n_outs : n_outs + len(outs)],
            *refs[n_outs + len(outs) + len(chain) :],
        )

    specs = [VMEM] * len(args)
    specs += [ANY] * (len(hbm) + len(deps)) + [VMEM] * len(chain)
    operands = [in_vmem(a) for a in args] + [in_hbm(h) for h in hbm]
    operands += [in_vmem(x) for x in (*deps, *chain)]
    return pl.pallas_call(
        body_with_chain if reads_chain else body,
        out_shape=list(outs) + [pltpu.VMEM(x.shape, x.dtype) for x in chain],
        in_specs=specs,
        out_specs=[VMEM] * (len(outs) + len(chain)),
        scratch_shapes=list(scratch),
        compiler_params=pltpu.CompilerParams(vmem_limit_bytes=SCOPED),
        cost_estimate=pl.CostEstimate(flops=0, bytes_accessed=10_000, transcendentals=0),
        input_output_aliases={n_skip + i: len(outs) + i for i in range(len(chain))},
        name=plain.__name__.removesuffix("_kernel"),
    )(*operands)


def on_device(latent_in, routes, router, gate_up, expert_down):
    n_dev = lax.axis_size("exp")
    local = gate_up.shape[0]
    eff = expert_down.shape[1]
    rows, lat = latent_in.shape
    wide = lat + TAIL

    def swap(x, bits):
        return lax.ppermute(x, "exp", [(i, i ^ bits) for i in range(n_dev)])

    def space(height, dtype):
        return pltpu.VMEM((height, lat), dtype)

    def weights(dep):
        return call(
            load_kernel,
            [
                pltpu.VMEM((lat, TAIL), jnp.bfloat16),
                pltpu.VMEM(gate_up.shape, gate_up.dtype),
                pltpu.VMEM(expert_down.shape, expert_down.dtype),
            ],
            deps=[dep],
            hbm=[router.T, gate_up, expert_down],
            scratch=[
                pltpu.VMEM((local, lat), jnp.bfloat16),
                pltpu.SemaphoreType.DMA((1 + local * (lat + eff) // PIECE,)),
            ],
        )

    bound = 2 * ((rows * routes.shape[1] + local * n_dev - 1) // (local * n_dev))
    slots = 4 * bound

    def group_pass(mine):
        held = weights(mine)

        def step(kernel, outs, args=(), deps=(), hand_on=(), **more):
            nonlocal held
            result = call(kernel, outs, args, deps, [*held, *hand_on], **more)
            held = result[len(outs) : len(outs) + len(held)]
            return result[: len(outs)] + result[len(outs) + len(held) :]

        def tie(x, deps=()):
            return step(tie_kernel, [], deps=deps, hand_on=[x])[0]

        other, keep, send, came, fold_keep, fold_send, y_came, far = {}, {}, {}, {}, {}, {}, {}, {}

        def gather(k, deps=()):
            other[k] = tie(swap(block[k], 2), deps)

        def compute(*ks):
            count = len(ks)
            blocks = []
            for k in ks:
                near = [block[k], other[k]]
                far[k] = [swap(one, 1) for one in near]
                blocks += near + far[k]
            result = step(
                functools.partial(expert_kernel, count),
                [space(2 * rows, jnp.float32)] * count + [space(rows, jnp.bfloat16)] * (2 * count),
                blocks,
                scratch=[
                    pltpu.VMEM((local, count * slots, lat), jnp.bfloat16),
                    pltpu.VMEM((local, count * slots, eff), jnp.bfloat16),
                    pltpu.VMEM((count, local * slots, lat), jnp.bfloat16),
                ],
            )
            for i, k in enumerate(ks):
                keep[k] = result[i]
                came[k] = [swap(part, 1) for part in result[count + 2 * i : count + 2 * i + 2]]

        def reduce_core(k, deps=()):
            fold_keep[k], fold_send[k] = step(
                fold_kernel, [space(rows, jnp.float32), space(rows, jnp.bfloat16)], [keep[k], *came[k]], deps
            )
            y_came[k] = swap(fold_send[k], 2)

        def reduce_y(k, *more):
            return step(add_kernel, [space(rows, jnp.bfloat16)], [fold_keep[k], y_came[k], *more])[0]

        z_2, z_1, y_0 = swap(mine, 8), swap(mine, 4), swap(mine, 2)
        block = {0: mine, 2: tie(z_2), 1: z_1}
        block[3] = swap(block[2], 4)
        other[0] = y_0
        gather(2, [block[1], block[3], y_0])
        gather(1)
        compute(2)
        gather(3)
        reduce_core(2)
        compute(3)
        reduce_core(3, [y_came[2]])
        compute(1, 0)
        z_3 = swap(reduce_y(3), 4)
        reduce_core(1)
        reduce_core(0)
        scores = None
        if n_dev == GROUP:
            packets = [p for k in range(4) for p in (block[k], far[k][0], other[k], far[k][1])]
            scores = step(
                scores_kernel,
                [pltpu.VMEM((rows, TAIL), jnp.float32)],
                [mine, *packets],
                scratch=[pltpu.VMEM((n_dev * local * lat // TAIL, TAIL), jnp.float32)],
            )[0]
        z_2 = swap(reduce_y(2, z_3), 8)
        z_1 = swap(reduce_y(1), 4)
        return scores, (fold_keep[0], z_2, z_1, y_came[0])

    packet = call(
        pack_kernel,
        [pltpu.VMEM((rows, wide), jnp.bfloat16)],
        hbm=[routes.T, latent_in, router.T],
        scratch=[
            pltpu.VMEM(routes.shape[::-1], routes.dtype),
            pltpu.VMEM((local, lat), jnp.bfloat16),
            pltpu.SemaphoreType.DMA((3,)),
        ],
    )[0]

    def finish(scores, parts):
        return pl.pallas_call(
            finish_kernel,
            out_shape=jax.ShapeDtypeStruct((rows, lat), jnp.bfloat16),
            in_specs=[VMEM] * (1 + len(parts)),
            out_specs=VMEM,
            compiler_params=pltpu.CompilerParams(vmem_limit_bytes=SCOPED),
            name="finish",
        )(*[in_vmem(p) for p in (scores, *parts)])

    if n_dev == GROUP:
        return finish(*group_pass(packet))

    def next_group(x):
        return lax.ppermute(x, "exp", [(i, (i + GROUP) % n_dev) for i in range(n_dev)])

    def step(carry, _):
        mine, total = carry
        total = call(total_kernel, [space(rows, jnp.float32)], [total, *group_pass(mine)[1]])[0]
        return (next_group(mine), next_group(total)), None

    start = (packet, jnp.zeros((rows, lat), jnp.float32))
    (_, total), _ = lax.scan(step, start, None, length=n_dev // GROUP)
    columns = lax.all_gather(router, "exp", axis=1, tiled=True)
    logits = jnp.dot(latent_in, columns, preferred_element_type=jnp.float32)
    labels = jnp.arange(n_dev * local, dtype=jnp.int32)
    mask = jnp.any(routes[:, :, None] == labels[None, None, :], axis=1)
    scores = jnp.sum(jnp.where(mask, jax.nn.sigmoid(logits), 0.0), axis=1, keepdims=True) * SCALE
    return finish(jnp.broadcast_to(scores, (rows, TAIL)), [total])


def solution(mesh):
    placed = (
        P(("grp", "exp"), None),
        P(("grp", "exp"), None),
        P(None, "exp"),
        P("exp", None, None),
        P("exp", None, None),
    )
    return jax.shard_map(
        on_device, mesh=mesh, in_specs=placed, out_specs=P(("grp", "exp"), None), check_vma=False
    )
```

```python
import functools

import jax
import jax.numpy as jnp
from jax import lax
from jax.experimental import pallas as pl
from jax.experimental.pallas import tpu as pltpu
from jax.sharding import PartitionSpec as P

GROUP = 16
SCOPED = 8 * 1024 * 1024
TAIL = 128
LINE = 16
SCALE = 2.0**40
STEP = 256
PIECE = 256


def pack_kernel(ids_hbm, row_hbm, router_hbm, out_ref, ids_ref, router_ref, sems):
    rows, lat = row_hbm.shape
    local = router_hbm.shape[0]
    top = ids_hbm.shape[0]
    copies = [
        pltpu.make_async_copy(ids_hbm, ids_ref, sems.at[0]),
        pltpu.make_async_copy(router_hbm, router_ref, sems.at[1]),
        pltpu.make_async_copy(row_hbm, out_ref.at[:, pl.ds(0, lat)], sems.at[2]),
    ]
    for copy in copies:
        copy.start()
    copies[0].wait()
    copies[1].wait()
    ids = ids_ref[...].astype(jnp.float32)
    router = router_ref[...].astype(jnp.float32)
    lines = [jnp.concatenate([ids, jnp.full((top, TAIL - rows), -1.0, jnp.float32)], axis=1)]
    lines.append(jnp.full((LINE - top, TAIL), -1.0, jnp.float32))
    for e in range(local):
        for c in range(0, lat, TAIL):
            lines.append(router[e : e + 1, c : c + TAIL])
    lines.append(jnp.full((rows - LINE - local * lat // TAIL, TAIL), -1.0, jnp.float32))
    out_ref[:, lat:] = jnp.concatenate(lines, axis=0).astype(jnp.bfloat16)
    copies[2].wait()


def load_kernel(router_hbm, up_hbm, down_hbm, columns_ref, up_ref, down_ref, router_ref, sems):
    get_router = pltpu.make_async_copy(router_hbm, router_ref, sems.at[0])
    get_router.start()
    copies = []
    for src, dst in ((up_hbm, up_ref), (down_hbm, down_ref)):
        for e in range(src.shape[0]):
            for r in range(0, src.shape[1], PIECE):
                at = (e, pl.ds(r, PIECE))
                copies.append(pltpu.make_async_copy(src.at[at], dst.at[at], sems.at[1 + len(copies)]))
    for copy in copies:
        copy.start()
    get_router.wait()
    local, lat = router_ref.shape
    wide = jnp.concatenate(
        [router_ref[...].astype(jnp.float32), jnp.zeros((TAIL - local, lat), jnp.float32)], axis=0
    )
    columns_ref[...] = wide.T.astype(jnp.bfloat16)
    for copy in copies:
        copy.wait()


def expert_kernel(count, *refs):
    blocks, refs = refs[: 4 * count], refs[4 * count :]
    (columns_ref, up_ref, down_ref), refs = refs[:3], refs[3:]
    keep_refs, refs = refs[:count], refs[count:]
    send_refs, (packed_ref, inner_ref, result_ref) = refs[: 2 * count], refs[2 * count :]
    rows, lat = blocks[0].shape[0], blocks[0].shape[1] - TAIL
    half = 2 * rows
    local, eff, _ = down_ref.shape
    slots = packed_ref.shape[1] // count

    def put(i, lanes, value):
        keep_refs[i][:, lanes] = value[:half]
        for j, ref in enumerate(send_refs[2 * i : 2 * i + 2]):
            ref[:, lanes] = value[half + j * rows : half + (j + 1) * rows].astype(jnp.bfloat16)

    def logits_of(values):
        return jnp.dot(values, columns_ref[...], preferred_element_type=jnp.float32)

    size = 2 * half
    row = lax.broadcasted_iota(jnp.int32, (size, size), 0)
    col = lax.broadcasted_iota(jnp.int32, (size, size), 1)
    before = jnp.where(col < row, 1.0, 0.0).astype(jnp.bfloat16)
    after = jnp.where(row < col, 1.0, 0.0).astype(jnp.bfloat16)
    line = lax.broadcasted_iota(jnp.int32, (LINE, size), 0)
    slot = lax.broadcasted_iota(jnp.int32, (size, slots), 1).astype(jnp.float32)
    slot_t = lax.broadcasted_iota(jnp.int32, (slots, size), 0).astype(jnp.float32)
    labels = [(lax.axis_index("exp") * local + e).astype(jnp.float32) for e in range(local)]
    spreads = []
    for i in range(count):
        batch = blocks[4 * i : 4 * i + 4]
        x = jnp.concatenate([ref[:, :lat] for ref in batch], axis=0)
        ids_t = jnp.concatenate([ref[:LINE, lat:].astype(jnp.float32)[:, :rows] for ref in batch], axis=1)
        masks_t = [jnp.max(jnp.where(ids_t == label, 1.0, 0.0), axis=0, keepdims=True) for label in labels]
        marks_t = jnp.zeros((LINE, size), jnp.float32)
        for e in range(local):
            marks_t = jnp.where(line == e, masks_t[e], marks_t)
        marks = jnp.concatenate([marks_t, jnp.zeros((TAIL - LINE, size), jnp.float32)], axis=0).T
        place_t = jnp.dot(marks_t.astype(jnp.bfloat16), after, preferred_element_type=jnp.float32)
        place = jnp.dot(before, marks.astype(jnp.bfloat16), preferred_element_type=jnp.float32)
        gather = jnp.concatenate(
            [
                jnp.where((slot_t == place_t[e : e + 1]) & (masks_t[e] > 0.0), 1.0, 0.0)
                for e in range(local)
            ],
            axis=0,
        ).astype(jnp.bfloat16)
        packed = jnp.dot(gather, x, preferred_element_type=jnp.float32).astype(jnp.bfloat16)
        spread = jnp.concatenate(
            [jnp.where((slot == place[:, e : e + 1]) & (marks[:, e : e + 1] > 0.0), 1.0, 0.0) for e in range(local)],
            axis=1,
        ).astype(jnp.bfloat16)
        for e in range(local):
            packed_ref[e, i * slots : (i + 1) * slots, :] = packed[e * slots : (e + 1) * slots]
        spreads.append(spread)
    for e in range(local):
        chosen = packed_ref[e]
        score = jax.nn.sigmoid(logits_of(chosen)[:, e : e + 1]) * SCALE
        for c in range(0, eff, STEP):
            gate = jnp.dot(chosen, up_ref[e, :, c : c + STEP], preferred_element_type=jnp.float32)
            up = jnp.dot(chosen, up_ref[e, :, eff + c : eff + c + STEP], preferred_element_type=jnp.float32)
            inner_ref[e, :, c : c + STEP] = (gate / (1.0 + jnp.exp(-gate)) * up * score).astype(jnp.bfloat16)
    for e in range(local):
        result = jnp.dot(inner_ref[e], down_ref[e], preferred_element_type=jnp.float32).astype(jnp.bfloat16)
        for i in range(count):
            result_ref[i, e * slots : (e + 1) * slots, :] = result[i * slots : (i + 1) * slots]
    for i in range(count):
        for c in range(0, lat, STEP):
            part = jnp.dot(spreads[i], result_ref[i, :, c : c + STEP], preferred_element_type=jnp.float32)
            put(i, slice(c, c + STEP), part)


def tie_kernel():
    pass


def fold_kernel(mine_ref, came_a_ref, came_b_ref, keep_ref, send_ref):
    rows = keep_ref.shape[0]
    keep_ref[...] = mine_ref[:rows] + came_a_ref[...].astype(jnp.float32)
    send_ref[...] = (mine_ref[rows:] + came_b_ref[...].astype(jnp.float32)).astype(jnp.bfloat16)


def add_kernel(mine_ref, *refs):
    total = mine_ref[...]
    for ref in refs[:-1]:
        total = total + ref[...].astype(jnp.float32)
    refs[-1][...] = total.astype(jnp.bfloat16)


def total_kernel(*refs):
    total_ref = refs[-1]
    total = refs[0][...]
    for ref in refs[1:-1]:
        total = total + ref[...].astype(jnp.float32)
    total_ref[...] = total


def scores_kernel(mine_ref, *refs):
    *packet_refs, out_ref, lines_ref = refs
    rows, lat = mine_ref.shape[0], mine_ref.shape[1] - TAIL
    chunks = lat // TAIL
    height = lines_ref.shape[0] // len(packet_refs)
    local = height // chunks
    for i, ref in enumerate(packet_refs):
        lines_ref[i * height : (i + 1) * height, :] = ref[LINE : LINE + height, lat:].astype(jnp.float32)
    number = len(packet_refs) * local
    logits = jnp.zeros((number, rows), jnp.float32)
    for c in range(chunks):
        columns = lines_ref[pl.ds(c, number, stride=chunks), :].astype(jnp.bfloat16)
        logits = logits + lax.dot_general(
            columns,
            mine_ref[:, c * TAIL : (c + 1) * TAIL],
            (((1,), (1,)), ((), ())),
            preferred_element_type=jnp.float32,
        )
    at = lax.broadcasted_iota(jnp.int32, (number, rows), 0)
    label = ((lax.axis_index("exp") ^ (at // local)) * local + at % local).astype(jnp.float32)
    ids = mine_ref[:LINE, lat:].astype(jnp.float32)[:, :rows]
    mask = jnp.zeros((number, rows), jnp.float32)
    for k in range(LINE):
        mask = jnp.where(ids[k : k + 1] == label, 1.0, mask)
    total = jnp.sum(jax.nn.sigmoid(logits) * (mask * SCALE), axis=0, keepdims=True)
    total = jnp.broadcast_to(total, (TAIL, rows))
    total = jnp.concatenate([total, jnp.ones((TAIL, TAIL - rows), jnp.float32)], axis=1)
    out_ref[...] = total.T[:rows]


def finish_kernel(scores_ref, *refs):
    total = refs[0][...]
    for ref in refs[1:-1]:
        total = total + ref[...].astype(jnp.float32)
    refs[-1][...] = (total / scores_ref[:, :1]).astype(jnp.bfloat16)


def in_vmem(x):
    return pltpu.with_memory_space_constraint(x, pltpu.VMEM)


def in_hbm(x):
    return pltpu.with_memory_space_constraint(x, pltpu.HBM)


VMEM = pl.BlockSpec(memory_space=pltpu.VMEM)
ANY = pl.BlockSpec(memory_space=pl.ANY)


def call(kernel, outs, args=(), deps=(), chain=(), hbm=(), scratch=()):
    plain = getattr(kernel, "func", kernel)
    reads_chain = plain is expert_kernel
    n_in = len(args) + len(hbm)
    n_skip = n_in + len(deps)
    n_outs = n_skip + len(chain)

    def body(*refs):
        kernel(*refs[:n_in], *refs[n_outs : n_outs + len(outs)], *refs[n_outs + len(outs) + len(chain) :])

    def body_with_chain(*refs):
        kernel(
            *refs[:n_in],
            *refs[n_skip:n_outs],
            *refs[n_outs : n_outs + len(outs)],
            *refs[n_outs + len(outs) + len(chain) :],
        )

    specs = [VMEM] * len(args)
    specs += [ANY] * (len(hbm) + len(deps)) + [VMEM] * len(chain)
    operands = [in_vmem(a) for a in args] + [in_hbm(h) for h in hbm]
    operands += [in_vmem(x) for x in (*deps, *chain)]
    return pl.pallas_call(
        body_with_chain if reads_chain else body,
        out_shape=list(outs) + [pltpu.VMEM(x.shape, x.dtype) for x in chain],
        in_specs=specs,
        out_specs=[VMEM] * (len(outs) + len(chain)),
        scratch_shapes=list(scratch),
        compiler_params=pltpu.CompilerParams(vmem_limit_bytes=SCOPED),
        cost_estimate=pl.CostEstimate(flops=0, bytes_accessed=10_000, transcendentals=0),
        input_output_aliases={n_skip + i: len(outs) + i for i in range(len(chain))},
        name=plain.__name__.removesuffix("_kernel"),
    )(*operands)


def on_device(latent_in, routes, router, gate_up, expert_down):
    n_dev = lax.axis_size("exp")
    local = gate_up.shape[0]
    eff = expert_down.shape[1]
    rows, lat = latent_in.shape
    wide = lat + TAIL

    def swap(x, bits):
        return lax.ppermute(x, "exp", [(i, i ^ bits) for i in range(n_dev)])

    def space(height, dtype):
        return pltpu.VMEM((height, lat), dtype)

    def weights(dep):
        return call(
            load_kernel,
            [
                pltpu.VMEM((lat, TAIL), jnp.bfloat16),
                pltpu.VMEM(gate_up.shape, gate_up.dtype),
                pltpu.VMEM(expert_down.shape, expert_down.dtype),
            ],
            deps=[dep],
            hbm=[router.T, gate_up, expert_down],
            scratch=[
                pltpu.VMEM((local, lat), jnp.bfloat16),
                pltpu.SemaphoreType.DMA((1 + local * (lat + eff) // PIECE,)),
            ],
        )

    bound = 2 * ((rows * routes.shape[1] + local * n_dev - 1) // (local * n_dev))
    slots = 4 * bound

    def group_pass(mine):
        held = weights(mine)

        def step(kernel, outs, args=(), deps=(), hand_on=(), **more):
            nonlocal held
            result = call(kernel, outs, args, deps, [*held, *hand_on], **more)
            held = result[len(outs) : len(outs) + len(held)]
            return result[: len(outs)] + result[len(outs) + len(held) :]

        def tie(x, deps=()):
            return step(tie_kernel, [], deps=deps, hand_on=[x])[0]

        other, keep, send, came, fold_keep, fold_send, y_came, far = {}, {}, {}, {}, {}, {}, {}, {}

        def gather(k, deps=()):
            other[k] = tie(swap(block[k], 2), deps)

        def compute(*ks):
            count = len(ks)
            blocks = []
            for k in ks:
                near = [block[k], other[k]]
                far[k] = far.get(k) or [swap(one, 1) for one in near]
                blocks += near + far[k]
            result = step(
                functools.partial(expert_kernel, count),
                [space(2 * rows, jnp.float32)] * count + [space(rows, jnp.bfloat16)] * (2 * count),
                blocks,
                scratch=[
                    pltpu.VMEM((local, count * slots, lat), jnp.bfloat16),
                    pltpu.VMEM((local, count * slots, eff), jnp.bfloat16),
                    pltpu.VMEM((count, local * slots, lat), jnp.bfloat16),
                ],
            )
            for i, k in enumerate(ks):
                keep[k] = result[i]
                came[k] = [swap(part, 1) for part in result[count + 2 * i : count + 2 * i + 2]]

        def reduce_core(k, deps=()):
            fold_keep[k], fold_send[k] = step(
                fold_kernel, [space(rows, jnp.float32), space(rows, jnp.bfloat16)], [keep[k], *came[k]], deps
            )
            y_came[k] = swap(fold_send[k], 2)

        def reduce_y(k, *more):
            return step(add_kernel, [space(rows, jnp.bfloat16)], [fold_keep[k], y_came[k], *more])[0]

        z_2, z_1, y_0 = swap(mine, 8), swap(mine, 4), swap(mine, 2)
        block = {0: mine, 2: tie(z_2), 1: z_1}
        block[3] = swap(block[2], 4)
        other[0] = y_0
        far[0] = [swap(mine, 1), swap(y_0, 1)]
        gather(2, [block[1], block[3], far[0][0]])
        gather(1, [far[0][1]])
        compute(2)
        gather(3, came[2])
        reduce_core(2)
        compute(3)
        other[0] = tie(other[0], [y_came[2]])
        reduce_core(3)
        compute(1, 0)
        z_3 = swap(reduce_y(3), 4)
        reduce_core(1)
        reduce_core(0)
        scores = None
        if n_dev == GROUP:
            packets = [p for k in range(4) for p in (block[k], far[k][0], other[k], far[k][1])]
            scores = step(
                scores_kernel,
                [pltpu.VMEM((rows, TAIL), jnp.float32)],
                [mine, *packets],
                scratch=[pltpu.VMEM((n_dev * local * lat // TAIL, TAIL), jnp.float32)],
            )[0]
        z_2 = swap(reduce_y(2, z_3), 8)
        z_1 = swap(reduce_y(1), 4)
        return scores, (fold_keep[0], z_2, z_1, y_came[0])

    packet = call(
        pack_kernel,
        [pltpu.VMEM((rows, wide), jnp.bfloat16)],
        hbm=[routes.T, latent_in, router.T],
        scratch=[
            pltpu.VMEM(routes.shape[::-1], routes.dtype),
            pltpu.VMEM((local, lat), jnp.bfloat16),
            pltpu.SemaphoreType.DMA((3,)),
        ],
    )[0]

    def finish(scores, parts):
        return pl.pallas_call(
            finish_kernel,
            out_shape=jax.ShapeDtypeStruct((rows, lat), jnp.bfloat16),
            in_specs=[VMEM] * (1 + len(parts)),
            out_specs=VMEM,
            compiler_params=pltpu.CompilerParams(vmem_limit_bytes=SCOPED),
            name="finish",
        )(*[in_vmem(p) for p in (scores, *parts)])

    if n_dev == GROUP:
        return finish(*group_pass(packet))

    def next_group(x):
        return lax.ppermute(x, "exp", [(i, (i + GROUP) % n_dev) for i in range(n_dev)])

    def step(carry, _):
        mine, total = carry
        total = call(total_kernel, [space(rows, jnp.float32)], [total, *group_pass(mine)[1]])[0]
        return (next_group(mine), next_group(total)), None

    start = (packet, jnp.zeros((rows, lat), jnp.float32))
    (_, total), _ = lax.scan(step, start, None, length=n_dev // GROUP)
    columns = lax.all_gather(router, "exp", axis=1, tiled=True)
    logits = jnp.dot(latent_in, columns, preferred_element_type=jnp.float32)
    labels = jnp.arange(n_dev * local, dtype=jnp.int32)
    mask = jnp.any(routes[:, :, None] == labels[None, None, :], axis=1)
    scores = jnp.sum(jnp.where(mask, jax.nn.sigmoid(logits), 0.0), axis=1, keepdims=True) * SCALE
    return finish(jnp.broadcast_to(scores, (rows, TAIL)), [total])


def solution(mesh):
    placed = (
        P(("grp", "exp"), None),
        P(("grp", "exp"), None),
        P(None, "exp"),
        P("exp", None, None),
        P("exp", None, None),
    )
    return jax.shard_map(
        on_device, mesh=mesh, in_specs=placed, out_specs=P(("grp", "exp"), None), check_vma=False
    )
```

```python
import functools

import jax
import jax.numpy as jnp
from jax import lax
from jax.experimental import pallas as pl
from jax.experimental.pallas import tpu as pltpu
from jax.sharding import PartitionSpec as P

GROUP = 16
SCOPED = 8 * 1024 * 1024
TAIL = 128
LINE = 16
SCALE = 2.0**40
STEP = 512
PIECE = 256


def pack_kernel(ids_hbm, row_hbm, router_hbm, out_ref, ids_ref, router_ref, sems):
    rows, lat = row_hbm.shape
    local = router_hbm.shape[0]
    top = ids_hbm.shape[0]
    copies = [
        pltpu.make_async_copy(ids_hbm, ids_ref, sems.at[0]),
        pltpu.make_async_copy(router_hbm, router_ref, sems.at[1]),
        pltpu.make_async_copy(row_hbm, out_ref.at[:, pl.ds(0, lat)], sems.at[2]),
    ]
    for copy in copies:
        copy.start()
    copies[0].wait()
    copies[1].wait()
    ids = ids_ref[...].astype(jnp.float32)
    router = router_ref[...].astype(jnp.float32)
    lines = [jnp.concatenate([ids, jnp.full((top, TAIL - rows), -1.0, jnp.float32)], axis=1)]
    lines.append(jnp.full((LINE - top, TAIL), -1.0, jnp.float32))
    for e in range(local):
        for c in range(0, lat, TAIL):
            lines.append(router[e : e + 1, c : c + TAIL])
    lines.append(jnp.full((rows - LINE - local * lat // TAIL, TAIL), -1.0, jnp.float32))
    out_ref[:, lat:] = jnp.concatenate(lines, axis=0).astype(jnp.bfloat16)
    copies[2].wait()


def load_kernel(router_hbm, up_hbm, down_hbm, columns_ref, up_ref, down_ref, router_ref, sems):
    get_router = pltpu.make_async_copy(router_hbm, router_ref, sems.at[0])
    get_router.start()
    copies = []
    for src, dst in ((up_hbm, up_ref), (down_hbm, down_ref)):
        for e in range(src.shape[0]):
            for r in range(0, src.shape[1], PIECE):
                at = (e, pl.ds(r, PIECE))
                copies.append(pltpu.make_async_copy(src.at[at], dst.at[at], sems.at[1 + len(copies)]))
    for copy in copies:
        copy.start()
    get_router.wait()
    local, lat = router_ref.shape
    wide = jnp.concatenate(
        [router_ref[...].astype(jnp.float32), jnp.zeros((TAIL - local, lat), jnp.float32)], axis=0
    )
    columns_ref[...] = wide.T.astype(jnp.bfloat16)
    for copy in copies:
        copy.wait()


def expert_kernel(count, *refs):
    blocks, refs = refs[: 4 * count], refs[4 * count :]
    (columns_ref, up_ref, down_ref), refs = refs[:3], refs[3:]
    keep_refs, refs = refs[:count], refs[count:]
    send_refs, (packed_ref, inner_ref, result_ref) = refs[: 2 * count], refs[2 * count :]
    rows, lat = blocks[0].shape[0], blocks[0].shape[1] - TAIL
    half = 2 * rows
    local, eff, _ = down_ref.shape
    slots = packed_ref.shape[1] // count

    def put(i, lanes, value):
        keep_refs[i][:, lanes] = value[:half]
        for j, ref in enumerate(send_refs[2 * i : 2 * i + 2]):
            ref[:, lanes] = value[half + j * rows : half + (j + 1) * rows].astype(jnp.bfloat16)

    def logits_of(values):
        return jnp.dot(values, columns_ref[...], preferred_element_type=jnp.float32)

    size = 2 * half
    row = lax.broadcasted_iota(jnp.int32, (size, size), 0)
    col = lax.broadcasted_iota(jnp.int32, (size, size), 1)
    before = jnp.where(col < row, 1.0, 0.0).astype(jnp.bfloat16)
    after = jnp.where(row < col, 1.0, 0.0).astype(jnp.bfloat16)
    line = lax.broadcasted_iota(jnp.int32, (LINE, size), 0)
    slot = lax.broadcasted_iota(jnp.int32, (size, slots), 1).astype(jnp.float32)
    slot_t = lax.broadcasted_iota(jnp.int32, (slots, size), 0).astype(jnp.float32)
    labels = [(lax.axis_index("exp") * local + e).astype(jnp.float32) for e in range(local)]
    spreads = []
    for i in range(count):
        batch = blocks[4 * i : 4 * i + 4]
        x = jnp.concatenate([ref[:, :lat] for ref in batch], axis=0)
        ids_t = jnp.concatenate([ref[:LINE, lat:].astype(jnp.float32)[:, :rows] for ref in batch], axis=1)
        masks_t = [jnp.max(jnp.where(ids_t == label, 1.0, 0.0), axis=0, keepdims=True) for label in labels]
        marks_t = jnp.zeros((LINE, size), jnp.float32)
        for e in range(local):
            marks_t = jnp.where(line == e, masks_t[e], marks_t)
        marks = jnp.concatenate([marks_t, jnp.zeros((TAIL - LINE, size), jnp.float32)], axis=0).T
        place_t = jnp.dot(marks_t.astype(jnp.bfloat16), after, preferred_element_type=jnp.float32)
        place = jnp.dot(before, marks.astype(jnp.bfloat16), preferred_element_type=jnp.float32)
        gather = jnp.concatenate(
            [
                jnp.where((slot_t == place_t[e : e + 1]) & (masks_t[e] > 0.0), 1.0, 0.0)
                for e in range(local)
            ],
            axis=0,
        ).astype(jnp.bfloat16)
        packed = jnp.dot(gather, x, preferred_element_type=jnp.float32).astype(jnp.bfloat16)
        spread = jnp.concatenate(
            [jnp.where((slot == place[:, e : e + 1]) & (marks[:, e : e + 1] > 0.0), 1.0, 0.0) for e in range(local)],
            axis=1,
        ).astype(jnp.bfloat16)
        for e in range(local):
            packed_ref[e, i * slots : (i + 1) * slots, :] = packed[e * slots : (e + 1) * slots]
        spreads.append(spread)
    for e in range(local):
        chosen = packed_ref[e]
        score = jax.nn.sigmoid(logits_of(chosen)[:, e : e + 1]) * SCALE
        for c in range(0, eff, STEP):
            gate = jnp.dot(chosen, up_ref[e, :, c : c + STEP], preferred_element_type=jnp.float32)
            up = jnp.dot(chosen, up_ref[e, :, eff + c : eff + c + STEP], preferred_element_type=jnp.float32)
            inner_ref[e, :, c : c + STEP] = (gate / (1.0 + jnp.exp(-gate)) * up * score).astype(jnp.bfloat16)
    for e in range(local):
        result = jnp.dot(inner_ref[e], down_ref[e], preferred_element_type=jnp.float32).astype(jnp.bfloat16)
        for i in range(count):
            result_ref[i, e * slots : (e + 1) * slots, :] = result[i * slots : (i + 1) * slots]
    for i in range(count):
        for c in range(0, lat, STEP):
            part = jnp.dot(spreads[i], result_ref[i, :, c : c + STEP], preferred_element_type=jnp.float32)
            put(i, slice(c, c + STEP), part)


def tie_kernel():
    pass


def fold_kernel(mine_ref, came_a_ref, came_b_ref, keep_ref, send_ref):
    rows = keep_ref.shape[0]
    keep_ref[...] = mine_ref[:rows] + came_a_ref[...].astype(jnp.float32)
    send_ref[...] = (mine_ref[rows:] + came_b_ref[...].astype(jnp.float32)).astype(jnp.bfloat16)


def add_kernel(mine_ref, *refs):
    total = mine_ref[...]
    for ref in refs[:-1]:
        total = total + ref[...].astype(jnp.float32)
    refs[-1][...] = total.astype(jnp.bfloat16)


def total_kernel(*refs):
    total_ref = refs[-1]
    total = refs[0][...]
    for ref in refs[1:-1]:
        total = total + ref[...].astype(jnp.float32)
    total_ref[...] = total


def scores_kernel(mine_ref, *refs):
    *packet_refs, out_ref, lines_ref = refs
    rows, lat = mine_ref.shape[0], mine_ref.shape[1] - TAIL
    chunks = lat // TAIL
    height = lines_ref.shape[0] // len(packet_refs)
    local = height // chunks
    for i, ref in enumerate(packet_refs):
        lines_ref[i * height : (i + 1) * height, :] = ref[LINE : LINE + height, lat:].astype(jnp.float32)
    number = len(packet_refs) * local
    logits = jnp.zeros((number, rows), jnp.float32)
    for c in range(chunks):
        columns = lines_ref[pl.ds(c, number, stride=chunks), :].astype(jnp.bfloat16)
        logits = logits + lax.dot_general(
            columns,
            mine_ref[:, c * TAIL : (c + 1) * TAIL],
            (((1,), (1,)), ((), ())),
            preferred_element_type=jnp.float32,
        )
    at = lax.broadcasted_iota(jnp.int32, (number, rows), 0)
    label = ((lax.axis_index("exp") ^ (at // local)) * local + at % local).astype(jnp.float32)
    ids = mine_ref[:LINE, lat:].astype(jnp.float32)[:, :rows]
    mask = jnp.zeros((number, rows), jnp.float32)
    for k in range(LINE):
        mask = jnp.where(ids[k : k + 1] == label, 1.0, mask)
    total = jnp.sum(jax.nn.sigmoid(logits) * (mask * SCALE), axis=0, keepdims=True)
    total = jnp.broadcast_to(total, (TAIL, rows))
    total = jnp.concatenate([total, jnp.ones((TAIL, TAIL - rows), jnp.float32)], axis=1)
    out_ref[...] = total.T[:rows]


def finish_kernel(scores_ref, *refs):
    total = refs[0][...]
    for ref in refs[1:-1]:
        total = total + ref[...].astype(jnp.float32)
    refs[-1][...] = (total / scores_ref[:, :1]).astype(jnp.bfloat16)


def in_vmem(x):
    return pltpu.with_memory_space_constraint(x, pltpu.VMEM)


def in_hbm(x):
    return pltpu.with_memory_space_constraint(x, pltpu.HBM)


VMEM = pl.BlockSpec(memory_space=pltpu.VMEM)
ANY = pl.BlockSpec(memory_space=pl.ANY)


def call(kernel, outs, args=(), deps=(), chain=(), hbm=(), scratch=()):
    plain = getattr(kernel, "func", kernel)
    reads_chain = plain is expert_kernel
    n_in = len(args) + len(hbm)
    n_skip = n_in + len(deps)
    n_outs = n_skip + len(chain)

    def body(*refs):
        kernel(*refs[:n_in], *refs[n_outs : n_outs + len(outs)], *refs[n_outs + len(outs) + len(chain) :])

    def body_with_chain(*refs):
        kernel(
            *refs[:n_in],
            *refs[n_skip:n_outs],
            *refs[n_outs : n_outs + len(outs)],
            *refs[n_outs + len(outs) + len(chain) :],
        )

    specs = [VMEM] * len(args)
    specs += [ANY] * (len(hbm) + len(deps)) + [VMEM] * len(chain)
    operands = [in_vmem(a) for a in args] + [in_hbm(h) for h in hbm]
    operands += [in_vmem(x) for x in (*deps, *chain)]
    return pl.pallas_call(
        body_with_chain if reads_chain else body,
        out_shape=list(outs) + [pltpu.VMEM(x.shape, x.dtype) for x in chain],
        in_specs=specs,
        out_specs=[VMEM] * (len(outs) + len(chain)),
        scratch_shapes=list(scratch),
        compiler_params=pltpu.CompilerParams(vmem_limit_bytes=SCOPED),
        cost_estimate=pl.CostEstimate(flops=0, bytes_accessed=10_000, transcendentals=0),
        input_output_aliases={n_skip + i: len(outs) + i for i in range(len(chain))},
        name=plain.__name__.removesuffix("_kernel"),
    )(*operands)


def on_device(latent_in, routes, router, gate_up, expert_down):
    n_dev = lax.axis_size("exp")
    local = gate_up.shape[0]
    eff = expert_down.shape[1]
    rows, lat = latent_in.shape
    wide = lat + TAIL

    def swap(x, bits):
        return lax.ppermute(x, "exp", [(i, i ^ bits) for i in range(n_dev)])

    def space(height, dtype):
        return pltpu.VMEM((height, lat), dtype)

    def weights(dep):
        return call(
            load_kernel,
            [
                pltpu.VMEM((lat, TAIL), jnp.bfloat16),
                pltpu.VMEM(gate_up.shape, gate_up.dtype),
                pltpu.VMEM(expert_down.shape, expert_down.dtype),
            ],
            deps=[dep],
            hbm=[router.T, gate_up, expert_down],
            scratch=[
                pltpu.VMEM((local, lat), jnp.bfloat16),
                pltpu.SemaphoreType.DMA((1 + local * (lat + eff) // PIECE,)),
            ],
        )

    bound = 2 * ((rows * routes.shape[1] + local * n_dev - 1) // (local * n_dev))
    slots = 4 * bound

    def group_pass(mine):
        held = weights(mine)

        def step(kernel, outs, args=(), deps=(), hand_on=(), **more):
            nonlocal held
            result = call(kernel, outs, args, deps, [*held, *hand_on], **more)
            held = result[len(outs) : len(outs) + len(held)]
            return result[: len(outs)] + result[len(outs) + len(held) :]

        def tie(x, deps=()):
            return step(tie_kernel, [], deps=deps, hand_on=[x])[0]

        other, keep, send, came, fold_keep, fold_send, y_came, far = {}, {}, {}, {}, {}, {}, {}, {}

        def gather(k, deps=()):
            other[k] = tie(swap(block[k], 2), deps)

        def compute(*ks):
            count = len(ks)
            blocks = []
            for k in ks:
                near = [block[k], other[k]]
                far[k] = far.get(k) or [swap(one, 1) for one in near]
                blocks += near + far[k]
            result = step(
                functools.partial(expert_kernel, count),
                [space(2 * rows, jnp.float32)] * count + [space(rows, jnp.bfloat16)] * (2 * count),
                blocks,
                scratch=[
                    pltpu.VMEM((local, count * slots, lat), jnp.bfloat16),
                    pltpu.VMEM((local, count * slots, eff), jnp.bfloat16),
                    pltpu.VMEM((count, local * slots, lat), jnp.bfloat16),
                ],
            )
            for i, k in enumerate(ks):
                keep[k] = result[i]
                came[k] = [swap(part, 1) for part in result[count + 2 * i : count + 2 * i + 2]]

        def reduce_core(k, deps=()):
            fold_keep[k], fold_send[k] = step(
                fold_kernel, [space(rows, jnp.float32), space(rows, jnp.bfloat16)], [keep[k], *came[k]], deps
            )
            y_came[k] = swap(fold_send[k], 2)

        def reduce_y(k, *more):
            return step(add_kernel, [space(rows, jnp.bfloat16)], [fold_keep[k], y_came[k], *more])[0]

        z_2, z_1, y_0 = swap(mine, 8), swap(mine, 4), swap(mine, 2)
        block = {0: mine, 2: tie(z_2), 1: z_1}
        block[3] = swap(block[2], 4)
        other[0] = y_0
        far[0] = [swap(mine, 1), swap(y_0, 1)]
        gather(2, [block[1], block[3], y_0])
        gather(1)
        compute(2)
        gather(3, came[2])
        reduce_core(2, far[0])
        compute(3)
        other[0] = tie(other[0], [y_came[2]])
        reduce_core(3)
        compute(1, 0)
        z_3 = swap(reduce_y(3), 4)
        reduce_core(1)
        reduce_core(0)
        scores = None
        if n_dev == GROUP:
            packets = [p for k in range(4) for p in (block[k], far[k][0], other[k], far[k][1])]
            scores = step(
                scores_kernel,
                [pltpu.VMEM((rows, TAIL), jnp.float32)],
                [mine, *packets],
                scratch=[pltpu.VMEM((n_dev * local * lat // TAIL, TAIL), jnp.float32)],
            )[0]
        z_2 = swap(reduce_y(2, z_3), 8)
        z_1 = swap(reduce_y(1), 4)
        return scores, (fold_keep[0], z_2, z_1, y_came[0])

    packet = call(
        pack_kernel,
        [pltpu.VMEM((rows, wide), jnp.bfloat16)],
        hbm=[routes.T, latent_in, router.T],
        scratch=[
            pltpu.VMEM(routes.shape[::-1], routes.dtype),
            pltpu.VMEM((local, lat), jnp.bfloat16),
            pltpu.SemaphoreType.DMA((3,)),
        ],
    )[0]

    def finish(scores, parts):
        return pl.pallas_call(
            finish_kernel,
            out_shape=jax.ShapeDtypeStruct((rows, lat), jnp.bfloat16),
            in_specs=[VMEM] * (1 + len(parts)),
            out_specs=VMEM,
            compiler_params=pltpu.CompilerParams(vmem_limit_bytes=SCOPED),
            name="finish",
        )(*[in_vmem(p) for p in (scores, *parts)])

    if n_dev == GROUP:
        return finish(*group_pass(packet))

    def next_group(x):
        return lax.ppermute(x, "exp", [(i, (i + GROUP) % n_dev) for i in range(n_dev)])

    def step(carry, _):
        mine, total = carry
        total = call(total_kernel, [space(rows, jnp.float32)], [total, *group_pass(mine)[1]])[0]
        return (next_group(mine), next_group(total)), None

    start = (packet, jnp.zeros((rows, lat), jnp.float32))
    (_, total), _ = lax.scan(step, start, None, length=n_dev // GROUP)
    columns = lax.all_gather(router, "exp", axis=1, tiled=True)
    logits = jnp.dot(latent_in, columns, preferred_element_type=jnp.float32)
    labels = jnp.arange(n_dev * local, dtype=jnp.int32)
    mask = jnp.any(routes[:, :, None] == labels[None, None, :], axis=1)
    scores = jnp.sum(jnp.where(mask, jax.nn.sigmoid(logits), 0.0), axis=1, keepdims=True) * SCALE
    return finish(jnp.broadcast_to(scores, (rows, TAIL)), [total])


def solution(mesh):
    placed = (
        P(("grp", "exp"), None),
        P(("grp", "exp"), None),
        P(None, "exp"),
        P("exp", None, None),
        P("exp", None, None),
    )
    return jax.shard_map(
        on_device, mesh=mesh, in_specs=placed, out_specs=P(("grp", "exp"), None), check_vma=False
    )
```

```python
import functools

import jax
import jax.numpy as jnp
from jax import lax
from jax.experimental import pallas as pl
from jax.experimental.pallas import tpu as pltpu
from jax.sharding import PartitionSpec as P

GROUP = 16
SCOPED = 8 * 1024 * 1024
TAIL = 128
LINE = 16
SCALE = 2.0**40
STEP = 512
PIECE = 256


def pack_kernel(ids_hbm, row_hbm, router_hbm, out_ref, ids_ref, router_ref, sems):
    rows, lat = row_hbm.shape
    local = router_hbm.shape[0]
    top = ids_hbm.shape[0]
    copies = [
        pltpu.make_async_copy(ids_hbm, ids_ref, sems.at[0]),
        pltpu.make_async_copy(router_hbm, router_ref, sems.at[1]),
        pltpu.make_async_copy(row_hbm, out_ref.at[:, pl.ds(0, lat)], sems.at[2]),
    ]
    for copy in copies:
        copy.start()
    copies[0].wait()
    copies[1].wait()
    ids = ids_ref[...].astype(jnp.float32)
    router = router_ref[...].astype(jnp.float32)
    lines = [jnp.concatenate([ids, jnp.full((top, TAIL - rows), -1.0, jnp.float32)], axis=1)]
    lines.append(jnp.full((LINE - top, TAIL), -1.0, jnp.float32))
    for e in range(local):
        for c in range(0, lat, TAIL):
            lines.append(router[e : e + 1, c : c + TAIL])
    lines.append(jnp.full((rows - LINE - local * lat // TAIL, TAIL), -1.0, jnp.float32))
    out_ref[:, lat:] = jnp.concatenate(lines, axis=0).astype(jnp.bfloat16)
    copies[2].wait()


def load_kernel(router_hbm, up_hbm, down_hbm, columns_ref, up_ref, down_ref, router_ref, sems):
    get_router = pltpu.make_async_copy(router_hbm, router_ref, sems.at[0])
    get_router.start()
    copies = []
    for src, dst in ((up_hbm, up_ref), (down_hbm, down_ref)):
        for e in range(src.shape[0]):
            for r in range(0, src.shape[1], PIECE):
                at = (e, pl.ds(r, PIECE))
                copies.append(pltpu.make_async_copy(src.at[at], dst.at[at], sems.at[1 + len(copies)]))
    for copy in copies:
        copy.start()
    get_router.wait()
    local, lat = router_ref.shape
    wide = jnp.concatenate(
        [router_ref[...].astype(jnp.float32), jnp.zeros((TAIL - local, lat), jnp.float32)], axis=0
    )
    columns_ref[...] = wide.T.astype(jnp.bfloat16)
    for copy in copies:
        copy.wait()


def expert_kernel(count, *refs):
    blocks, refs = refs[: 4 * count], refs[4 * count :]
    (columns_ref, up_ref, down_ref), refs = refs[:3], refs[3:]
    keep_refs, refs = refs[:count], refs[count:]
    send_refs, (packed_ref, inner_ref, result_ref) = refs[: 2 * count], refs[2 * count :]
    rows, lat = blocks[0].shape[0], blocks[0].shape[1] - TAIL
    half = 2 * rows
    local, eff, _ = down_ref.shape
    slots = packed_ref.shape[1] // count

    def put(i, lanes, value):
        keep_refs[i][:, lanes] = value[:half]
        for j, ref in enumerate(send_refs[2 * i : 2 * i + 2]):
            ref[:, lanes] = value[half + j * rows : half + (j + 1) * rows].astype(jnp.bfloat16)

    def logits_of(values):
        return jnp.dot(values, columns_ref[...], preferred_element_type=jnp.float32)

    size = 2 * half
    row = lax.broadcasted_iota(jnp.int32, (size, size), 0)
    col = lax.broadcasted_iota(jnp.int32, (size, size), 1)
    before = jnp.where(col < row, 1.0, 0.0).astype(jnp.bfloat16)
    after = jnp.where(row < col, 1.0, 0.0).astype(jnp.bfloat16)
    line = lax.broadcasted_iota(jnp.int32, (LINE, size), 0)
    slot = lax.broadcasted_iota(jnp.int32, (size, slots), 1).astype(jnp.float32)
    slot_t = lax.broadcasted_iota(jnp.int32, (slots, size), 0).astype(jnp.float32)
    labels = [(lax.axis_index("exp") * local + e).astype(jnp.float32) for e in range(local)]
    spreads = []
    for i in range(count):
        batch = blocks[4 * i : 4 * i + 4]
        x = jnp.concatenate([ref[:, :lat] for ref in batch], axis=0)
        ids_t = jnp.concatenate([ref[:LINE, lat:].astype(jnp.float32)[:, :rows] for ref in batch], axis=1)
        masks_t = [jnp.max(jnp.where(ids_t == label, 1.0, 0.0), axis=0, keepdims=True) for label in labels]
        marks_t = jnp.zeros((LINE, size), jnp.float32)
        for e in range(local):
            marks_t = jnp.where(line == e, masks_t[e], marks_t)
        marks = jnp.concatenate([marks_t, jnp.zeros((TAIL - LINE, size), jnp.float32)], axis=0).T
        place_t = jnp.dot(marks_t.astype(jnp.bfloat16), after, preferred_element_type=jnp.float32)
        place = jnp.dot(before, marks.astype(jnp.bfloat16), preferred_element_type=jnp.float32)
        gather = jnp.concatenate(
            [
                jnp.where((slot_t == place_t[e : e + 1]) & (masks_t[e] > 0.0), 1.0, 0.0)
                for e in range(local)
            ],
            axis=0,
        ).astype(jnp.bfloat16)
        packed = jnp.dot(gather, x, preferred_element_type=jnp.float32).astype(jnp.bfloat16)
        spread = jnp.concatenate(
            [jnp.where((slot == place[:, e : e + 1]) & (marks[:, e : e + 1] > 0.0), 1.0, 0.0) for e in range(local)],
            axis=1,
        ).astype(jnp.bfloat16)
        for e in range(local):
            packed_ref[e, i * slots : (i + 1) * slots, :] = packed[e * slots : (e + 1) * slots]
        spreads.append(spread)
    for e in range(local):
        chosen = packed_ref[e]
        score = jax.nn.sigmoid(logits_of(chosen)[:, e : e + 1]) * SCALE
        for c in range(0, eff, STEP):
            gate = jnp.dot(chosen, up_ref[e, :, c : c + STEP], preferred_element_type=jnp.float32)
            up = jnp.dot(chosen, up_ref[e, :, eff + c : eff + c + STEP], preferred_element_type=jnp.float32)
            inner_ref[e, :, c : c + STEP] = (gate / (1.0 + jnp.exp(-gate)) * up * score).astype(jnp.bfloat16)
    for e in range(local):
        result = jnp.dot(inner_ref[e], down_ref[e], preferred_element_type=jnp.float32).astype(jnp.bfloat16)
        for i in range(count):
            result_ref[i, e * slots : (e + 1) * slots, :] = result[i * slots : (i + 1) * slots]
    for i in range(count):
        for c in range(0, lat, STEP):
            part = jnp.dot(spreads[i], result_ref[i, :, c : c + STEP], preferred_element_type=jnp.float32)
            put(i, slice(c, c + STEP), part)


def tie_kernel():
    pass


def fold_kernel(mine_ref, came_a_ref, came_b_ref, keep_ref, send_ref):
    rows = keep_ref.shape[0]
    keep_ref[...] = mine_ref[:rows] + came_a_ref[...].astype(jnp.float32)
    send_ref[...] = (mine_ref[rows:] + came_b_ref[...].astype(jnp.float32)).astype(jnp.bfloat16)


def add_kernel(mine_ref, *refs):
    total = mine_ref[...]
    for ref in refs[:-1]:
        total = total + ref[...].astype(jnp.float32)
    refs[-1][...] = total.astype(jnp.bfloat16)


def total_kernel(*refs):
    total_ref = refs[-1]
    total = refs[0][...]
    for ref in refs[1:-1]:
        total = total + ref[...].astype(jnp.float32)
    total_ref[...] = total


def scores_kernel(mine_ref, *refs):
    *packet_refs, out_ref, lines_ref = refs
    rows, lat = mine_ref.shape[0], mine_ref.shape[1] - TAIL
    chunks = lat // TAIL
    height = lines_ref.shape[0] // len(packet_refs)
    local = height // chunks
    for i, ref in enumerate(packet_refs):
        lines_ref[i * height : (i + 1) * height, :] = ref[LINE : LINE + height, lat:].astype(jnp.float32)
    number = len(packet_refs) * local
    logits = jnp.zeros((number, rows), jnp.float32)
    for c in range(chunks):
        columns = lines_ref[pl.ds(c, number, stride=chunks), :].astype(jnp.bfloat16)
        logits = logits + lax.dot_general(
            columns,
            mine_ref[:, c * TAIL : (c + 1) * TAIL],
            (((1,), (1,)), ((), ())),
            preferred_element_type=jnp.float32,
        )
    at = lax.broadcasted_iota(jnp.int32, (number, rows), 0)
    label = ((lax.axis_index("exp") ^ (at // local)) * local + at % local).astype(jnp.float32)
    ids = mine_ref[:LINE, lat:].astype(jnp.float32)[:, :rows]
    mask = jnp.zeros((number, rows), jnp.float32)
    for k in range(LINE):
        mask = jnp.where(ids[k : k + 1] == label, 1.0, mask)
    total = jnp.sum(jax.nn.sigmoid(logits) * (mask * SCALE), axis=0, keepdims=True)
    total = jnp.broadcast_to(total, (TAIL, rows))
    total = jnp.concatenate([total, jnp.ones((TAIL, TAIL - rows), jnp.float32)], axis=1)
    out_ref[...] = total.T[:rows]


def finish_kernel(scores_ref, *refs):
    total = refs[0][...]
    for ref in refs[1:-1]:
        total = total + ref[...].astype(jnp.float32)
    refs[-1][...] = (total / scores_ref[:, :1]).astype(jnp.bfloat16)


def in_vmem(x):
    return pltpu.with_memory_space_constraint(x, pltpu.VMEM)


def in_hbm(x):
    return pltpu.with_memory_space_constraint(x, pltpu.HBM)


VMEM = pl.BlockSpec(memory_space=pltpu.VMEM)
ANY = pl.BlockSpec(memory_space=pl.ANY)


def call(kernel, outs, args=(), deps=(), chain=(), hbm=(), scratch=()):
    plain = getattr(kernel, "func", kernel)
    reads_chain = plain is expert_kernel
    n_in = len(args) + len(hbm)
    n_skip = n_in + len(deps)
    n_outs = n_skip + len(chain)

    def body(*refs):
        kernel(*refs[:n_in], *refs[n_outs : n_outs + len(outs)], *refs[n_outs + len(outs) + len(chain) :])

    def body_with_chain(*refs):
        kernel(
            *refs[:n_in],
            *refs[n_skip:n_outs],
            *refs[n_outs : n_outs + len(outs)],
            *refs[n_outs + len(outs) + len(chain) :],
        )

    specs = [VMEM] * len(args)
    specs += [ANY] * (len(hbm) + len(deps)) + [VMEM] * len(chain)
    operands = [in_vmem(a) for a in args] + [in_hbm(h) for h in hbm]
    operands += [in_vmem(x) for x in (*deps, *chain)]
    return pl.pallas_call(
        body_with_chain if reads_chain else body,
        out_shape=list(outs) + [pltpu.VMEM(x.shape, x.dtype) for x in chain],
        in_specs=specs,
        out_specs=[VMEM] * (len(outs) + len(chain)),
        scratch_shapes=list(scratch),
        compiler_params=pltpu.CompilerParams(vmem_limit_bytes=SCOPED),
        cost_estimate=pl.CostEstimate(flops=0, bytes_accessed=10_000, transcendentals=0),
        input_output_aliases={n_skip + i: len(outs) + i for i in range(len(chain))},
        name=plain.__name__.removesuffix("_kernel"),
    )(*operands)


def on_device(latent_in, routes, router, gate_up, expert_down):
    n_dev = lax.axis_size("exp")
    local = gate_up.shape[0]
    eff = expert_down.shape[1]
    rows, lat = latent_in.shape
    wide = lat + TAIL

    def swap(x, bits):
        return lax.ppermute(x, "exp", [(i, i ^ bits) for i in range(n_dev)])

    def space(height, dtype):
        return pltpu.VMEM((height, lat), dtype)

    def weights(dep):
        return call(
            load_kernel,
            [
                pltpu.VMEM((lat, TAIL), jnp.bfloat16),
                pltpu.VMEM(gate_up.shape, gate_up.dtype),
                pltpu.VMEM(expert_down.shape, expert_down.dtype),
            ],
            deps=[dep],
            hbm=[router.T, gate_up, expert_down],
            scratch=[
                pltpu.VMEM((local, lat), jnp.bfloat16),
                pltpu.SemaphoreType.DMA((1 + local * (lat + eff) // PIECE,)),
            ],
        )

    bound = 2 * ((rows * routes.shape[1] + local * n_dev - 1) // (local * n_dev))
    slots = 4 * bound

    def group_pass(mine):
        held = weights(mine)

        def step(kernel, outs, args=(), deps=(), hand_on=(), **more):
            nonlocal held
            result = call(kernel, outs, args, deps, [*held, *hand_on], **more)
            held = result[len(outs) : len(outs) + len(held)]
            return result[: len(outs)] + result[len(outs) + len(held) :]

        def tie(x, deps=()):
            return step(tie_kernel, [], deps=deps, hand_on=[x])[0]

        other, keep, send, came, fold_keep, fold_send, y_came, far = {}, {}, {}, {}, {}, {}, {}, {}

        def gather(k, deps=()):
            other[k] = tie(swap(block[k], 2), deps)

        def compute(*ks):
            count = len(ks)
            blocks = []
            for k in ks:
                near = [block[k], other[k]]
                far[k] = far.get(k) or [swap(one, 1) for one in near]
                blocks += near + far[k]
            result = step(
                functools.partial(expert_kernel, count),
                [space(2 * rows, jnp.float32)] * count + [space(rows, jnp.bfloat16)] * (2 * count),
                blocks,
                scratch=[
                    pltpu.VMEM((local, count * slots, lat), jnp.bfloat16),
                    pltpu.VMEM((local, count * slots, eff), jnp.bfloat16),
                    pltpu.VMEM((count, local * slots, lat), jnp.bfloat16),
                ],
            )
            for i, k in enumerate(ks):
                keep[k] = result[i]
                came[k] = [swap(part, 1) for part in result[count + 2 * i : count + 2 * i + 2]]

        def reduce_core(k, deps=()):
            fold_keep[k], fold_send[k] = step(
                fold_kernel, [space(rows, jnp.float32), space(rows, jnp.bfloat16)], [keep[k], *came[k]], deps
            )
            y_came[k] = swap(fold_send[k], 2)

        def reduce_y(k, *more):
            return step(add_kernel, [space(rows, jnp.bfloat16)], [fold_keep[k], y_came[k], *more])[0]

        z_2, z_1, y_0 = swap(mine, 8), swap(mine, 4), swap(mine, 2)
        block = {0: mine, 2: tie(z_2), 1: z_1}
        block[3] = swap(block[2], 4)
        other[0] = y_0
        far[0] = [swap(mine, 1), swap(y_0, 1)]
        gather(2, [block[1], block[3], y_0])
        gather(1)
        compute(2)
        gather(3, came[2])
        reduce_core(2, far[0])
        compute(3)
        other[0] = tie(other[0], [y_came[2]])
        reduce_core(3)
        compute(1)
        z_3 = swap(reduce_y(3), 4)
        compute(0)
        reduce_core(1)
        z_2 = swap(reduce_y(2, z_3), 8)
        z_1 = swap(reduce_y(1), 4)
        reduce_core(0)
        scores = None
        if n_dev == GROUP:
            packets = [p for k in range(4) for p in (block[k], far[k][0], other[k], far[k][1])]
            scores = step(
                scores_kernel,
                [pltpu.VMEM((rows, TAIL), jnp.float32)],
                [mine, *packets],
                scratch=[pltpu.VMEM((n_dev * local * lat // TAIL, TAIL), jnp.float32)],
            )[0]
        keep_0 = call(tie_kernel, [], deps=[z_2], chain=[fold_keep[0]])[0]
        return scores, (keep_0, z_2, z_1, y_came[0])

    packet = call(
        pack_kernel,
        [pltpu.VMEM((rows, wide), jnp.bfloat16)],
        hbm=[routes.T, latent_in, router.T],
        scratch=[
            pltpu.VMEM(routes.shape[::-1], routes.dtype),
            pltpu.VMEM((local, lat), jnp.bfloat16),
            pltpu.SemaphoreType.DMA((3,)),
        ],
    )[0]

    def finish(scores, parts):
        return pl.pallas_call(
            finish_kernel,
            out_shape=jax.ShapeDtypeStruct((rows, lat), jnp.bfloat16),
            in_specs=[VMEM] * (1 + len(parts)),
            out_specs=VMEM,
            compiler_params=pltpu.CompilerParams(vmem_limit_bytes=SCOPED),
            name="finish",
        )(*[in_vmem(p) for p in (scores, *parts)])

    if n_dev == GROUP:
        return finish(*group_pass(packet))

    def next_group(x):
        return lax.ppermute(x, "exp", [(i, (i + GROUP) % n_dev) for i in range(n_dev)])

    def step(carry, _):
        mine, total = carry
        total = call(total_kernel, [space(rows, jnp.float32)], [total, *group_pass(mine)[1]])[0]
        return (next_group(mine), next_group(total)), None

    start = (packet, jnp.zeros((rows, lat), jnp.float32))
    (_, total), _ = lax.scan(step, start, None, length=n_dev // GROUP)
    columns = lax.all_gather(router, "exp", axis=1, tiled=True)
    logits = jnp.dot(latent_in, columns, preferred_element_type=jnp.float32)
    labels = jnp.arange(n_dev * local, dtype=jnp.int32)
    mask = jnp.any(routes[:, :, None] == labels[None, None, :], axis=1)
    scores = jnp.sum(jnp.where(mask, jax.nn.sigmoid(logits), 0.0), axis=1, keepdims=True) * SCALE
    return finish(jnp.broadcast_to(scores, (rows, TAIL)), [total])


def solution(mesh):
    placed = (
        P(("grp", "exp"), None),
        P(("grp", "exp"), None),
        P(None, "exp"),
        P("exp", None, None),
        P("exp", None, None),
    )
    return jax.shard_map(
        on_device, mesh=mesh, in_specs=placed, out_specs=P(("grp", "exp"), None), check_vma=False
    )
```

```python
import functools

import jax
import jax.numpy as jnp
from jax import lax
from jax.experimental import pallas as pl
from jax.experimental.pallas import tpu as pltpu
from jax.sharding import PartitionSpec as P

GROUP = 16
SCOPED = 8 * 1024 * 1024
TAIL = 128
LINE = 16
SCALE = 2.0**40
STEP = 512
PIECE = 128


def pack_kernel(ids_hbm, row_hbm, router_hbm, out_ref, ids_ref, router_ref, sems):
    rows, lat = row_hbm.shape
    local = router_hbm.shape[0]
    top = ids_hbm.shape[0]
    copies = [
        pltpu.make_async_copy(ids_hbm, ids_ref, sems.at[0]),
        pltpu.make_async_copy(router_hbm, router_ref, sems.at[1]),
        pltpu.make_async_copy(row_hbm, out_ref.at[:, pl.ds(0, lat)], sems.at[2]),
    ]
    for copy in copies:
        copy.start()
    copies[0].wait()
    copies[1].wait()
    ids = ids_ref[...].astype(jnp.float32)
    router = router_ref[...].astype(jnp.float32)
    lines = [jnp.concatenate([ids, jnp.full((top, TAIL - rows), -1.0, jnp.float32)], axis=1)]
    lines.append(jnp.full((LINE - top, TAIL), -1.0, jnp.float32))
    for e in range(local):
        for c in range(0, lat, TAIL):
            lines.append(router[e : e + 1, c : c + TAIL])
    lines.append(jnp.full((rows - LINE - local * lat // TAIL, TAIL), -1.0, jnp.float32))
    out_ref[:, lat:] = jnp.concatenate(lines, axis=0).astype(jnp.bfloat16)
    copies[2].wait()


def load_kernel(router_hbm, up_hbm, down_hbm, columns_ref, up_ref, down_ref, router_ref, sems):
    get_router = pltpu.make_async_copy(router_hbm, router_ref, sems.at[0])
    get_router.start()
    copies = []
    for src, dst in ((up_hbm, up_ref), (down_hbm, down_ref)):
        for e in range(src.shape[0]):
            for r in range(0, src.shape[1], PIECE):
                at = (e, pl.ds(r, PIECE))
                copies.append(pltpu.make_async_copy(src.at[at], dst.at[at], sems.at[1 + len(copies)]))
    for copy in copies:
        copy.start()
    get_router.wait()
    local, lat = router_ref.shape
    wide = jnp.concatenate(
        [router_ref[...].astype(jnp.float32), jnp.zeros((TAIL - local, lat), jnp.float32)], axis=0
    )
    columns_ref[...] = wide.T.astype(jnp.bfloat16)
    for copy in copies:
        copy.wait()


def expert_kernel(count, *refs):
    blocks, refs = refs[: 4 * count], refs[4 * count :]
    (columns_ref, up_ref, down_ref), refs = refs[:3], refs[3:]
    keep_refs, refs = refs[:count], refs[count:]
    send_refs, (packed_ref, inner_ref, result_ref) = refs[: 2 * count], refs[2 * count :]
    rows, lat = blocks[0].shape[0], blocks[0].shape[1] - TAIL
    half = 2 * rows
    local, eff, _ = down_ref.shape
    slots = packed_ref.shape[1] // count

    def put(i, lanes, value):
        keep_refs[i][:, lanes] = value[:half]
        for j, ref in enumerate(send_refs[2 * i : 2 * i + 2]):
            ref[:, lanes] = value[half + j * rows : half + (j + 1) * rows].astype(jnp.bfloat16)

    def logits_of(values):
        return jnp.dot(values, columns_ref[...], preferred_element_type=jnp.float32)

    size = 2 * half
    row = lax.broadcasted_iota(jnp.int32, (size, size), 0)
    col = lax.broadcasted_iota(jnp.int32, (size, size), 1)
    before = jnp.where(col < row, 1.0, 0.0).astype(jnp.bfloat16)
    after = jnp.where(row < col, 1.0, 0.0).astype(jnp.bfloat16)
    line = lax.broadcasted_iota(jnp.int32, (LINE, size), 0)
    slot = lax.broadcasted_iota(jnp.int32, (size, slots), 1).astype(jnp.float32)
    slot_t = lax.broadcasted_iota(jnp.int32, (slots, size), 0).astype(jnp.float32)
    labels = [(lax.axis_index("exp") * local + e).astype(jnp.float32) for e in range(local)]
    spreads = []
    for i in range(count):
        batch = blocks[4 * i : 4 * i + 4]
        x = jnp.concatenate([ref[:, :lat] for ref in batch], axis=0)
        ids_t = jnp.concatenate([ref[:LINE, lat:].astype(jnp.float32)[:, :rows] for ref in batch], axis=1)
        masks_t = [jnp.max(jnp.where(ids_t == label, 1.0, 0.0), axis=0, keepdims=True) for label in labels]
        marks_t = jnp.zeros((LINE, size), jnp.float32)
        for e in range(local):
            marks_t = jnp.where(line == e, masks_t[e], marks_t)
        marks = jnp.concatenate([marks_t, jnp.zeros((TAIL - LINE, size), jnp.float32)], axis=0).T
        place_t = jnp.dot(marks_t.astype(jnp.bfloat16), after, preferred_element_type=jnp.float32)
        place = jnp.dot(before, marks.astype(jnp.bfloat16), preferred_element_type=jnp.float32)
        gather = jnp.concatenate(
            [
                jnp.where((slot_t == place_t[e : e + 1]) & (masks_t[e] > 0.0), 1.0, 0.0)
                for e in range(local)
            ],
            axis=0,
        ).astype(jnp.bfloat16)
        packed = jnp.dot(gather, x, preferred_element_type=jnp.float32).astype(jnp.bfloat16)
        spread = jnp.concatenate(
            [jnp.where((slot == place[:, e : e + 1]) & (marks[:, e : e + 1] > 0.0), 1.0, 0.0) for e in range(local)],
            axis=1,
        ).astype(jnp.bfloat16)
        for e in range(local):
            packed_ref[e, i * slots : (i + 1) * slots, :] = packed[e * slots : (e + 1) * slots]
        spreads.append(spread)
    for e in range(local):
        chosen = packed_ref[e]
        score = jax.nn.sigmoid(logits_of(chosen)[:, e : e + 1]) * SCALE
        for c in range(0, eff, STEP):
            gate = jnp.dot(chosen, up_ref[e, :, c : c + STEP], preferred_element_type=jnp.float32)
            up = jnp.dot(chosen, up_ref[e, :, eff + c : eff + c + STEP], preferred_element_type=jnp.float32)
            inner_ref[e, :, c : c + STEP] = (gate / (1.0 + jnp.exp(-gate)) * up * score).astype(jnp.bfloat16)
    for e in range(local):
        result = jnp.dot(inner_ref[e], down_ref[e], preferred_element_type=jnp.float32).astype(jnp.bfloat16)
        for i in range(count):
            result_ref[i, e * slots : (e + 1) * slots, :] = result[i * slots : (i + 1) * slots]
    for i in range(count):
        for c in range(0, lat, STEP):
            part = jnp.dot(spreads[i], result_ref[i, :, c : c + STEP], preferred_element_type=jnp.float32)
            put(i, slice(c, c + STEP), part)


def tie_kernel():
    pass


def fold_kernel(mine_ref, came_a_ref, came_b_ref, keep_ref, send_ref):
    rows = keep_ref.shape[0]
    keep_ref[...] = mine_ref[:rows] + came_a_ref[...].astype(jnp.float32)
    send_ref[...] = (mine_ref[rows:] + came_b_ref[...].astype(jnp.float32)).astype(jnp.bfloat16)


def add_kernel(mine_ref, *refs):
    total = mine_ref[...]
    for ref in refs[:-1]:
        total = total + ref[...].astype(jnp.float32)
    refs[-1][...] = total.astype(jnp.bfloat16)


def total_kernel(*refs):
    total_ref = refs[-1]
    total = refs[0][...]
    for ref in refs[1:-1]:
        total = total + ref[...].astype(jnp.float32)
    total_ref[...] = total


def scores_kernel(mine_ref, *refs):
    *packet_refs, out_ref, lines_ref = refs
    rows, lat = mine_ref.shape[0], mine_ref.shape[1] - TAIL
    chunks = lat // TAIL
    height = lines_ref.shape[0] // len(packet_refs)
    local = height // chunks
    for i, ref in enumerate(packet_refs):
        lines_ref[i * height : (i + 1) * height, :] = ref[LINE : LINE + height, lat:].astype(jnp.float32)
    number = len(packet_refs) * local
    logits = jnp.zeros((number, rows), jnp.float32)
    for c in range(chunks):
        columns = lines_ref[pl.ds(c, number, stride=chunks), :].astype(jnp.bfloat16)
        logits = logits + lax.dot_general(
            columns,
            mine_ref[:, c * TAIL : (c + 1) * TAIL],
            (((1,), (1,)), ((), ())),
            preferred_element_type=jnp.float32,
        )
    at = lax.broadcasted_iota(jnp.int32, (number, rows), 0)
    label = ((lax.axis_index("exp") ^ (at // local)) * local + at % local).astype(jnp.float32)
    ids = mine_ref[:LINE, lat:].astype(jnp.float32)[:, :rows]
    mask = jnp.zeros((number, rows), jnp.float32)
    for k in range(LINE):
        mask = jnp.where(ids[k : k + 1] == label, 1.0, mask)
    total = jnp.sum(jax.nn.sigmoid(logits) * (mask * SCALE), axis=0, keepdims=True)
    total = jnp.broadcast_to(total, (TAIL, rows))
    total = jnp.concatenate([total, jnp.ones((TAIL, TAIL - rows), jnp.float32)], axis=1)
    out_ref[...] = total.T[:rows]


def finish_kernel(scores_ref, *refs):
    total = refs[0][...]
    for ref in refs[1:-1]:
        total = total + ref[...].astype(jnp.float32)
    refs[-1][...] = (total / scores_ref[:, :1]).astype(jnp.bfloat16)


def in_vmem(x):
    return pltpu.with_memory_space_constraint(x, pltpu.VMEM)


def in_hbm(x):
    return pltpu.with_memory_space_constraint(x, pltpu.HBM)


VMEM = pl.BlockSpec(memory_space=pltpu.VMEM)
ANY = pl.BlockSpec(memory_space=pl.ANY)


def call(kernel, outs, args=(), deps=(), chain=(), hbm=(), scratch=()):
    plain = getattr(kernel, "func", kernel)
    reads_chain = plain is expert_kernel
    n_in = len(args) + len(hbm)
    n_skip = n_in + len(deps)
    n_outs = n_skip + len(chain)

    def body(*refs):
        kernel(*refs[:n_in], *refs[n_outs : n_outs + len(outs)], *refs[n_outs + len(outs) + len(chain) :])

    def body_with_chain(*refs):
        kernel(
            *refs[:n_in],
            *refs[n_skip:n_outs],
            *refs[n_outs : n_outs + len(outs)],
            *refs[n_outs + len(outs) + len(chain) :],
        )

    specs = [VMEM] * len(args)
    specs += [ANY] * (len(hbm) + len(deps)) + [VMEM] * len(chain)
    operands = [in_vmem(a) for a in args] + [in_hbm(h) for h in hbm]
    operands += [in_vmem(x) for x in (*deps, *chain)]
    return pl.pallas_call(
        body_with_chain if reads_chain else body,
        out_shape=list(outs) + [pltpu.VMEM(x.shape, x.dtype) for x in chain],
        in_specs=specs,
        out_specs=[VMEM] * (len(outs) + len(chain)),
        scratch_shapes=list(scratch),
        compiler_params=pltpu.CompilerParams(vmem_limit_bytes=SCOPED),
        cost_estimate=pl.CostEstimate(flops=0, bytes_accessed=10_000, transcendentals=0),
        input_output_aliases={n_skip + i: len(outs) + i for i in range(len(chain))},
        name=plain.__name__.removesuffix("_kernel"),
    )(*operands)


def on_device(latent_in, routes, router, gate_up, expert_down):
    n_dev = lax.axis_size("exp")
    local = gate_up.shape[0]
    eff = expert_down.shape[1]
    rows, lat = latent_in.shape
    wide = lat + TAIL

    def swap(x, bits):
        return lax.ppermute(x, "exp", [(i, i ^ bits) for i in range(n_dev)])

    def space(height, dtype):
        return pltpu.VMEM((height, lat), dtype)

    def weights(dep):
        return call(
            load_kernel,
            [
                pltpu.VMEM((lat, TAIL), jnp.bfloat16),
                pltpu.VMEM(gate_up.shape, gate_up.dtype),
                pltpu.VMEM(expert_down.shape, expert_down.dtype),
            ],
            deps=[dep],
            hbm=[router.T, gate_up, expert_down],
            scratch=[
                pltpu.VMEM((local, lat), jnp.bfloat16),
                pltpu.SemaphoreType.DMA((1 + local * (lat + eff) // PIECE,)),
            ],
        )

    bound = 2 * ((rows * routes.shape[1] + local * n_dev - 1) // (local * n_dev))
    slots = 4 * bound

    def group_pass(mine):
        held = weights(mine)

        def step(kernel, outs, args=(), deps=(), hand_on=(), **more):
            nonlocal held
            result = call(kernel, outs, args, deps, [*held, *hand_on], **more)
            held = result[len(outs) : len(outs) + len(held)]
            return result[: len(outs)] + result[len(outs) + len(held) :]

        def tie(x, deps=()):
            return step(tie_kernel, [], deps=deps, hand_on=[x])[0]

        other, keep, send, came, fold_keep, fold_send, y_came, far = {}, {}, {}, {}, {}, {}, {}, {}

        def gather(k, deps=()):
            other[k] = tie(swap(block[k], 2), deps)

        def compute(*ks):
            count = len(ks)
            blocks = []
            for k in ks:
                near = [block[k], other[k]]
                far[k] = far.get(k) or [swap(one, 1) for one in near]
                blocks += near + far[k]
            result = step(
                functools.partial(expert_kernel, count),
                [space(2 * rows, jnp.float32)] * count + [space(rows, jnp.bfloat16)] * (2 * count),
                blocks,
                scratch=[
                    pltpu.VMEM((local, count * slots, lat), jnp.bfloat16),
                    pltpu.VMEM((local, count * slots, eff), jnp.bfloat16),
                    pltpu.VMEM((count, local * slots, lat), jnp.bfloat16),
                ],
            )
            for i, k in enumerate(ks):
                keep[k] = result[i]
                came[k] = [swap(part, 1) for part in result[count + 2 * i : count + 2 * i + 2]]

        def reduce_core(k, deps=()):
            fold_keep[k], fold_send[k] = step(
                fold_kernel, [space(rows, jnp.float32), space(rows, jnp.bfloat16)], [keep[k], *came[k]], deps
            )
            y_came[k] = swap(fold_send[k], 2)

        def reduce_y(k, *more):
            return step(add_kernel, [space(rows, jnp.bfloat16)], [fold_keep[k], y_came[k], *more])[0]

        z_2, z_1, y_0 = swap(mine, 8), swap(mine, 4), swap(mine, 2)
        block = {0: mine, 2: tie(z_2), 1: z_1}
        block[3] = swap(block[2], 4)
        other[0] = y_0
        far[0] = [swap(mine, 1), swap(y_0, 1)]
        gather(2, [block[1], block[3], y_0])
        gather(1)
        compute(2)
        gather(3, came[2])
        reduce_core(2, far[0])
        compute(3)
        other[0] = tie(other[0], [y_came[2]])
        reduce_core(3)
        compute(1, 0)
        z_3 = swap(reduce_y(3), 4)
        reduce_core(1)
        reduce_core(0)
        scores = None
        if n_dev == GROUP:
            packets = [p for k in range(4) for p in (block[k], far[k][0], other[k], far[k][1])]
            scores = step(
                scores_kernel,
                [pltpu.VMEM((rows, TAIL), jnp.float32)],
                [mine, *packets],
                scratch=[pltpu.VMEM((n_dev * local * lat // TAIL, TAIL), jnp.float32)],
            )[0]
        z_2 = swap(reduce_y(2, z_3), 8)
        z_1 = swap(reduce_y(1), 4)
        return scores, (fold_keep[0], z_2, z_1, y_came[0])

    packet = call(
        pack_kernel,
        [pltpu.VMEM((rows, wide), jnp.bfloat16)],
        hbm=[routes.T, latent_in, router.T],
        scratch=[
            pltpu.VMEM(routes.shape[::-1], routes.dtype),
            pltpu.VMEM((local, lat), jnp.bfloat16),
            pltpu.SemaphoreType.DMA((3,)),
        ],
    )[0]

    def finish(scores, parts):
        return pl.pallas_call(
            finish_kernel,
            out_shape=jax.ShapeDtypeStruct((rows, lat), jnp.bfloat16),
            in_specs=[VMEM] * (1 + len(parts)),
            out_specs=VMEM,
            compiler_params=pltpu.CompilerParams(vmem_limit_bytes=SCOPED),
            name="finish",
        )(*[in_vmem(p) for p in (scores, *parts)])

    if n_dev == GROUP:
        return finish(*group_pass(packet))

    def next_group(x):
        return lax.ppermute(x, "exp", [(i, (i + GROUP) % n_dev) for i in range(n_dev)])

    def step(carry, _):
        mine, total = carry
        total = call(total_kernel, [space(rows, jnp.float32)], [total, *group_pass(mine)[1]])[0]
        return (next_group(mine), next_group(total)), None

    start = (packet, jnp.zeros((rows, lat), jnp.float32))
    (_, total), _ = lax.scan(step, start, None, length=n_dev // GROUP)
    columns = lax.all_gather(router, "exp", axis=1, tiled=True)
    logits = jnp.dot(latent_in, columns, preferred_element_type=jnp.float32)
    labels = jnp.arange(n_dev * local, dtype=jnp.int32)
    mask = jnp.any(routes[:, :, None] == labels[None, None, :], axis=1)
    scores = jnp.sum(jnp.where(mask, jax.nn.sigmoid(logits), 0.0), axis=1, keepdims=True) * SCALE
    return finish(jnp.broadcast_to(scores, (rows, TAIL)), [total])


def solution(mesh):
    placed = (
        P(("grp", "exp"), None),
        P(("grp", "exp"), None),
        P(None, "exp"),
        P("exp", None, None),
        P("exp", None, None),
    )
    return jax.shard_map(
        on_device, mesh=mesh, in_specs=placed, out_specs=P(("grp", "exp"), None), check_vma=False
    )
```

```python
import functools

import jax
import jax.numpy as jnp
from jax import lax
from jax.experimental import pallas as pl
from jax.experimental.pallas import tpu as pltpu
from jax.sharding import PartitionSpec as P

GROUP = 16
SCOPED = 8 * 1024 * 1024
TAIL = 128
LINE = 16
SCALE = 2.0**40
STEP = 512
PIECE = 512


def pack_kernel(ids_hbm, row_hbm, router_hbm, out_ref, ids_ref, router_ref, sems):
    rows, lat = row_hbm.shape
    local = router_hbm.shape[0]
    top = ids_hbm.shape[0]
    copies = [
        pltpu.make_async_copy(ids_hbm, ids_ref, sems.at[0]),
        pltpu.make_async_copy(router_hbm, router_ref, sems.at[1]),
        pltpu.make_async_copy(row_hbm, out_ref.at[:, pl.ds(0, lat)], sems.at[2]),
    ]
    for copy in copies:
        copy.start()
    copies[0].wait()
    copies[1].wait()
    ids = ids_ref[...].astype(jnp.float32)
    router = router_ref[...].astype(jnp.float32)
    lines = [jnp.concatenate([ids, jnp.full((top, TAIL - rows), -1.0, jnp.float32)], axis=1)]
    lines.append(jnp.full((LINE - top, TAIL), -1.0, jnp.float32))
    for e in range(local):
        for c in range(0, lat, TAIL):
            lines.append(router[e : e + 1, c : c + TAIL])
    lines.append(jnp.full((rows - LINE - local * lat // TAIL, TAIL), -1.0, jnp.float32))
    out_ref[:, lat:] = jnp.concatenate(lines, axis=0).astype(jnp.bfloat16)
    copies[2].wait()


def load_kernel(router_hbm, up_hbm, down_hbm, columns_ref, up_ref, down_ref, router_ref, sems):
    get_router = pltpu.make_async_copy(router_hbm, router_ref, sems.at[0])
    get_router.start()
    copies = []
    for src, dst in ((up_hbm, up_ref), (down_hbm, down_ref)):
        for e in range(src.shape[0]):
            for r in range(0, src.shape[1], PIECE):
                at = (e, pl.ds(r, PIECE))
                copies.append(pltpu.make_async_copy(src.at[at], dst.at[at], sems.at[1 + len(copies)]))
    for copy in copies:
        copy.start()
    get_router.wait()
    local, lat = router_ref.shape
    wide = jnp.concatenate(
        [router_ref[...].astype(jnp.float32), jnp.zeros((TAIL - local, lat), jnp.float32)], axis=0
    )
    columns_ref[...] = wide.T.astype(jnp.bfloat16)
    for copy in copies:
        copy.wait()


def expert_kernel(count, *refs):
    blocks, refs = refs[: 4 * count], refs[4 * count :]
    (columns_ref, up_ref, down_ref), refs = refs[:3], refs[3:]
    keep_refs, refs = refs[:count], refs[count:]
    send_refs, (packed_ref, inner_ref, result_ref) = refs[: 2 * count], refs[2 * count :]
    rows, lat = blocks[0].shape[0], blocks[0].shape[1] - TAIL
    half = 2 * rows
    local, eff, _ = down_ref.shape
    slots = packed_ref.shape[1] // count

    def put(i, lanes, value):
        keep_refs[i][:, lanes] = value[:half]
        for j, ref in enumerate(send_refs[2 * i : 2 * i + 2]):
            ref[:, lanes] = value[half + j * rows : half + (j + 1) * rows].astype(jnp.bfloat16)

    def logits_of(values):
        return jnp.dot(values, columns_ref[...], preferred_element_type=jnp.float32)

    size = 2 * half
    row = lax.broadcasted_iota(jnp.int32, (size, size), 0)
    col = lax.broadcasted_iota(jnp.int32, (size, size), 1)
    before = jnp.where(col < row, 1.0, 0.0).astype(jnp.bfloat16)
    after = jnp.where(row < col, 1.0, 0.0).astype(jnp.bfloat16)
    line = lax.broadcasted_iota(jnp.int32, (LINE, size), 0)
    slot = lax.broadcasted_iota(jnp.int32, (size, slots), 1).astype(jnp.float32)
    slot_t = lax.broadcasted_iota(jnp.int32, (slots, size), 0).astype(jnp.float32)
    labels = [(lax.axis_index("exp") * local + e).astype(jnp.float32) for e in range(local)]
    spreads = []
    for i in range(count):
        batch = blocks[4 * i : 4 * i + 4]
        x = jnp.concatenate([ref[:, :lat] for ref in batch], axis=0)
        ids_t = jnp.concatenate([ref[:LINE, lat:].astype(jnp.float32)[:, :rows] for ref in batch], axis=1)
        masks_t = [jnp.max(jnp.where(ids_t == label, 1.0, 0.0), axis=0, keepdims=True) for label in labels]
        marks_t = jnp.zeros((LINE, size), jnp.float32)
        for e in range(local):
            marks_t = jnp.where(line == e, masks_t[e], marks_t)
        marks = jnp.concatenate([marks_t, jnp.zeros((TAIL - LINE, size), jnp.float32)], axis=0).T
        place_t = jnp.dot(marks_t.astype(jnp.bfloat16), after, preferred_element_type=jnp.float32)
        place = jnp.dot(before, marks.astype(jnp.bfloat16), preferred_element_type=jnp.float32)
        gather = jnp.concatenate(
            [
                jnp.where((slot_t == place_t[e : e + 1]) & (masks_t[e] > 0.0), 1.0, 0.0)
                for e in range(local)
            ],
            axis=0,
        ).astype(jnp.bfloat16)
        packed = jnp.dot(gather, x, preferred_element_type=jnp.float32).astype(jnp.bfloat16)
        spread = jnp.concatenate(
            [jnp.where((slot == place[:, e : e + 1]) & (marks[:, e : e + 1] > 0.0), 1.0, 0.0) for e in range(local)],
            axis=1,
        ).astype(jnp.bfloat16)
        for e in range(local):
            packed_ref[e, i * slots : (i + 1) * slots, :] = packed[e * slots : (e + 1) * slots]
        spreads.append(spread)
    for e in range(local):
        chosen = packed_ref[e]
        score = jax.nn.sigmoid(logits_of(chosen)[:, e : e + 1]) * SCALE
        for c in range(0, eff, STEP):
            gate = jnp.dot(chosen, up_ref[e, :, c : c + STEP], preferred_element_type=jnp.float32)
            up = jnp.dot(chosen, up_ref[e, :, eff + c : eff + c + STEP], preferred_element_type=jnp.float32)
            inner_ref[e, :, c : c + STEP] = (gate / (1.0 + jnp.exp(-gate)) * up * score).astype(jnp.bfloat16)
    for e in range(local):
        result = jnp.dot(inner_ref[e], down_ref[e], preferred_element_type=jnp.float32).astype(jnp.bfloat16)
        for i in range(count):
            result_ref[i, e * slots : (e + 1) * slots, :] = result[i * slots : (i + 1) * slots]
    for i in range(count):
        for c in range(0, lat, STEP):
            part = jnp.dot(spreads[i], result_ref[i, :, c : c + STEP], preferred_element_type=jnp.float32)
            put(i, slice(c, c + STEP), part)


def tie_kernel():
    pass


def fold_kernel(mine_ref, came_a_ref, came_b_ref, keep_ref, send_ref):
    rows = keep_ref.shape[0]
    keep_ref[...] = mine_ref[:rows] + came_a_ref[...].astype(jnp.float32)
    send_ref[...] = (mine_ref[rows:] + came_b_ref[...].astype(jnp.float32)).astype(jnp.bfloat16)


def add_kernel(mine_ref, *refs):
    total = mine_ref[...]
    for ref in refs[:-1]:
        total = total + ref[...].astype(jnp.float32)
    refs[-1][...] = total.astype(jnp.bfloat16)


def total_kernel(*refs):
    total_ref = refs[-1]
    total = refs[0][...]
    for ref in refs[1:-1]:
        total = total + ref[...].astype(jnp.float32)
    total_ref[...] = total


def scores_kernel(mine_ref, *refs):
    *packet_refs, out_ref, lines_ref = refs
    rows, lat = mine_ref.shape[0], mine_ref.shape[1] - TAIL
    chunks = lat // TAIL
    height = lines_ref.shape[0] // len(packet_refs)
    local = height // chunks
    for i, ref in enumerate(packet_refs):
        lines_ref[i * height : (i + 1) * height, :] = ref[LINE : LINE + height, lat:].astype(jnp.float32)
    number = len(packet_refs) * local
    logits = jnp.zeros((number, rows), jnp.float32)
    for c in range(chunks):
        columns = lines_ref[pl.ds(c, number, stride=chunks), :].astype(jnp.bfloat16)
        logits = logits + lax.dot_general(
            columns,
            mine_ref[:, c * TAIL : (c + 1) * TAIL],
            (((1,), (1,)), ((), ())),
            preferred_element_type=jnp.float32,
        )
    at = lax.broadcasted_iota(jnp.int32, (number, rows), 0)
    label = ((lax.axis_index("exp") ^ (at // local)) * local + at % local).astype(jnp.float32)
    ids = mine_ref[:LINE, lat:].astype(jnp.float32)[:, :rows]
    mask = jnp.zeros((number, rows), jnp.float32)
    for k in range(LINE):
        mask = jnp.where(ids[k : k + 1] == label, 1.0, mask)
    total = jnp.sum(jax.nn.sigmoid(logits) * (mask * SCALE), axis=0, keepdims=True)
    total = jnp.broadcast_to(total, (TAIL, rows))
    total = jnp.concatenate([total, jnp.ones((TAIL, TAIL - rows), jnp.float32)], axis=1)
    out_ref[...] = total.T[:rows]


def finish_kernel(scores_ref, *refs):
    total = refs[0][...]
    for ref in refs[1:-1]:
        total = total + ref[...].astype(jnp.float32)
    refs[-1][...] = (total / scores_ref[:, :1]).astype(jnp.bfloat16)


def in_vmem(x):
    return pltpu.with_memory_space_constraint(x, pltpu.VMEM)


def in_hbm(x):
    return pltpu.with_memory_space_constraint(x, pltpu.HBM)


VMEM = pl.BlockSpec(memory_space=pltpu.VMEM)
ANY = pl.BlockSpec(memory_space=pl.ANY)


def call(kernel, outs, args=(), deps=(), chain=(), hbm=(), scratch=()):
    plain = getattr(kernel, "func", kernel)
    reads_chain = plain is expert_kernel
    n_in = len(args) + len(hbm)
    n_skip = n_in + len(deps)
    n_outs = n_skip + len(chain)

    def body(*refs):
        kernel(*refs[:n_in], *refs[n_outs : n_outs + len(outs)], *refs[n_outs + len(outs) + len(chain) :])

    def body_with_chain(*refs):
        kernel(
            *refs[:n_in],
            *refs[n_skip:n_outs],
            *refs[n_outs : n_outs + len(outs)],
            *refs[n_outs + len(outs) + len(chain) :],
        )

    specs = [VMEM] * len(args)
    specs += [ANY] * (len(hbm) + len(deps)) + [VMEM] * len(chain)
    operands = [in_vmem(a) for a in args] + [in_hbm(h) for h in hbm]
    operands += [in_vmem(x) for x in (*deps, *chain)]
    return pl.pallas_call(
        body_with_chain if reads_chain else body,
        out_shape=list(outs) + [pltpu.VMEM(x.shape, x.dtype) for x in chain],
        in_specs=specs,
        out_specs=[VMEM] * (len(outs) + len(chain)),
        scratch_shapes=list(scratch),
        compiler_params=pltpu.CompilerParams(vmem_limit_bytes=SCOPED),
        cost_estimate=pl.CostEstimate(flops=0, bytes_accessed=10_000, transcendentals=0),
        input_output_aliases={n_skip + i: len(outs) + i for i in range(len(chain))},
        name=plain.__name__.removesuffix("_kernel"),
    )(*operands)


def on_device(latent_in, routes, router, gate_up, expert_down):
    n_dev = lax.axis_size("exp")
    local = gate_up.shape[0]
    eff = expert_down.shape[1]
    rows, lat = latent_in.shape
    wide = lat + TAIL

    def swap(x, bits):
        return lax.ppermute(x, "exp", [(i, i ^ bits) for i in range(n_dev)])

    def space(height, dtype):
        return pltpu.VMEM((height, lat), dtype)

    def weights(dep):
        return call(
            load_kernel,
            [
                pltpu.VMEM((lat, TAIL), jnp.bfloat16),
                pltpu.VMEM(gate_up.shape, gate_up.dtype),
                pltpu.VMEM(expert_down.shape, expert_down.dtype),
            ],
            deps=[dep],
            hbm=[router.T, gate_up, expert_down],
            scratch=[
                pltpu.VMEM((local, lat), jnp.bfloat16),
                pltpu.SemaphoreType.DMA((1 + local * (lat + eff) // PIECE,)),
            ],
        )

    bound = 2 * ((rows * routes.shape[1] + local * n_dev - 1) // (local * n_dev))
    slots = 4 * bound

    def group_pass(mine):
        held = weights(mine)

        def step(kernel, outs, args=(), deps=(), hand_on=(), **more):
            nonlocal held
            result = call(kernel, outs, args, deps, [*held, *hand_on], **more)
            held = result[len(outs) : len(outs) + len(held)]
            return result[: len(outs)] + result[len(outs) + len(held) :]

        def tie(x, deps=()):
            return step(tie_kernel, [], deps=deps, hand_on=[x])[0]

        other, keep, send, came, fold_keep, fold_send, y_came, far = {}, {}, {}, {}, {}, {}, {}, {}

        def gather(k, deps=()):
            other[k] = tie(swap(block[k], 2), deps)

        def compute(*ks):
            count = len(ks)
            blocks = []
            for k in ks:
                near = [block[k], other[k]]
                far[k] = far.get(k) or [swap(one, 1) for one in near]
                blocks += near + far[k]
            result = step(
                functools.partial(expert_kernel, count),
                [space(2 * rows, jnp.float32)] * count + [space(rows, jnp.bfloat16)] * (2 * count),
                blocks,
                scratch=[
                    pltpu.VMEM((local, count * slots, lat), jnp.bfloat16),
                    pltpu.VMEM((local, count * slots, eff), jnp.bfloat16),
                    pltpu.VMEM((count, local * slots, lat), jnp.bfloat16),
                ],
            )
            for i, k in enumerate(ks):
                keep[k] = result[i]
                came[k] = [swap(part, 1) for part in result[count + 2 * i : count + 2 * i + 2]]

        def reduce_core(k, deps=()):
            fold_keep[k], fold_send[k] = step(
                fold_kernel, [space(rows, jnp.float32), space(rows, jnp.bfloat16)], [keep[k], *came[k]], deps
            )
            y_came[k] = swap(fold_send[k], 2)

        def reduce_y(k, *more):
            return step(add_kernel, [space(rows, jnp.bfloat16)], [fold_keep[k], y_came[k], *more])[0]

        z_2, z_1, y_0 = swap(mine, 8), swap(mine, 4), swap(mine, 2)
        block = {0: mine, 2: tie(z_2), 1: z_1}
        block[3] = swap(block[2], 4)
        other[0] = y_0
        far[0] = [swap(mine, 1), swap(y_0, 1)]
        gather(2, [block[1], block[3], y_0])
        gather(1)
        compute(2)
        gather(3, came[2])
        reduce_core(2, far[0])
        compute(3)
        other[0] = tie(other[0], [y_came[2]])
        reduce_core(3)
        compute(1, 0)
        z_3 = swap(reduce_y(3), 4)
        reduce_core(1)
        reduce_core(0)
        scores = None
        if n_dev == GROUP:
            packets = [p for k in range(4) for p in (block[k], far[k][0], other[k], far[k][1])]
            scores = step(
                scores_kernel,
                [pltpu.VMEM((rows, TAIL), jnp.float32)],
                [mine, *packets],
                scratch=[pltpu.VMEM((n_dev * local * lat // TAIL + 8, TAIL), jnp.float32)],
            )[0]
        z_2 = swap(reduce_y(2, z_3), 8)
        z_1 = swap(reduce_y(1), 4)
        return scores, (fold_keep[0], z_2, z_1, y_came[0])

    packet = call(
        pack_kernel,
        [pltpu.VMEM((rows, wide), jnp.bfloat16)],
        hbm=[routes.T, latent_in, router.T],
        scratch=[
            pltpu.VMEM(routes.shape[::-1], routes.dtype),
            pltpu.VMEM((local, lat), jnp.bfloat16),
            pltpu.SemaphoreType.DMA((3,)),
        ],
    )[0]

    def finish(scores, parts):
        return pl.pallas_call(
            finish_kernel,
            out_shape=jax.ShapeDtypeStruct((rows, lat), jnp.bfloat16),
            in_specs=[VMEM] * (1 + len(parts)),
            out_specs=VMEM,
            compiler_params=pltpu.CompilerParams(vmem_limit_bytes=SCOPED),
            name="finish",
        )(*[in_vmem(p) for p in (scores, *parts)])

    if n_dev == GROUP:
        return finish(*group_pass(packet))

    def next_group(x):
        return lax.ppermute(x, "exp", [(i, (i + GROUP) % n_dev) for i in range(n_dev)])

    def step(carry, _):
        mine, total = carry
        total = call(total_kernel, [space(rows, jnp.float32)], [total, *group_pass(mine)[1]])[0]
        return (next_group(mine), next_group(total)), None

    start = (packet, jnp.zeros((rows, lat), jnp.float32))
    (_, total), _ = lax.scan(step, start, None, length=n_dev // GROUP)
    columns = lax.all_gather(router, "exp", axis=1, tiled=True)
    logits = jnp.dot(latent_in, columns, preferred_element_type=jnp.float32)
    labels = jnp.arange(n_dev * local, dtype=jnp.int32)
    mask = jnp.any(routes[:, :, None] == labels[None, None, :], axis=1)
    scores = jnp.sum(jnp.where(mask, jax.nn.sigmoid(logits), 0.0), axis=1, keepdims=True) * SCALE
    return finish(jnp.broadcast_to(scores, (rows, TAIL)), [total])


def solution(mesh):
    placed = (
        P(("grp", "exp"), None),
        P(("grp", "exp"), None),
        P(None, "exp"),
        P("exp", None, None),
        P("exp", None, None),
    )
    return jax.shard_map(
        on_device, mesh=mesh, in_specs=placed, out_specs=P(("grp", "exp"), None), check_vma=False
    )
```
